32 devices in a mesh: fsdp: 8 (over z, y), tp: 4 (over x, core).
Axes of the slice: x: 2, y: 2, z: 4, core: 2. Of those that a mesh axis runs over, the one named last changes fastest.
Arguments:
- layer_in: bfloat16 [8192, 2048], P(('fsdp', 'tp')), may hold values from -6 to 6
- seq_lengths: int32 [8, 8], P('fsdp'), may hold values from 1 to 512, 1024 in all within a row
- attn_gain: float32 [2048], P(('fsdp', 'tp')), may hold values from 0.5 to 1.5
- w_query: bfloat16 [2048, 2048], P('fsdp', 'tp'), may hold values from -0.125 to 0.125
- w_key: bfloat16 [2048, 256], P('fsdp', 'tp'), may hold values from -0.125 to 0.125
- w_value: bfloat16 [2048, 256], P('fsdp', 'tp'), may hold values from -0.125 to 0.125
- w_output: bfloat16 [2048, 2048], P('tp', 'fsdp'), may hold values from -0.75 to 0.75
- mlp_gain: float32 [2048], P(('fsdp', 'tp')), may hold values from 0.5 to 1.5
- w_gate: bfloat16 [2048, 5632], P('fsdp', 'tp'), may hold values from -0.125 to 0.125
- w_up: bfloat16 [2048, 5632], P('fsdp', 'tp'), may hold values from -0.125 to 0.125
- w_down: bfloat16 [5632, 2048], P('tp', 'fsdp'), may hold values from -0.078125 to 0.078125
- out_grad: bfloat16 [8192, 2048], P(('fsdp', 'tp')), may hold values from -6 to 6
Outputs:
- layer_out: bfloat16 [8192, 2048], P(('fsdp', 'tp'))
- in_grad: float32 [8192, 2048], P(('fsdp', 'tp'))
- attn_gain_grad: float32 [2048], P(('fsdp', 'tp'))
- w_query_grad: float32 [2048, 2048], P('fsdp', 'tp')
- w_key_grad: float32 [2048, 256], P('fsdp', 'tp')
- w_value_grad: float32 [2048, 256], P('fsdp', 'tp')
- w_output_grad: float32 [2048, 2048], P('tp', 'fsdp')
- mlp_gain_grad: float32 [2048], P(('fsdp', 'tp'))
- w_gate_grad: float32 [2048, 5632], P('fsdp', 'tp')
- w_up_grad: float32 [2048, 5632], P('fsdp', 'tp')
- w_down_grad: float32 [5632, 2048], P('tp', 'fsdp')
The draws below stay inside these ranges and needn't reach their ends.
Inputs may be any that keep to these rules, and one draw needn't show every extreme that they name: `seq_lengths`: each row holds the lengths of the 8 sequences packed in order into one group of 1024 tokens; they sum to 1024 and the longest of every row is exactly 512.
All inputs are finite; a program needn't handle non-finite values.
Results may differ from the reference program's by a relative error of at most 0.019.
Values may be sent and summed in bfloat16 or wider, within the bound.
No kernel may reach another device: no remote copies, remote signals or barrier semaphores. Data moves between devices by JAX's collectives and lax.ppermute only.
A program may use at most 192 MiB of HBM per device.

```python
import math
import jax
import jax.numpy as jnp
import numpy as np
from jax import lax

D = 2048
H = 32
KVH = 4
HD = 64
FF = 5632
TOK_GRP = 1024
MAXLEN = 512
NSEQ = 8
GROUPS = 8
TOKENS = 8192
QD = 2048
KVD = 256


def levels(rng, shape, split, least, top_value):
    loudness, own = 1.0, jax.random.fold_in(rng, 6)
    for dim, parts in split:
        heights = jnp.exp(jax.random.uniform(jax.random.fold_in(own, dim), (parts,), jnp.float32, least / len(split), top_value / len(split)))
        loudness = loudness * jnp.repeat(heights, shape[dim] // parts).reshape([-1 if axis == dim else 1 for axis in range(len(shape))])
    return loudness


def split_up(amount, total, limit, skew):
    loads = [(1 << 20) // math.isqrt(standing ** skew) + 1 for standing in range(2, amount + 1)]
    surplus, counts = total - limit - (amount - 1), [1] * (amount - 1)
    while surplus > 0:
        candidates = [i for i in range(amount - 1) if counts[i] < limit]
        pool, budget = sum([loads[i] for i in candidates]), surplus
        for i in candidates:
            more = min(limit - counts[i], max(1, budget * loads[i] // pool), surplus)
            counts[i] = counts[i] + more
            surplus = surplus - more
    return np.array([limit] + counts)


def uneven(key, number_of, total, reach, lean):
    if number_of == 2:
        one = jax.random.randint(key, (), max(1, total - reach), min(reach, total - 1) + 1)
        return jnp.stack([one, total - one])
    tallies = jnp.asarray(split_up(number_of, total, reach, lean), jnp.int32)
    twos = (number_of - 1) // 2
    giver, receiver = tallies[1:1 + 2 * twos:2], tallies[2:2 + 2 * twos:2]
    room = jnp.minimum(giver - 1, reach - receiver)
    shifted = jax.random.randint(jax.random.fold_in(key, 1), (twos,), 0, 1 << 20) % (room + 1)
    tallies = tallies.at[1:1 + 2 * twos:2].set(giver - shifted).at[2:2 + 2 * twos:2].set(receiver + shifted)
    return tallies[jax.random.permutation(jax.random.fold_in(key, 2), number_of)]


def gaussian(own_key, shape, scale, bound, shards=(), held_as=jnp.bfloat16):
    entries = jax.random.normal(own_key, shape, jnp.float32) * scale
    if len(shards) > 0:
        entries = levels(own_key, shape, shards, -0.22, 0.18) * entries
    return jnp.clip(entries, min=-bound, max=bound).astype(held_as)


def setup_inputs(seed: int = 0) -> dict:
    key_of = jax.random.split(jax.random.key(seed), 13)
    layer_in = gaussian(key_of[0], (TOKENS, D), 1.0, 6.0, ((0, 32),))
    seq_lengths = jax.vmap(lambda own: uneven(own, NSEQ, TOK_GRP, MAXLEN, 2))(jax.random.split(key_of[1], GROUPS)).reshape((GROUPS, NSEQ)).astype(jnp.int32)
    attn_gain = jnp.clip(1.0 + 0.1 * jax.random.normal(key_of[2], (D,), jnp.float32), 0.5, 1.5)
    w_query = gaussian(key_of[3], (D, QD), D ** -0.5, 0.125, ((0, 8), (1, 4)))
    w_key = gaussian(key_of[4], (D, KVD), D ** -0.5, 0.125, ((0, 8), (1, 4)))
    w_value = gaussian(key_of[5], (D, KVD), D ** -0.5, 0.125, ((0, 8), (1, 4)))
    w_output = gaussian(key_of[6], (QD, D), (D // 32) ** -0.5, 0.75, ((0, 4), (1, 8)))
    mlp_gain = jnp.clip(1.0 + 0.1 * jax.random.normal(key_of[7], (D,), jnp.float32), 0.5, 1.5)
    w_gate = gaussian(key_of[8], (D, FF), D ** -0.5, 0.125, ((0, 8), (1, 4)))
    w_up = gaussian(key_of[9], (D, FF), D ** -0.5, 0.125, ((0, 8), (1, 4)))
    w_down = gaussian(key_of[10], (FF, D), FF ** -0.5, 0.078125, ((0, 4), (1, 8)))
    out_grad = gaussian(key_of[11], (TOKENS, D), 1.0, 6.0, ((0, 32),))
    return {"layer_in": layer_in, "seq_lengths": seq_lengths, "attn_gain": attn_gain, "w_query": w_query, "w_key": w_key, "w_value": w_value, "w_output": w_output, "mlp_gain": mlp_gain, "w_gate": w_gate, "w_up": w_up, "w_down": w_down, "out_grad": out_grad}


EPSILON = 1e-05
ROPE_BASE = 10000.0
MASKED_OUT = -1e+30

@jax.custom_vjp
def low(v):
    return lax.optimization_barrier(v.astype(jnp.bfloat16)).astype(jnp.float32)

@jax.custom_vjp
def low_back(v):
    return v

def low_keep(v):
    return (low(v), None)

def low_pass(kept, grad):
    return (grad,)

def back_keep(v):
    return (v, None)

def back_low(kept, grad):
    return (low(grad),)
low.defvjp(low_keep, low_pass)
low_back.defvjp(back_keep, back_low)

def positions(lengths, count):
    starts = jnp.cumsum(lengths, axis=-1) - lengths
    indices = jnp.arange(count, dtype=jnp.int32)
    inside = (indices[None, :, None] >= starts[:, None, :]) & (indices[None, :, None] < (starts + lengths)[:, None, :])
    first_at = lax.optimization_barrier(jnp.sum(jnp.where(inside, starts[:, None, :], 0), axis=-1))
    return (indices[None, :] - first_at).astype(jnp.int32)

def rope_tables(where_at, width):
    half_width = width // 2
    inverse_freq = ROPE_BASE ** (-(jnp.arange(half_width, dtype=jnp.float32) * 2.0 / width))
    angles = where_at.astype(jnp.float32)[:, None] * inverse_freq[None, :]
    angles = jnp.concatenate([angles, angles], axis=1)
    return (jnp.cos(angles), jnp.sin(angles))

def turn(values):
    half_width = values.shape[-1] // 2
    return jnp.concatenate([-values[..., half_width:], values[..., :half_width]], axis=-1)

def rotate(values, cosine_tab, sine_tab):
    return values * cosine_tab[:, None, :] + turn(values) * sine_tab[:, None, :]

def norm_rows(values, gain):
    inverse = lax.rsqrt(lax.optimization_barrier(jnp.mean(values * values, axis=-1, keepdims=True)) + EPSILON)
    return values * inverse * gain

def matmul_hi(left, right):
    return jnp.dot(left, right, precision=lax.Precision.HIGHEST)

def group_attention(queries, keyed, values, where_at):
    count = queries.shape[0]
    kv_count = keyed.shape[1]
    grouped = queries.reshape(count, kv_count, -1, queries.shape[-1])
    scores = jnp.einsum('qkgd,tkd->kgqt', grouped, keyed, precision=lax.Precision.HIGHEST) * (1.0 / math.sqrt(HD))
    scores = low_back(scores)
    indices = jnp.arange(count, dtype=jnp.int32)
    allowed = (indices[None, :] <= indices[:, None]) & (indices[None, :] >= (indices - where_at)[:, None])
    scores = jnp.where(allowed[None, None], scores, MASKED_OUT)
    shares = low(jax.nn.softmax(scores, axis=-1))
    blended = jnp.einsum('kgqt,tkd->qkgd', shares, values, precision=lax.Precision.HIGHEST)
    return blended.reshape(count, -1)

def attend_step(carry, pieces):
    return (carry, group_attention(pieces[0], pieces[1], pieces[2], pieces[3]))

def reference(layer_in, seq_lengths, attn_gain, w_query, w_key, w_value, w_output, mlp_gain, w_gate, w_up, w_down, out_grad):
    where_groups = positions(seq_lengths, TOK_GRP)
    cosine_tab, sine_tab = rope_tables(where_groups.reshape(TOKENS), HD)
    stepper = jax.checkpoint(attend_step)

    def forward(layer_f, gain_one, proj_query, proj_key, proj_value, proj_output, gain_two, proj_gate, proj_up, proj_down):
        normed_one = low(norm_rows(layer_f, gain_one))
        queries = low_back(matmul_hi(normed_one, proj_query)).reshape(TOKENS, H, HD)
        keyed = low_back(matmul_hi(normed_one, proj_key)).reshape(TOKENS, KVH, HD)
        values = low(low_back(matmul_hi(normed_one, proj_value))).reshape(TOKENS, KVH, HD)
        queries = low(rotate(queries, cosine_tab, sine_tab))
        keyed = low(rotate(keyed, cosine_tab, sine_tab))
        pieces = (queries.reshape(GROUPS, TOK_GRP, H, HD), keyed.reshape(GROUPS, TOK_GRP, KVH, HD), values.reshape(GROUPS, TOK_GRP, KVH, HD), where_groups)
        carry_end, attended = lax.scan(stepper, jnp.zeros((), jnp.float32), pieces)
        attended = low(low_back(attended.reshape(TOKENS, QD)))
        middle_sum = layer_f + low_back(matmul_hi(attended, proj_output))
        normed_two = low(norm_rows(middle_sum, gain_two))
        gate_pre = low_back(matmul_hi(normed_two, proj_gate))
        up_pre = low_back(matmul_hi(normed_two, proj_up))
        hidden = low(jax.nn.silu(gate_pre) * up_pre)
        return middle_sum + low_back(matmul_hi(hidden, proj_down))
    primals = (layer_in.astype(jnp.float32), attn_gain.astype(jnp.float32), w_query.astype(jnp.float32), w_key.astype(jnp.float32), w_value.astype(jnp.float32), w_output.astype(jnp.float32), mlp_gain.astype(jnp.float32), w_gate.astype(jnp.float32), w_up.astype(jnp.float32), w_down.astype(jnp.float32))
    result, pullback = jax.vjp(forward, *primals)
    grads = pullback(out_grad.astype(jnp.float32))
    return (result.astype(jnp.bfloat16), grads[0], grads[1], grads[2], grads[3], grads[4], grads[5], grads[6], grads[7], grads[8], grads[9])
```

```python
import math

import jax
import jax.numpy as jnp
from jax import lax
from jax.experimental import pallas as pl
from jax.experimental.pallas import tpu as pltpu
from jax.sharding import PartitionSpec as P

HD = 64
MAXLEN = 512
EPSILON = 1e-05
ROPE_BASE = 10000.0
MASKED_OUT = -1e30
COLUMN_BLOCKS = 8
ROW_BLOCKS = 4
VMEM = 56 * 1024 * 1024
F32 = jnp.float32
BF16 = jnp.bfloat16


def positions(lengths, count):
    starts = jnp.cumsum(lengths, axis=-1) - lengths
    indices = jnp.arange(count, dtype=jnp.int32)
    inside = (indices[None, :, None] >= starts[:, None, :]) & (
        indices[None, :, None] < (starts + lengths)[:, None, :]
    )
    first_at = jnp.sum(jnp.where(inside, starts[:, None, :], 0), axis=-1)
    return first_at, indices[None, :] - first_at


def rope_tables(where_at, width):
    half_width = width // 2
    inverse_freq = ROPE_BASE ** (-(jnp.arange(half_width, dtype=F32) * 2.0 / width))
    angles = where_at.astype(F32)[:, None] * inverse_freq[None, :]
    cosine, sine = jnp.cos(angles), jnp.sin(angles)
    return jnp.concatenate([cosine] * 4, axis=1), jnp.concatenate([sine] * 4, axis=1)


def project(left, weight):
    return jnp.dot(left, weight, preferred_element_type=F32)


def project_back(grad, weight):
    return jnp.einsum("tc,dc->td", grad, weight, preferred_element_type=F32)


def outer(left, right):
    return jnp.einsum("ta,tb->ab", left, right, preferred_element_type=F32)


def call(body, outs, operands, flops=0, nbytes=0, **more):
    return pl.pallas_call(
        body,
        out_shape=outs,
        compiler_params=pltpu.CompilerParams(vmem_limit_bytes=VMEM),
        cost_estimate=pl.CostEstimate(flops=flops, bytes_accessed=nbytes, transcendentals=0),
        **more,
    )(*operands)


def whole(count):
    return [pl.BlockSpec(memory_space=pltpu.VMEM)] * count


SCALARS = pl.BlockSpec(memory_space=pltpu.SMEM)


def spans(order, width):
    step = width // COLUMN_BLOCKS
    return [
        (slice(j * step, (j + 1) * step), pl.ds(pl.multiple_of(order[j] * step, step), step))
        for j in range(COLUMN_BLOCKS)
    ]


def true_rows(order, i, count):
    return pl.ds(pl.multiple_of(order[COLUMN_BLOCKS + i] * count, count), count)


def held_place(order, i, count):
    at = order[COLUMN_BLOCKS + ROW_BLOCKS + i]
    return pl.ds(pl.multiple_of(at * count, count), count)


def turned(values, lanes):
    width = values.shape[-1]
    first = (lanes % HD) < HD // 2
    return jnp.where(
        first, -pltpu.roll(values, width - HD // 2, 1), pltpu.roll(values, HD // 2, 1)
    )


def norm_project(order, blocks, weights, cosine, sine):
    count, width = blocks[0].shape
    total = weights.shape[1]
    kv = 2 * HD

    def body(order, x0, x1, x2, x3, w, c, s, normed, out):
        for i, x in enumerate((x0, x1, x2, x3)):
            rows = slice(i * count, (i + 1) * count)
            values = x[...].astype(F32)
            inverse = lax.rsqrt(jnp.mean(values * values, axis=-1, keepdims=True) + EPSILON)
            for held, true in spans(order, width):
                normed[rows, held] = (x[:, true].astype(F32) * inverse).astype(BF16)
            product = jnp.dot(normed[rows, :], w[...], preferred_element_type=F32)
            place = true_rows(order, i, count)
            cos, sin = c[place, :], s[place, :]
            lanes = lax.broadcasted_iota(jnp.int32, cos.shape, 1)
            for at in range(0, total, 128):
                part = product[:, at : at + 128]
                if at + 128 > total - kv:
                    co, si = jnp.where(lanes < HD, cos, 1.0), jnp.where(lanes < HD, sin, 0.0)
                else:
                    co, si = cos, sin
                out[place, at : at + 128] = (part * co + turned(part, lanes) * si).astype(BF16)

    return call(
        body,
        (
            jax.ShapeDtypeStruct((ROW_BLOCKS * count, width), BF16),
            jax.ShapeDtypeStruct((ROW_BLOCKS * count, total), BF16),
        ),
        (order, *blocks, weights, cosine, sine),
        flops=2 * ROW_BLOCKS * count * width * total,
        nbytes=2 * (2 * ROW_BLOCKS * count * width + width * total),
        in_specs=[SCALARS] + whole(7),
        out_specs=tuple(whole(2)),
    )


def window(i, span):
    return max(0, i * span - MAXLEN), (i + 1) * span


def shown(first, i, span):
    low, high = window(i, span)
    keys = low + lax.broadcasted_iota(jnp.int32, (high - low, span), 0)
    rows = i * span + lax.broadcasted_iota(jnp.int32, (high - low, span), 1)
    return (keys <= rows) & (keys >= first[:, i * span : (i + 1) * span])


def dot_nt(left, right):
    return lax.dot_general(left, right, (((1,), (1,)), ((), ())), preferred_element_type=F32)


def dot_tn(left, right):
    return lax.dot_general(left, right, (((0,), (0,)), ((), ())), preferred_element_type=F32)


def attention(order, qkv, first, pairs):
    rows = qkv.shape[0]
    span = rows // ROW_BLOCKS
    width = 2 * HD

    def body(order, q, kv, first, out, logs):
        for i in range(ROW_BLOCKS):
            low, high = window(i, span)
            allowed = shown(first, i, span)
            keys, values = kv[low:high, :HD], kv[low:high, HD:]
            results = []
            for h in range(2):
                queries = q[i * span : (i + 1) * span, h * HD : (h + 1) * HD] * 0.125
                scores = jnp.where(allowed, dot_nt(keys, queries.astype(BF16)), MASKED_OUT)
                top = jnp.max(scores, axis=0, keepdims=True)
                shares = jnp.exp(scores - top)
                total = jnp.sum(shares, axis=0, keepdims=True)
                mixed = dot_tn(values, shares.astype(BF16)) / total
                results.append(mixed)
                logs[0, h : h + 1, i * span : (i + 1) * span] = top + jnp.log(total)
            both = jnp.concatenate(results, axis=0)
            out[held_place(order, i, span), :] = both.T.astype(BF16)

    return call(
        body,
        (
            jax.ShapeDtypeStruct((rows, pairs * width), BF16),
            jax.ShapeDtypeStruct((pairs, 2, rows), F32),
        ),
        (order, qkv, qkv, first),
        flops=4 * rows * 768 * HD * 2 * pairs * 8,
        nbytes=2 * rows * pairs * width * 2,
        grid=(pairs,),
        in_specs=[
            SCALARS,
            pl.BlockSpec((rows, width), lambda p: (0, p)),
            pl.BlockSpec((rows, width), lambda p: (0, pairs)),
            pl.BlockSpec((1, rows), lambda p: (0, 0)),
        ],
        out_specs=(
            pl.BlockSpec((rows, width), lambda p: (0, p)),
            pl.BlockSpec((1, 2, rows), lambda p: (p, 0, 0)),
        ),
    )


def attention_back(order, qkv, first, logs, grads, cosine, sine, pairs):
    rows = qkv.shape[0]
    span = rows // ROW_BLOCKS
    width = 2 * HD

    def body(order, q, kv, first, logs, grad, c, s, dq, dkv, total):
        @pl.when(pl.program_id(0) == 0)
        def _():
            total[...] = jnp.zeros_like(total)

        lanes = lax.broadcasted_iota(jnp.int32, (span, width), 1)
        for i in range(ROW_BLOCKS):
            low, high = window(i, span)
            allowed = shown(first, i, span)
            place = held_place(order, i, span)
            keys, values = kv[low:high, :HD], kv[low:high, HD:]
            results, key_part, value_part = [], 0.0, 0.0
            for h in range(2):
                head = slice(h * HD, (h + 1) * HD)
                queries = (q[i * span : (i + 1) * span, head] * 0.125).astype(BF16)
                came = grad[place, head]
                log = logs[0, h : h + 1, i * span : (i + 1) * span]
                shares = jnp.where(allowed, jnp.exp(dot_nt(keys, queries) - log), 0.0)
                change = dot_nt(values, came)
                inner = jnp.sum(shares * change, axis=0, keepdims=True)
                score_grads = (shares * (change - inner)).astype(BF16)
                value_part += jnp.dot(shares.astype(BF16), came, preferred_element_type=F32)
                key_part += jnp.dot(score_grads, queries, preferred_element_type=F32)
                results.append(dot_tn(keys, score_grads) * 0.125)
            total[low:high, :] += jnp.concatenate([key_part, value_part], axis=1)
            query_grad = jnp.concatenate(results, axis=0).T
            at = slice(i * span, (i + 1) * span)
            dq[place, :] = (
                query_grad * c[at, :] - turned(query_grad * s[at, :], lanes)
            ).astype(BF16)

        @pl.when(pl.program_id(0) == pairs - 1)
        def _():
            for i in range(ROW_BLOCKS):
                at = slice(i * span, (i + 1) * span)
                cos = jnp.where(lanes < HD, c[at, :], 1.0)
                sin = jnp.where(lanes < HD, s[at, :], 0.0)
                part = total[at, :]
                dkv[held_place(order, i, span), :] = (
                    part * cos - turned(part * sin, lanes)
                ).astype(BF16)

    return call(
        body,
        (
            jax.ShapeDtypeStruct((rows, pairs * width), BF16),
            jax.ShapeDtypeStruct((rows, width), BF16),
        ),
        (order, qkv, qkv, first, logs, grads, cosine, sine),
        flops=10 * rows * 768 * HD * 2 * pairs * 8,
        nbytes=2 * rows * pairs * width * 3,
        grid=(pairs,),
        in_specs=[
            SCALARS,
            pl.BlockSpec((rows, width), lambda p: (0, p)),
            pl.BlockSpec((rows, width), lambda p: (0, pairs)),
            pl.BlockSpec((1, rows), lambda p: (0, 0)),
            pl.BlockSpec((1, 2, rows), lambda p: (p, 0, 0)),
            pl.BlockSpec((rows, width), lambda p: (0, p)),
            pl.BlockSpec((rows, width), lambda p: (0, 0)),
            pl.BlockSpec((rows, width), lambda p: (0, 0)),
        ],
        out_specs=(
            pl.BlockSpec((rows, width), lambda p: (0, p)),
            pl.BlockSpec((rows, width), lambda p: (0, 0)),
        ),
        scratch_shapes=[pltpu.VMEM((rows, width), F32)],
    )


def held_rows(order, blocks):
    count, width = blocks[0].shape

    def body(order, a, b, c, d, out):
        for i, block in enumerate((a, b, c, d)):
            for held, true in spans(order, width):
                out[i * count : (i + 1) * count, held] = block[:, true]

    return call(
        body,
        jax.ShapeDtypeStruct((ROW_BLOCKS * count, width), BF16),
        (order, *blocks),
        nbytes=4 * ROW_BLOCKS * count * width,
        in_specs=[SCALARS] + whole(4),
        out_specs=whole(1)[0],
    )


def middle(order, layer_in, near, far):
    count, width = layer_in.shape

    def body(order, x, near, far, mid, unit, inverse):
        for held, true in spans(order, width):
            mid[:, held] = x[:, true].astype(F32) + near[:, held] + far[:, held].astype(F32)
        values = mid[...]
        scale = lax.rsqrt(jnp.mean(values * values, axis=-1, keepdims=True) + EPSILON)
        inverse[...] = scale
        unit[...] = (values * scale).astype(BF16)

    return call(
        body,
        (
            jax.ShapeDtypeStruct((count, width), F32),
            jax.ShapeDtypeStruct((count, width), BF16),
            jax.ShapeDtypeStruct((count, 1), F32),
        ),
        (order, layer_in, near, far),
        nbytes=20 * count * width,
        in_specs=[SCALARS] + whole(3),
        out_specs=tuple(whole(3)),
    )


def layer_end(order, mid, near, far):
    count, width = mid.shape

    def body(order, mid, near, far, out):
        for held, true in spans(order, width):
            total = mid[:, held] + near[:, held] + far[:, held].astype(F32)
            out[:, true] = total.astype(BF16)

    return call(
        body,
        jax.ShapeDtypeStruct((count, width), BF16),
        (order, mid, near, far),
        nbytes=14 * count * width,
        in_specs=[SCALARS] + whole(3),
        out_specs=whole(1)[0],
    )


def middle_back(order, out_grad, mid, inverse, near, far):
    count, width = mid.shape

    def body(order, dy, mid, inverse, near, far, grad, low):
        scale = inverse[...]
        grad_unit = near[...] + far[...].astype(F32)
        unit = mid[...] * scale
        inner = jnp.mean(grad_unit * unit, axis=-1, keepdims=True)
        grad[...] = scale * (grad_unit - unit * inner)
        for held, true in spans(order, width):
            total = grad[:, held] + dy[:, true].astype(F32)
            grad[:, held] = total
            low[:, held] = total.astype(BF16)

    return call(
        body,
        (
            jax.ShapeDtypeStruct((count, width), F32),
            jax.ShapeDtypeStruct((count, width), BF16),
        ),
        (order, out_grad, mid, inverse, near, far),
        nbytes=20 * count * width,
        in_specs=[SCALARS] + whole(5),
        out_specs=tuple(whole(2)),
    )


def input_back(order, layer_in, grad_mid, near, far):
    count, width = grad_mid.shape

    def body(order, x, grad_mid, near, far, out, unit):
        values = x[...].astype(F32)
        scale = lax.rsqrt(jnp.mean(values * values, axis=-1, keepdims=True) + EPSILON)
        for held, true in spans(order, width):
            unit[:, held] = x[:, true].astype(F32) * scale
        grad_unit = near[...] + far[...].astype(F32)
        inner = jnp.mean(grad_unit * unit[...], axis=-1, keepdims=True)
        unit[...] = grad_mid[...] + scale * (grad_unit - unit[...] * inner)
        for held, true in spans(order, width):
            out[:, true] = unit[:, held]

    return call(
        body,
        jax.ShapeDtypeStruct((count, width), F32),
        (order, layer_in, grad_mid, near, far),
        nbytes=16 * count * width,
        in_specs=[SCALARS] + whole(4),
        out_specs=whole(1)[0],
        scratch_shapes=[pltpu.VMEM((count, width), F32)],
    )


def after(value, *others):
    return lax.optimization_barrier((value, *others))[0]


class Direct:
    def __init__(self):
        self.order = jnp.array(list(range(COLUMN_BLOCKS)) + 2 * list(range(ROW_BLOCKS)), jnp.int32)

    def own_gains(self, gains):
        return [lax.all_gather(g, "tp", axis=0, tiled=True) for g in gains]

    def share_gains(self, terms):
        return [lax.psum_scatter(g, "tp", scatter_dimension=0, tiled=True) for g in terms]

    def gather_weight(self, shard, axis):
        return lax.all_gather(shard, "fsdp", axis=axis, tiled=True)

    def sum_grads(self, left, right, axis):
        total = outer(left, right).astype(BF16)
        return lax.psum_scatter(total, "fsdp", scatter_dimension=axis, tiled=True).astype(F32)

    def gather_rows(self, rows):
        return jnp.split(lax.all_gather(rows, "tp", axis=0, tiled=True), ROW_BLOCKS)

    def sum_rows(self, product, left):
        total = product(left).astype(BF16)
        near = lax.psum_scatter(total, "tp", scatter_dimension=0, tiled=True)
        return near.astype(F32), jnp.zeros_like(near)


class Paired:
    def __init__(self):
        self.f = lax.axis_index("fsdp")
        self.t = lax.axis_index("tp")
        self.zs, self.ys = [], []
        masks = [2 * a + b for b in (0, 1) for a in range(4)]
        places = jnp.array([0, 2, 1, 3], jnp.int32)
        near = self.t ^ jnp.arange(ROW_BLOCKS, dtype=jnp.int32)
        swapped = ((near & 1) << 1) | (near >> 1)
        self.order = jnp.concatenate(
            [self.f ^ jnp.array(masks, jnp.int32), self.t ^ places, swapped]
        )

    def fs(self, values, mask):
        return lax.ppermute(values, "fsdp", [(i, i ^ mask) for i in range(8)])

    def ts(self, values, mask):
        return lax.ppermute(values, "tp", [(i, i ^ mask) for i in range(4)])

    def along(self, chain, moves):
        values = [value for value, _ in moves]
        if chain:
            tied = lax.optimization_barrier((values, chain[-1]))
            values = tied[0]
        came = [self.fs(value, mask) for value, (_, mask) in zip(values, moves, strict=True)]
        chain.append(came)
        return came

    def own_gains(self, gains):
        own = jnp.stack(gains)
        near = jnp.stack([own, self.ts(own, 1)], axis=1)
        near = jnp.where((self.t & 1) == 1, near[:, ::-1], near)
        both = jnp.stack([near, self.ts(near, 2)], axis=1)
        both = jnp.where((self.t >> 1) == 1, both[:, ::-1], both)
        both = both.reshape(len(gains), -1)
        return [both[i] for i in range(len(gains))]

    def share_gains(self, terms):
        both = jnp.stack(terms).reshape(len(terms), 2, 2, -1)
        both = jnp.where((self.t >> 1) == 1, both[:, ::-1], both)
        both = both[:, 0] + self.ts(both[:, 1], 2)
        both = jnp.where((self.t & 1) == 1, both[:, ::-1], both)
        both = both[:, 0] + self.ts(both[:, 1], 1)
        return [both[i] for i in range(len(terms))]

    def gather_weight(self, shard, axis):
        one, two = self.along(self.zs, [(shard, 2), (shard, 4)])
        (three,) = self.along(self.zs, [(shard, 6)])
        low = jnp.concatenate([shard, one], axis=axis)
        (low_across,) = self.along(self.ys, [(low, 1)])
        high = jnp.concatenate([two, three], axis=axis)
        (high_across,) = self.along(self.ys, [(high, 1)])
        return jnp.concatenate([low, high, low_across, high_across], axis=axis)

    def sum_grads(self, left, right, axis):
        split = left if axis == 0 else right
        step = split.shape[1] // 8

        def part(first, last):
            at = slice(first * step, last * step)
            if axis == 0:
                return outer(left[:, at], right)
            return outer(left, right[:, at])

        def pieces(came):
            return jnp.split(came.astype(F32), 2, axis=axis)

        (came,) = self.along(self.ys, [(part(6, 8).astype(BF16), 1)])
        two, three = pieces(came)
        (far,) = self.along(self.zs, [((part(3, 4) + three).astype(BF16), 6)])
        (came,) = self.along(self.ys, [(part(4, 6).astype(BF16), 1)])
        zero, one = pieces(came)
        moves = [((part(1, 2) + one).astype(BF16), 2), ((part(2, 3) + two).astype(BF16), 4)]
        near, middle_one = self.along(self.zs, moves)
        return (part(0, 1) + zero) + far.astype(F32) + near.astype(F32) + middle_one.astype(F32)

    def gather_rows(self, rows):
        far = self.ts(rows, 2)
        return [rows, far, self.ts(rows, 1), self.ts(far, 1)]

    def sum_rows(self, product, left):
        count = left[0].shape[0] // 4
        away = product([v[2 * count :] for v in left]).astype(BF16)
        came = self.ts(away, 1)
        far = product([v[count : 2 * count] for v in left]) + came[count:].astype(F32)
        far = self.ts(far.astype(BF16), 2)
        near = product([v[:count] for v in left]) + came[:count].astype(F32)
        return near, far


def local(
    layer_in,
    seq_lengths,
    attn_gain,
    w_query,
    w_key,
    w_value,
    w_output,
    mlp_gain,
    w_gate,
    w_up,
    w_down,
    out_grad,
):
    way = Paired() if (lax.axis_size("fsdp"), lax.axis_size("tp")) == (8, 4) else Direct()
    order = way.order
    group_rows = layer_in.shape[0] * lax.axis_size("tp")
    query_width, key_width = w_query.shape[1], w_key.shape[1]
    pairs = query_width // (2 * HD)

    input_blocks = way.gather_rows(layer_in)
    gain_one, gain_two = way.own_gains([attn_gain, mlp_gain])
    gain_one, gain_two = gain_one[:, None], gain_two[:, None]
    w_qkv = jnp.concatenate([w_query, w_key, w_value], axis=1)
    w_output_all = way.gather_weight(w_output, 1)
    w_qkv_all = way.gather_weight((w_qkv.astype(F32) * gain_one).astype(BF16), 0)
    w_gate_all = way.gather_weight((w_gate.astype(F32) * gain_two).astype(BF16), 0)
    w_up_all = way.gather_weight((w_up.astype(F32) * gain_two).astype(BF16), 0)
    w_down_all = way.gather_weight(w_down, 1)

    first_at, where_at = positions(seq_lengths, group_rows)
    cosine, sine = rope_tables(where_at[0], HD)
    rows_one, qkv = norm_project(order, input_blocks, w_qkv_all, cosine, sine)
    attended, logs = attention(order, qkv, first_at, pairs)
    near, far = way.sum_rows(lambda v: project(v[0], w_output_all), [attended])
    mid, unit_two, inverse_two = middle(order, layer_in, near, far)
    rows_two = jnp.concatenate(way.gather_rows(unit_two), axis=0)
    gate_pre = project(rows_two, w_gate_all)
    up_pre = project(rows_two, w_up_all)
    hidden = (jax.nn.silu(gate_pre) * up_pre).astype(BF16)
    grad_rows = held_rows(order, way.gather_rows(out_grad))
    grad_down_sh = way.sum_grads(hidden, grad_rows, 1)
    near, far = way.sum_rows(lambda v: project(v[0], w_down_all), [hidden])
    layer_out = layer_end(order, mid, near, far)

    grad_hidden = project_back(grad_rows, w_down_all)
    sigmoid_gate = jax.nn.sigmoid(gate_pre)
    grad_gate = (
        grad_hidden * up_pre * sigmoid_gate * (1.0 + gate_pre * (1.0 - sigmoid_gate))
    ).astype(BF16)
    grad_up = (grad_hidden * gate_pre * sigmoid_gate).astype(BF16)
    near, far = way.sum_rows(
        lambda v: project_back(v[0], w_gate_all) + project_back(v[1], w_up_all),
        [grad_gate, grad_up],
    )
    grad_gate_sh = way.sum_grads(rows_two, grad_gate, 0)
    grad_up_sh = way.sum_grads(rows_two, grad_up, 0)
    grad_mid, grad_mid_low = middle_back(order, out_grad, mid, inverse_two, near, far)
    grad_mid_rows = jnp.concatenate(way.gather_rows(grad_mid_low), axis=0)
    grad_attended = project_back(grad_mid_rows, w_output_all).astype(BF16)
    grad_output_sh = way.sum_grads(attended, grad_mid_rows, 1)
    grad_query, grad_kv = attention_back(
        order, qkv, first_at, logs, grad_attended, cosine, sine, pairs
    )
    grad_qkv = jnp.concatenate([grad_query, grad_kv], axis=1)
    near, far = way.sum_rows(lambda v: project_back(v[0], w_qkv_all), [grad_qkv])
    in_grad = input_back(order, layer_in, grad_mid, near, far)
    grad_qkv_sh = way.sum_grads(rows_one, grad_qkv, 0)
    gain_one_term = jnp.sum(grad_qkv_sh * w_qkv.astype(F32), axis=1)
    gain_two_term = jnp.sum(
        grad_gate_sh * w_gate.astype(F32) + grad_up_sh * w_up.astype(F32), axis=1
    )
    gain_one_grad, gain_two_grad = way.share_gains([gain_one_term, gain_two_term])
    grad_qkv_sh = grad_qkv_sh * gain_one
    return (
        layer_out,
        in_grad,
        gain_one_grad,
        grad_qkv_sh[:, :query_width],
        grad_qkv_sh[:, query_width : query_width + key_width],
        grad_qkv_sh[:, query_width + key_width :],
        grad_output_sh,
        gain_two_grad,
        grad_gate_sh * gain_two,
        grad_up_sh * gain_two,
        grad_down_sh,
    )


def solution(mesh):
    placed = (
        P(("fsdp", "tp"), None),
        P("fsdp", None),
        P(("fsdp", "tp")),
        P("fsdp", "tp"),
        P("fsdp", "tp"),
        P("fsdp", "tp"),
        P("tp", "fsdp"),
        P(("fsdp", "tp")),
        P("fsdp", "tp"),
        P("fsdp", "tp"),
        P("tp", "fsdp"),
        P(("fsdp", "tp"), None),
    )
    return jax.shard_map(
        local,
        mesh=mesh,
        in_specs=placed,
        out_specs=(
            P(("fsdp", "tp"), None),
            P(("fsdp", "tp"), None),
            P(("fsdp", "tp")),
            P("fsdp", "tp"),
            P("fsdp", "tp"),
            P("fsdp", "tp"),
            P("tp", "fsdp"),
            P(("fsdp", "tp")),
            P("fsdp", "tp"),
            P("fsdp", "tp"),
            P("tp", "fsdp"),
        ),
        check_vma=False,
    )
```

```python
import math

import jax
import jax.numpy as jnp
from jax import lax
from jax.experimental import pallas as pl
from jax.experimental.pallas import tpu as pltpu
from jax.sharding import PartitionSpec as P

HD = 64
MAXLEN = 512
EPSILON = 1e-05
ROPE_BASE = 10000.0
MASKED_OUT = -1e30
TILE = 512
COLUMN_BLOCKS = 8
ROW_BLOCKS = 4
VMEM = 56 * 1024 * 1024
F32 = jnp.float32
BF16 = jnp.bfloat16


def positions(lengths, count):
    starts = jnp.cumsum(lengths, axis=-1) - lengths
    indices = jnp.arange(count, dtype=jnp.int32)
    inside = (indices[None, :, None] >= starts[:, None, :]) & (
        indices[None, :, None] < (starts + lengths)[:, None, :]
    )
    first_at = jnp.sum(jnp.where(inside, starts[:, None, :], 0), axis=-1)
    return first_at, indices[None, :] - first_at


def rope_tables(where_at, width):
    half_width = width // 2
    inverse_freq = ROPE_BASE ** (-(jnp.arange(half_width, dtype=F32) * 2.0 / width))
    angles = where_at.astype(F32)[:, None] * inverse_freq[None, :]
    cosine, sine = jnp.cos(angles), jnp.sin(angles)
    return jnp.concatenate([cosine] * 4, axis=1), jnp.concatenate([sine] * 4, axis=1)


def project(left, weight):
    return jnp.dot(left, weight, preferred_element_type=F32)


def project_back(grad, weight):
    return jnp.einsum("tc,dc->td", grad, weight, preferred_element_type=F32)


def outer(left, right):
    return jnp.einsum("ta,tb->ab", left, right, preferred_element_type=F32)


def call(body, outs, operands, flops=0, nbytes=0, **more):
    return pl.pallas_call(
        body,
        out_shape=outs,
        compiler_params=pltpu.CompilerParams(vmem_limit_bytes=VMEM),
        cost_estimate=pl.CostEstimate(flops=flops, bytes_accessed=nbytes, transcendentals=0),
        **more,
    )(*operands)


def whole(count):
    return [pl.BlockSpec(memory_space=pltpu.VMEM)] * count


SCALARS = pl.BlockSpec(memory_space=pltpu.SMEM)


def spans(order, width):
    step = width // COLUMN_BLOCKS
    return [
        (slice(j * step, (j + 1) * step), pl.ds(pl.multiple_of(order[j] * step, step), step))
        for j in range(COLUMN_BLOCKS)
    ]


def turned(values, lanes):
    width = values.shape[-1]
    first = (lanes % HD) < HD // 2
    return jnp.where(
        first, -pltpu.roll(values, width - HD // 2, 1), pltpu.roll(values, HD // 2, 1)
    )


def norm_project(order, gathered, weights_low, weights_high, cosine, sine):
    count, width = gathered.shape[0] // ROW_BLOCKS, gathered.shape[1]
    half, total = weights_low.shape
    kv = 2 * HD

    def body(order, x, low, high, c, s, normed, out):
        values = x[...].astype(F32)
        inverse = lax.rsqrt(jnp.mean(values * values, axis=-1, keepdims=True) + EPSILON)
        for held, true in spans(order, width):
            normed[:, held] = (x[:, true].astype(F32) * inverse).astype(BF16)
        product = project(normed[:, :half], low[...])
        product = product + project(normed[:, half:], high[...])
        cos, sin = c[...], s[...]
        lanes = lax.broadcasted_iota(jnp.int32, cos.shape, 1)
        for at in range(0, total, 128):
            part = product[:, at : at + 128]
            if at + 128 > total - kv:
                co, si = jnp.where(lanes < HD, cos, 1.0), jnp.where(lanes < HD, sin, 0.0)
            else:
                co, si = cos, sin
            out[:, at : at + 128] = (part * co + turned(part, lanes) * si).astype(BF16)

    def tiles(columns):
        return pl.BlockSpec((count, columns), lambda i: (i, 0))

    weight = pl.BlockSpec((half, total), lambda i: (0, 0), pipeline_mode=pl.Buffered(1))
    return call(
        body,
        (
            jax.ShapeDtypeStruct((ROW_BLOCKS * count, width), BF16),
            jax.ShapeDtypeStruct((ROW_BLOCKS * count, total), BF16),
        ),
        (order, gathered, weights_low, weights_high, cosine, sine),
        flops=2 * ROW_BLOCKS * count * width * total,
        nbytes=2 * (2 * ROW_BLOCKS * count * width + width * total),
        grid=(ROW_BLOCKS,),
        in_specs=[SCALARS, tiles(width), weight, weight, tiles(2 * HD), tiles(2 * HD)],
        out_specs=(tiles(width), tiles(total)),
    )


def window(i, span):
    return max(0, i * span - MAXLEN), (i + 1) * span


def shown(first, i, span):
    low, high = window(i, span)
    keys = low + lax.broadcasted_iota(jnp.int32, (high - low, span), 0)
    rows = i * span + lax.broadcasted_iota(jnp.int32, (high - low, span), 1)
    return (keys <= rows) & (keys >= first[:, i * span : (i + 1) * span])


def dot_nt(left, right):
    return lax.dot_general(left, right, (((1,), (1,)), ((), ())), preferred_element_type=F32)


def dot_tn(left, right):
    return lax.dot_general(left, right, (((0,), (0,)), ((), ())), preferred_element_type=F32)


def attention(qkv, first, pairs):
    rows = qkv.shape[0]
    span = rows // ROW_BLOCKS
    width = 2 * HD

    def body(q, kv, first, out, logs):
        for i in range(ROW_BLOCKS):
            low, high = window(i, span)
            allowed = shown(first, i, span)
            keys, values = kv[low:high, :HD], kv[low:high, HD:]
            results = []
            for h in range(2):
                queries = q[i * span : (i + 1) * span, h * HD : (h + 1) * HD] * 0.125
                scores = jnp.where(allowed, dot_nt(keys, queries.astype(BF16)), MASKED_OUT)
                top = jnp.max(scores, axis=0, keepdims=True)
                shares = jnp.exp(scores - top)
                total = jnp.sum(shares, axis=0, keepdims=True)
                mixed = dot_tn(values, shares.astype(BF16)) / total
                results.append(mixed)
                logs[0, h : h + 1, i * span : (i + 1) * span] = top + jnp.log(total)
            both = jnp.concatenate(results, axis=0)
            out[i * span : (i + 1) * span, :] = both.T.astype(BF16)

    return call(
        body,
        (
            jax.ShapeDtypeStruct((rows, pairs * width), BF16),
            jax.ShapeDtypeStruct((pairs, 2, rows), F32),
        ),
        (qkv, qkv, first),
        flops=4 * rows * 768 * HD * 2 * pairs * 8,
        nbytes=2 * rows * pairs * width * 2,
        grid=(pairs,),
        in_specs=[
            pl.BlockSpec((rows, width), lambda p: (0, p)),
            pl.BlockSpec((rows, width), lambda p: (0, pairs)),
            pl.BlockSpec((1, rows), lambda p: (0, 0)),
        ],
        out_specs=(
            pl.BlockSpec((rows, width), lambda p: (0, p)),
            pl.BlockSpec((1, 2, rows), lambda p: (p, 0, 0)),
        ),
    )


def attention_back(qkv, first, logs, grads, cosine, sine, pairs):
    rows = qkv.shape[0]
    span = rows // ROW_BLOCKS
    width = 2 * HD

    def body(q, kv, first, logs, grad, c, s, dq, dkv, total):
        @pl.when(pl.program_id(0) == 0)
        def _():
            total[...] = jnp.zeros_like(total)

        lanes = lax.broadcasted_iota(jnp.int32, (span, width), 1)
        for i in range(ROW_BLOCKS):
            low, high = window(i, span)
            allowed = shown(first, i, span)
            at = slice(i * span, (i + 1) * span)
            keys, values = kv[low:high, :HD], kv[low:high, HD:]
            results, key_part, value_part = [], 0.0, 0.0
            for h in range(2):
                head = slice(h * HD, (h + 1) * HD)
                queries = (q[i * span : (i + 1) * span, head] * 0.125).astype(BF16)
                came = grad[at, head]
                log = logs[0, h : h + 1, i * span : (i + 1) * span]
                shares = jnp.where(allowed, jnp.exp(dot_nt(keys, queries) - log), 0.0)
                change = dot_nt(values, came)
                inner = jnp.sum(shares * change, axis=0, keepdims=True)
                score_grads = (shares * (change - inner)).astype(BF16)
                value_part += jnp.dot(shares.astype(BF16), came, preferred_element_type=F32)
                key_part += jnp.dot(score_grads, queries, preferred_element_type=F32)
                results.append(dot_tn(keys, score_grads) * 0.125)
            total[low:high, :] += jnp.concatenate([key_part, value_part], axis=1)
            query_grad = jnp.concatenate(results, axis=0).T
            dq[at, :] = (
                query_grad * c[at, :] - turned(query_grad * s[at, :], lanes)
            ).astype(BF16)

        @pl.when(pl.program_id(0) == pairs - 1)
        def _():
            for i in range(ROW_BLOCKS):
                at = slice(i * span, (i + 1) * span)
                cos = jnp.where(lanes < HD, c[at, :], 1.0)
                sin = jnp.where(lanes < HD, s[at, :], 0.0)
                part = total[at, :]
                dkv[at, :] = (
                    part * cos - turned(part * sin, lanes)
                ).astype(BF16)

    return call(
        body,
        (
            jax.ShapeDtypeStruct((rows, pairs * width), BF16),
            jax.ShapeDtypeStruct((rows, width), BF16),
        ),
        (qkv, qkv, first, logs, grads, cosine, sine),
        flops=10 * rows * 768 * HD * 2 * pairs * 8,
        nbytes=2 * rows * pairs * width * 3,
        grid=(pairs,),
        in_specs=[
            pl.BlockSpec((rows, width), lambda p: (0, p)),
            pl.BlockSpec((rows, width), lambda p: (0, pairs)),
            pl.BlockSpec((1, rows), lambda p: (0, 0)),
            pl.BlockSpec((1, 2, rows), lambda p: (p, 0, 0)),
            pl.BlockSpec((rows, width), lambda p: (0, p)),
            pl.BlockSpec((rows, width), lambda p: (0, 0)),
            pl.BlockSpec((rows, width), lambda p: (0, 0)),
        ],
        out_specs=(
            pl.BlockSpec((rows, width), lambda p: (0, p)),
            pl.BlockSpec((rows, width), lambda p: (0, 0)),
        ),
        scratch_shapes=[pltpu.VMEM((rows, width), F32)],
    )


def row_kernel(multiply, left, weights, width, extra, outs, finish, tile=TILE):
    rows = left[0].shape[0]
    tile = min(tile, rows)
    many = len(left), len(left) + len(weights), len(left) + len(weights) + len(extra)

    def body(*refs):
        product = multiply(refs[: many[0]], refs[many[0] : many[1]])
        finish(product, refs[many[1] : many[2]], refs[many[2] :])

    def tiles(columns):
        return pl.BlockSpec((tile, columns), lambda i: (i, 0))

    inner = sum(weight.size for weight in weights)
    return pl.pallas_call(
        body,
        out_shape=tuple(jax.ShapeDtypeStruct((rows, width), kind) for kind in outs),
        grid=(rows // tile,),
        in_specs=[tiles(v.shape[1]) for v in left]
        + [
            pl.BlockSpec(v.shape, lambda i: (0, 0), pipeline_mode=pl.Buffered(1)) for v in weights
        ]
        + [tiles(width)] * len(extra),
        out_specs=tuple([tiles(width)] * len(outs)),
        compiler_params=pltpu.CompilerParams(vmem_limit_bytes=VMEM),
        cost_estimate=pl.CostEstimate(
            flops=2 * rows * inner, bytes_accessed=2 * inner, transcendentals=0
        ),
    )(*left, *weights, *extra)


def down_rows(left, weights):
    (x,) = left
    total, at = None, 0
    for w in weights:
        term = jnp.dot(x[:, at : at + w.shape[0]], w[...], preferred_element_type=F32)
        total, at = term if total is None else total + term, at + w.shape[0]
    return total


def gate_part(rows_two, weights):
    def finish(product, extra, outs):
        outs[0][...] = product

    return row_kernel(down_rows, [rows_two], weights, weights[0].shape[1], [], [F32], finish)[0]


def up_part(rows_two, weights, gate_pre):
    def finish(up, extra, outs):
        gate = extra[0][...]
        sigmoid = 1.0 / (1.0 + jnp.exp(-gate))
        silu = gate * sigmoid
        outs[0][...] = (silu * up).astype(BF16)
        outs[1][...] = (up * sigmoid * (1.0 + gate * (1.0 - sigmoid))).astype(BF16)
        outs[2][...] = silu.astype(BF16)

    return row_kernel(
        down_rows, [rows_two], weights, weights[0].shape[1], [gate_pre], [BF16] * 3, finish, 256
    )


def hidden_back(grad_rows, whole_part, pieces, gate_factor, up_factor):
    def multiply(left, weights):
        (x,) = left
        products = [dot_nt(x[...], weights[0][...])]
        if len(weights) > 1:
            step = weights[1].shape[1] // 2
            total = None
            for a, w in enumerate(weights[1:]):
                term = dot_nt(x[:, a * step : (a + 1) * step], w[:, :step])
                term += dot_nt(x[:, (4 + a) * step : (5 + a) * step], w[:, step:])
                total = term if total is None else total + term
            products.append(total)
        return products

    def finish(products, extra, outs):
        at = 0
        for product in products:
            columns = slice(at, at + product.shape[1])
            for factor, out in zip(extra, outs, strict=True):
                out[:, columns] = (product * factor[:, columns].astype(F32)).astype(BF16)
            at += product.shape[1]

    return row_kernel(
        multiply,
        [grad_rows],
        [whole_part, *pieces],
        gate_factor.shape[1],
        [gate_factor, up_factor],
        [BF16] * 2,
        finish,
    )


def feed_back(grad_gate, grad_up, w_gate, w_up):
    def multiply(left, weights):
        return dot_nt(left[0][...], weights[0][...]) + dot_nt(left[1][...], weights[1][...])

    def finish(product, extra, outs):
        outs[0][...] = product.astype(BF16)

    return row_kernel(
        multiply, [grad_gate, grad_up], [w_gate, w_up], w_gate.shape[0], [], [BF16], finish
    )[0]


def held_rows(order, gathered):
    rows, width = gathered.shape
    count = rows // ROW_BLOCKS

    def body(order, x, out):
        for held, true in spans(order, width):
            out[:, held] = x[:, true]

    spec = pl.BlockSpec((count, width), lambda i: (i, 0))
    return call(
        body,
        jax.ShapeDtypeStruct((rows, width), BF16),
        (order, gathered),
        nbytes=4 * rows * width,
        grid=(ROW_BLOCKS,),
        in_specs=[SCALARS, spec],
        out_specs=spec,
    )


def middle(order, layer_in, came):
    count, width = layer_in.shape

    def body(order, x, came, mid, unit, inverse):
        for held, true in spans(order, width):
            mid[:, held] = x[:, true].astype(F32) + came[:, held].astype(F32)
        values = mid[...]
        scale = lax.rsqrt(jnp.mean(values * values, axis=-1, keepdims=True) + EPSILON)
        inverse[...] = scale
        unit[...] = (values * scale).astype(BF16)

    return call(
        body,
        (
            jax.ShapeDtypeStruct((count, width), F32),
            jax.ShapeDtypeStruct((count, width), BF16),
            jax.ShapeDtypeStruct((count, 1), F32),
        ),
        (order, layer_in, came),
        nbytes=20 * count * width,
        in_specs=[SCALARS] + whole(2),
        out_specs=tuple(whole(3)),
    )


def layer_end(order, mid, came):
    count, width = mid.shape

    def body(order, mid, came, out):
        for held, true in spans(order, width):
            total = mid[:, held] + came[:, held].astype(F32)
            out[:, true] = total.astype(BF16)

    return call(
        body,
        jax.ShapeDtypeStruct((count, width), BF16),
        (order, mid, came),
        nbytes=14 * count * width,
        in_specs=[SCALARS] + whole(2),
        out_specs=whole(1)[0],
    )


def middle_back(order, out_grad, mid, inverse, came):
    count, width = mid.shape

    def body(order, dy, mid, inverse, came, grad, low):
        scale = inverse[...]
        grad_unit = came[...].astype(F32)
        unit = mid[...] * scale
        inner = jnp.mean(grad_unit * unit, axis=-1, keepdims=True)
        grad[...] = scale * (grad_unit - unit * inner)
        for held, true in spans(order, width):
            total = grad[:, held] + dy[:, true].astype(F32)
            grad[:, held] = total
            low[:, held] = total.astype(BF16)

    return call(
        body,
        (
            jax.ShapeDtypeStruct((count, width), F32),
            jax.ShapeDtypeStruct((count, width), BF16),
        ),
        (order, out_grad, mid, inverse, came),
        nbytes=20 * count * width,
        in_specs=[SCALARS] + whole(4),
        out_specs=tuple(whole(2)),
    )


def input_back(order, layer_in, grad_mid, came):
    count, width = grad_mid.shape

    def body(order, x, grad_mid, came, out, unit):
        values = x[...].astype(F32)
        scale = lax.rsqrt(jnp.mean(values * values, axis=-1, keepdims=True) + EPSILON)
        for held, true in spans(order, width):
            unit[:, held] = x[:, true].astype(F32) * scale
        grad_unit = came[...].astype(F32)
        inner = jnp.mean(grad_unit * unit[...], axis=-1, keepdims=True)
        unit[...] = grad_mid[...] + scale * (grad_unit - unit[...] * inner)
        for held, true in spans(order, width):
            out[:, true] = unit[:, held]

    return call(
        body,
        jax.ShapeDtypeStruct((count, width), F32),
        (order, layer_in, grad_mid, came),
        nbytes=16 * count * width,
        in_specs=[SCALARS] + whole(3),
        out_specs=whole(1)[0],
        scratch_shapes=[pltpu.VMEM((count, width), F32)],
    )


def gather_rows(rows):
    return lax.all_gather(rows, "tp", axis=0, tiled=True)


def sum_rows(partial):
    return lax.psum_scatter(partial, "tp", scatter_dimension=0, tiled=True)


class Taker:
    def __init__(self, held):
        self.held = held

    def __getattr__(self, name):
        return self.held.pop(name)


class Held(dict):
    __getattr__ = dict.__getitem__

    @property
    def out(self):
        return Taker(self)


def fence(state):
    if isinstance(state, Held):
        return Held(lax.optimization_barrier(dict(state)))
    return lax.optimization_barrier(state)


def zed(values, step):
    return lax.ppermute(values, "fsdp", [(i, i ^ (2 * step)) for i in range(8)])


def why(values):
    return lax.ppermute(values, "fsdp", [(i, i ^ 1) for i in range(8)])


def teep(values, mask):
    return lax.ppermute(values, "tp", [(i, i ^ mask) for i in range(4)])


def own_gains(gains):
    t = lax.axis_index("tp")
    own = jnp.stack(gains)
    near = jnp.stack([own, teep(own, 1)], axis=1)
    near = jnp.where((t & 1) == 1, near[:, ::-1], near)
    both = jnp.stack([near, teep(near, 2)], axis=1)
    both = jnp.where((t >> 1) == 1, both[:, ::-1], both)
    return both.reshape(len(gains), -1)


def share_gains(terms):
    t = lax.axis_index("tp")
    both = jnp.stack(terms).reshape(len(terms), 2, 2, -1)
    both = jnp.where((t >> 1) == 1, both[:, ::-1], both)
    both = both[:, 0] + teep(both[:, 1], 2)
    both = jnp.where((t & 1) == 1, both[:, ::-1], both)
    both = both[:, 0] + teep(both[:, 1], 1)
    return [both[i] for i in range(len(terms))]


def part(left, right, axis, first, last):
    step = (left if axis == 0 else right).shape[1] // COLUMN_BLOCKS
    at = slice(first * step, last * step)
    if axis == 0:
        return outer(left[:, at], right)
    return outer(left, right[:, at])


def sliced(values, axis, i, count):
    size = values.shape[axis] // count
    return lax.slice_in_dim(values, i * size, (i + 1) * size, axis=axis)


def joined(values, axis, i, came, j, count):
    return sliced(values, axis, i, 4).astype(F32) + sliced(came, axis, j, count).astype(F32)


def summed(total, came):
    for values in came:
        total = total + values.astype(F32)
    return total


def scheduled(
    layer_in,
    seq_lengths,
    attn_gain,
    w_query,
    w_key,
    w_value,
    w_output,
    mlp_gain,
    w_gate,
    w_up,
    w_down,
    out_grad,
):
    group_rows = layer_in.shape[0] * lax.axis_size("tp")
    query_width, key_width = w_query.shape[1], w_key.shape[1]
    pairs = query_width // (2 * HD)
    masks = [2 * a + b for b in (0, 1) for a in range(4)]
    order = lax.axis_index("fsdp") ^ jnp.array(masks, jnp.int32)
    cut = w_down.shape[0] // 256 * 128 + 128

    input_rows = gather_rows(layer_in)
    down_high = w_down[cut:]
    v = Held(
        o=jnp.concatenate([w_output] + [zed(w_output, a) for a in (1, 2, 3)], axis=1),
        dq=[jnp.concatenate([down_high, why(down_high)], axis=1)],
        down_low=w_down[:cut],
        gains=own_gains([attn_gain, mlp_gain])[:, :, None],
        order=order,
        layer_in=layer_in,
        out_grad=out_grad,
        w_qkv=jnp.concatenate([w_query, w_key, w_value], axis=1),
        w_gate=w_gate,
        w_up=w_up,
    )
    first_at, where_at = positions(seq_lengths, group_rows)
    v.update(first_at=first_at, tables=rope_tables(where_at[0], HD))
    v = fence(v)

    q = (v.w_qkv.astype(F32) * v.gains[0]).astype(BF16)
    q = jnp.concatenate([q] + [zed(q, a) for a in (1, 2, 3)], axis=0)
    oy = why(v.o)
    grad_gathered = gather_rows(v.out_grad)
    g = [(v.w_gate.astype(F32) * v.gains[1]).astype(BF16)]
    u = [(v.w_up.astype(F32) * v.gains[1]).astype(BF16)]
    v.update(q=q, oy=oy, g=g, u=u)
    v = fence(v)

    g = v.g + [zed(v.g[0], 1), zed(v.g[0], 2)]
    qy = why(v.q)
    w_output_all = jnp.concatenate([v.out.o, v.out.oy], axis=1)
    v.update(g=g, qy=qy, w_output_all=w_output_all)
    v = fence(v)

    g = v.g + [zed(v.g[0], 3)]
    gy = [why(v.g[0]), why(v.g[1])]
    rows_one, qkv = norm_project(v.order, input_rows, v.q, v.qy, *v.tables)
    attended, logs = attention(qkv, v.first_at, pairs)
    partial = project(attended, v.w_output_all).astype(BF16)
    v.update(g=g, gy=gy, rows_one=rows_one, qkv=qkv, attended=attended, logs=logs)
    v.update(partial=partial)
    v = fence(v)

    came = sum_rows(v.out.partial)
    u = v.u + [zed(v.u[0], 1), zed(v.u[0], 2)]
    gy = v.gy + [why(v.g[2]), why(v.g[3])]
    grad_rows = held_rows(v.order, grad_gathered)
    v.update(u=u, gy=gy, grad_rows=grad_rows)
    v = fence(v)

    u = v.u + [zed(v.u[0], 3)]
    uy = [why(v.u[0]), why(v.u[1])]
    w_gate_all = jnp.concatenate(v.out.g + v.out.gy, axis=0)
    mid, unit_two, inverse_two = middle(v.order, v.layer_in, came)
    v.update(u=u, uy=uy, w_gate_all=w_gate_all)
    v.update(mid=mid, unit_two=unit_two, inverse_two=inverse_two)
    v = fence(v)

    low = v.out.down_low
    low = [low] + [zed(low, a) for a in (1, 2, 3)]
    uy = [why(v.u[2]), why(v.u[3])]
    w_up_most = jnp.concatenate(v.out.u + v.out.uy, axis=0)
    rows_two = gather_rows(v.out.unit_two)
    low = jnp.concatenate(low, axis=1)
    v.update(low=low, uy=uy, w_up_most=w_up_most)
    v = fence(v)

    dq = v.dq + [zed(v.dq[0], 1), zed(v.dq[0], 2)]
    low_across = why(v.low)
    gate_pre = gate_part(rows_two, [v.w_gate_all])
    hidden, gate_factor, up_factor = up_part(rows_two, [v.w_up_most, *v.uy], gate_pre)
    down_away = [part(hidden, v.grad_rows, 1, 6, 8).astype(BF16)]
    v.update(dq=dq, low_across=low_across, rows_two=rows_two, hidden=hidden)
    v.update(factors=[gate_factor, up_factor], down_away=down_away)
    v = fence(v)

    dq = v.dq + [zed(v.dq[0], 3)]
    first = why(v.down_away[0])
    down_away = part(v.hidden, v.grad_rows, 1, 4, 6).astype(BF16)
    down_kept = part(v.hidden, v.grad_rows, 1, 0, 4).astype(BF16)
    low_all = jnp.concatenate([v.out.low, v.out.low_across], axis=1)
    w_up_all = jnp.concatenate([v.out.w_up_most, *v.out.uy], axis=0)
    v.update(dq=dq, first=first, down_away=down_away, down_kept=down_kept)
    v.update(low_all=low_all, w_up_all=w_up_all)
    v = fence(v)

    far = zed(joined(v.down_kept, 1, 3, v.first, 1, 2).astype(BF16), 3)
    second = why(v.down_away)
    grad_gate, grad_up = hidden_back(v.grad_rows, v.low_all, v.dq, *v.out.factors)
    partial = feed_back(grad_gate, grad_up, v.w_gate_all, v.w_up_all)
    gate_away = [part(v.rows_two, grad_gate, 0, 6, 8).astype(BF16)]
    v.update(far=far, second=second, grad_gate=grad_gate, grad_up=grad_up, gate_away=gate_away)
    v.update(partial=partial)
    v = fence(v)

    came = sum_rows(v.out.partial)
    near = [
        zed(joined(v.down_kept, 1, 1, v.second, 1, 2).astype(BF16), 1),
        zed(joined(v.down_kept, 1, 2, v.first, 0, 2).astype(BF16), 2),
    ]
    down_own = joined(v.out.down_kept, 1, 0, v.second, 0, 2)
    first = why(v.gate_away[0])
    gate_away = part(v.rows_two, v.grad_gate, 0, 4, 6).astype(BF16)
    gate_kept = part(v.rows_two, v.grad_gate, 0, 0, 4).astype(BF16)
    up_away = [part(v.rows_two, v.grad_up, 0, 6, 8).astype(BF16)]
    v.update(near=near, down_own=down_own, first=first)
    v.update(gate_away=gate_away, gate_kept=gate_kept, up_away=up_away)
    v = fence(v)

    grad_down_sh = summed(v.out.down_own, [v.far, *v.near])
    far = zed(joined(v.gate_kept, 0, 3, v.first, 1, 2).astype(BF16), 3)
    second = why(v.gate_away)
    grad_mid, grad_mid_low = middle_back(
        v.order, v.out_grad, v.mid, v.inverse_two, came
    )
    up_away = v.up_away + [part(v.rows_two, v.grad_up, 0, 4, 6).astype(BF16)]
    up_kept = part(v.rows_two, v.grad_up, 0, 0, 4).astype(BF16)
    v.update(grad_down_sh=grad_down_sh, far=far, second=second, grad_mid=grad_mid)
    v.update(grad_mid_low=grad_mid_low)
    v.update(up_away=up_away, up_kept=up_kept)
    v = fence(v)

    grad_mid_rows = gather_rows(v.out.grad_mid_low)
    near = [
        zed(joined(v.gate_kept, 0, 1, v.second, 1, 2).astype(BF16), 1),
        zed(joined(v.gate_kept, 0, 2, v.first, 0, 2).astype(BF16), 2),
    ]
    gate_own = joined(v.out.gate_kept, 0, 0, v.second, 0, 2)
    first = why(v.up_away[0])
    dq = v.out.dq
    half = dq[0].shape[1] // 2
    high_all = jnp.concatenate([w[:, :half] for w in dq] + [w[:, half:] for w in dq], axis=1)
    low_all = v.out.low_all
    partial = project(v.hidden[:, :cut], low_all)
    output_part = (partial + project(v.hidden[:, cut:], high_all)).astype(BF16)
    v.update(near=near, gate_own=gate_own, first=first, output_part=output_part)
    v = fence(v)

    gate_terms = [v.far, *v.near]
    far = zed(joined(v.up_kept, 0, 3, v.first, 1, 2).astype(BF16), 3)
    second = why(v.up_away[1])
    grad_attended = project_back(grad_mid_rows, v.w_output_all).astype(BF16)
    grad_query, grad_kv = attention_back(
        v.qkv, v.first_at, v.logs, grad_attended, *v.tables, pairs
    )
    grad_qkv = jnp.concatenate([grad_query, grad_kv], axis=1)
    came_out = sum_rows(v.output_part)
    v.update(gate_terms=gate_terms, far=far, second=second)
    v.update(grad_qkv=grad_qkv, grad_mid_rows=grad_mid_rows)
    v = fence(v)

    near = [
        zed(joined(v.up_kept, 0, 1, v.second, 1, 2).astype(BF16), 1),
        zed(joined(v.up_kept, 0, 2, v.first, 0, 2).astype(BF16), 2),
    ]
    up_own = joined(v.out.up_kept, 0, 0, v.second, 0, 2)
    first = why(part(v.rows_one, v.grad_qkv, 0, 4, 8).astype(BF16))
    w_qkv_all = jnp.concatenate([v.q, v.qy], axis=0)
    partial = project_back(v.grad_qkv, w_qkv_all).astype(BF16)
    qkv_kept = part(v.rows_one, v.grad_qkv, 0, 0, 4).astype(BF16)
    output_away = part(v.attended, v.grad_mid_rows, 1, 4, 8).astype(BF16)
    grad_gate_sh = summed(v.out.gate_own, v.out.gate_terms)
    v.update(near=near, up_own=up_own, first=first, qkv_kept=qkv_kept, output_away=output_away)
    v.update(partial=partial, grad_gate_sh=grad_gate_sh)
    v = fence(v)

    came = sum_rows(v.out.partial)
    pieces = [
        zed(joined(v.qkv_kept, 0, a, v.first, a, 4).astype(BF16), a) for a in (1, 2, 3)
    ]
    qkv_own = joined(v.qkv_kept, 0, 0, v.first, 0, 4)
    second = why(v.output_away)
    gain_one, gain_two = v.gains[0], v.gains[1]
    grad_gate_sh = v.grad_gate_sh
    grad_up_sh = summed(v.out.up_own, [v.far, *v.near])
    gain_two_term = jnp.sum(
        grad_gate_sh * v.w_gate.astype(F32) + grad_up_sh * v.w_up.astype(F32), axis=1
    )
    output_kept = part(v.attended, v.grad_mid_rows, 1, 0, 4).astype(BF16)
    layer_out = layer_end(v.order, v.mid, came_out)
    v.update(pieces=pieces, qkv_own=qkv_own, second=second, gain_two_term=gain_two_term)
    v.update(grad_gate_sh=grad_gate_sh * gain_two, grad_up_sh=grad_up_sh * gain_two)
    v.update(output_kept=output_kept, layer_out=layer_out)
    v = fence(v)

    pieces = [
        zed(joined(v.output_kept, 1, a, v.second, a, 4).astype(BF16), a) for a in (1, 2, 3)
    ]
    output_own = joined(v.output_kept, 1, 0, v.second, 0, 4)
    grad_qkv_sh = summed(v.qkv_own, v.pieces)
    gain_one_term = jnp.sum(grad_qkv_sh * v.w_qkv.astype(F32), axis=1)
    gain_one_grad, gain_two_grad = share_gains([gain_one_term, v.gain_two_term])
    grad_qkv_sh = grad_qkv_sh * v.gains[0]
    in_grad = input_back(v.order, v.layer_in, v.grad_mid, came)
    in_grad, output_own = fence((in_grad, output_own))
    return (
        v.layer_out,
        in_grad,
        gain_one_grad,
        grad_qkv_sh[:, :query_width],
        grad_qkv_sh[:, query_width : query_width + key_width],
        grad_qkv_sh[:, query_width + key_width :],
        summed(output_own, pieces),
        gain_two_grad,
        v.grad_gate_sh,
        v.grad_up_sh,
        v.grad_down_sh,
    )


def direct(
    layer_in,
    seq_lengths,
    attn_gain,
    w_query,
    w_key,
    w_value,
    w_output,
    mlp_gain,
    w_gate,
    w_up,
    w_down,
    out_grad,
):
    def gather(shard, axis):
        return lax.all_gather(shard, "fsdp", axis=axis, tiled=True)

    def scatter(left, right, axis):
        total = outer(left, right).astype(BF16)
        return lax.psum_scatter(total, "fsdp", scatter_dimension=axis, tiled=True).astype(F32)

    group_rows = layer_in.shape[0] * lax.axis_size("tp")
    query_width, key_width = w_query.shape[1], w_key.shape[1]
    pairs = query_width // (2 * HD)
    order = jnp.arange(COLUMN_BLOCKS, dtype=jnp.int32)
    gain_one, gain_two = [
        lax.all_gather(gain, "tp", axis=0, tiled=True)[:, None] for gain in (attn_gain, mlp_gain)
    ]
    w_qkv = jnp.concatenate([w_query, w_key, w_value], axis=1)
    w_output_all = gather(w_output, 1)
    w_qkv_all = gather((w_qkv.astype(F32) * gain_one).astype(BF16), 0)
    w_gate_all = gather((w_gate.astype(F32) * gain_two).astype(BF16), 0)
    w_up_all = gather((w_up.astype(F32) * gain_two).astype(BF16), 0)
    w_down_all = gather(w_down, 1)
    first_at, where_at = positions(seq_lengths, group_rows)
    cosine, sine = rope_tables(where_at[0], HD)
    rows_one, qkv = norm_project(
        order, gather_rows(layer_in), *jnp.split(w_qkv_all, 2), cosine, sine
    )
    grad_rows = held_rows(order, gather_rows(out_grad))
    attended, logs = attention(qkv, first_at, pairs)
    came = sum_rows(project(attended, w_output_all).astype(BF16))
    mid, unit_two, inverse_two = middle(order, layer_in, came)
    rows_two = gather_rows(unit_two)
    gate_pre = gate_part(rows_two, [w_gate_all])
    hidden, gate_factor, up_factor = up_part(rows_two, [w_up_all], gate_pre)
    grad_down_sh = scatter(hidden, grad_rows, 1)
    came = sum_rows(project(hidden, w_down_all).astype(BF16))
    layer_out = layer_end(order, mid, came)
    grad_gate, grad_up = hidden_back(grad_rows, w_down_all, [], gate_factor, up_factor)
    came = sum_rows(feed_back(grad_gate, grad_up, w_gate_all, w_up_all))
    grad_gate_sh = scatter(rows_two, grad_gate, 0)
    grad_up_sh = scatter(rows_two, grad_up, 0)
    grad_mid, grad_mid_low = middle_back(order, out_grad, mid, inverse_two, came)
    grad_mid_rows = gather_rows(grad_mid_low)
    grad_attended = project_back(grad_mid_rows, w_output_all).astype(BF16)
    grad_output_sh = scatter(attended, grad_mid_rows, 1)
    grad_query, grad_kv = attention_back(
        qkv, first_at, logs, grad_attended, cosine, sine, pairs
    )
    grad_qkv = jnp.concatenate([grad_query, grad_kv], axis=1)
    came = sum_rows(project_back(grad_qkv, w_qkv_all).astype(BF16))
    in_grad = input_back(order, layer_in, grad_mid, came)
    grad_qkv_sh = scatter(rows_one, grad_qkv, 0)
    gain_one_term = jnp.sum(grad_qkv_sh * w_qkv.astype(F32), axis=1)
    gain_two_term = jnp.sum(
        grad_gate_sh * w_gate.astype(F32) + grad_up_sh * w_up.astype(F32), axis=1
    )
    gain_one_grad, gain_two_grad = [
        lax.psum_scatter(term, "tp", scatter_dimension=0, tiled=True)
        for term in (gain_one_term, gain_two_term)
    ]
    grad_qkv_sh = grad_qkv_sh * gain_one
    return (
        layer_out,
        in_grad,
        gain_one_grad,
        grad_qkv_sh[:, :query_width],
        grad_qkv_sh[:, query_width : query_width + key_width],
        grad_qkv_sh[:, query_width + key_width :],
        grad_output_sh,
        gain_two_grad,
        grad_gate_sh * gain_two,
        grad_up_sh * gain_two,
        grad_down_sh,
    )


def solution(mesh):
    placed = (
        P(("fsdp", "tp"), None),
        P("fsdp", None),
        P(("fsdp", "tp")),
        P("fsdp", "tp"),
        P("fsdp", "tp"),
        P("fsdp", "tp"),
        P("tp", "fsdp"),
        P(("fsdp", "tp")),
        P("fsdp", "tp"),
        P("fsdp", "tp"),
        P("tp", "fsdp"),
        P(("fsdp", "tp"), None),
    )
    paired = (mesh.shape["fsdp"], mesh.shape["tp"]) == (8, 4)
    return jax.shard_map(
        scheduled if paired else direct,
        mesh=mesh,
        in_specs=placed,
        out_specs=(
            P(("fsdp", "tp"), None),
            P(("fsdp", "tp"), None),
            P(("fsdp", "tp")),
            P("fsdp", "tp"),
            P("fsdp", "tp"),
            P("fsdp", "tp"),
            P("tp", "fsdp"),
            P(("fsdp", "tp")),
            P("fsdp", "tp"),
            P("fsdp", "tp"),
            P("tp", "fsdp"),
        ),
        check_vma=False,
    )
```

```python
import math

import jax
import jax.numpy as jnp
from jax import lax
from jax.experimental import pallas as pl
from jax.experimental.pallas import tpu as pltpu
from jax.sharding import PartitionSpec as P

HD = 64
MAXLEN = 512
EPSILON = 1e-05
ROPE_BASE = 10000.0
MASKED_OUT = -1e30
TILE = 512
COLUMN_BLOCKS = 8
ROW_BLOCKS = 4
VMEM = 56 * 1024 * 1024
F32 = jnp.float32
BF16 = jnp.bfloat16


def positions(lengths, count):
    starts = jnp.cumsum(lengths, axis=-1) - lengths
    indices = jnp.arange(count, dtype=jnp.int32)
    inside = (indices[None, :, None] >= starts[:, None, :]) & (
        indices[None, :, None] < (starts + lengths)[:, None, :]
    )
    first_at = jnp.sum(jnp.where(inside, starts[:, None, :], 0), axis=-1)
    return first_at, indices[None, :] - first_at


def rope_tables(where_at, width):
    half_width = width // 2
    inverse_freq = ROPE_BASE ** (-(jnp.arange(half_width, dtype=F32) * 2.0 / width))
    angles = where_at.astype(F32)[:, None] * inverse_freq[None, :]
    cosine, sine = jnp.cos(angles), jnp.sin(angles)
    return jnp.concatenate([cosine] * 4, axis=1), jnp.concatenate([sine] * 4, axis=1)


def project(left, weight):
    return jnp.dot(left, weight, preferred_element_type=F32)


def project_back(grad, weight):
    return jnp.einsum("tc,dc->td", grad, weight, preferred_element_type=F32)


def outer(left, right):
    return jnp.einsum("ta,tb->ab", left, right, preferred_element_type=F32)


def call(body, outs, operands, flops=0, nbytes=0, **more):
    return pl.pallas_call(
        body,
        out_shape=outs,
        compiler_params=pltpu.CompilerParams(vmem_limit_bytes=VMEM),
        cost_estimate=pl.CostEstimate(flops=1, bytes_accessed=1, transcendentals=0),
        **more,
    )(*operands)


def whole(count):
    return [pl.BlockSpec(memory_space=pltpu.VMEM)] * count


SCALARS = pl.BlockSpec(memory_space=pltpu.SMEM)


def spans(order, width):
    step = width // COLUMN_BLOCKS
    return [
        (slice(j * step, (j + 1) * step), pl.ds(pl.multiple_of(order[j] * step, step), step))
        for j in range(COLUMN_BLOCKS)
    ]


def turned(values, lanes):
    width = values.shape[-1]
    first = (lanes % HD) < HD // 2
    return jnp.where(
        first, -pltpu.roll(values, width - HD // 2, 1), pltpu.roll(values, HD // 2, 1)
    )


def unit_rows(order, gathered):
    rows, width = gathered.shape
    count = rows // ROW_BLOCKS

    def body(order, x, out):
        values = x[...].astype(F32)
        inverse = lax.rsqrt(jnp.mean(values * values, axis=-1, keepdims=True) + EPSILON)
        for held, true in spans(order, width):
            out[:, held] = (x[:, true].astype(F32) * inverse).astype(BF16)

    spec = pl.BlockSpec((count, width), lambda i: (i, 0))
    return call(
        body,
        jax.ShapeDtypeStruct((rows, width), BF16),
        (order, gathered),
        nbytes=4 * rows * width,
        grid=(ROW_BLOCKS,),
        in_specs=[SCALARS, spec],
        out_specs=spec,
    )


def project_rotate(rows_one, weights_low, weights_high, cosine, sine):
    rows, width = rows_one.shape
    count = rows // ROW_BLOCKS
    half, total = weights_low.shape
    kv = 2 * HD

    def body(x, low, high, c, s, out):
        product = project(x[:, :half], low[...]) + project(x[:, half:], high[...])
        cos, sin = c[...], s[...]
        lanes = lax.broadcasted_iota(jnp.int32, cos.shape, 1)
        for at in range(0, total, 128):
            part = product[:, at : at + 128]
            if at + 128 > total - kv:
                co, si = jnp.where(lanes < HD, cos, 1.0), jnp.where(lanes < HD, sin, 0.0)
            else:
                co, si = cos, sin
            out[:, at : at + 128] = (part * co + turned(part, lanes) * si).astype(BF16)

    def tiles(columns):
        return pl.BlockSpec((count, columns), lambda i: (i, 0))

    weight = pl.BlockSpec((half, total), lambda i: (0, 0), pipeline_mode=pl.Buffered(1))
    return call(
        body,
        jax.ShapeDtypeStruct((rows, total), BF16),
        (rows_one, weights_low, weights_high, cosine, sine),
        flops=2 * rows * width * total,
        nbytes=2 * (rows * width + width * total),
        grid=(ROW_BLOCKS,),
        in_specs=[tiles(width), weight, weight, tiles(2 * HD), tiles(2 * HD)],
        out_specs=tiles(total),
    )


def window(i, span):
    return max(0, i * span - MAXLEN), (i + 1) * span


def shown(first, i, span):
    low, high = window(i, span)
    keys = low + lax.broadcasted_iota(jnp.int32, (high - low, span), 0)
    rows = i * span + lax.broadcasted_iota(jnp.int32, (high - low, span), 1)
    return (keys <= rows) & (keys >= first[:, i * span : (i + 1) * span])


def dot_nt(left, right):
    return lax.dot_general(left, right, (((1,), (1,)), ((), ())), preferred_element_type=F32)


def dot_tn(left, right):
    return lax.dot_general(left, right, (((0,), (0,)), ((), ())), preferred_element_type=F32)


def attention(qkv, first, pairs):
    rows = qkv.shape[0]
    span = rows // ROW_BLOCKS
    width = 2 * HD

    def body(q, kv, first, out, logs):
        for i in range(ROW_BLOCKS):
            low, high = window(i, span)
            allowed = shown(first, i, span)
            keys, values = kv[low:high, :HD], kv[low:high, HD:]
            results = []
            for h in range(2):
                queries = q[i * span : (i + 1) * span, h * HD : (h + 1) * HD] * 0.125
                scores = jnp.where(allowed, dot_nt(keys, queries.astype(BF16)), MASKED_OUT)
                top = jnp.max(scores, axis=0, keepdims=True)
                shares = jnp.exp(scores - top)
                total = jnp.sum(shares, axis=0, keepdims=True)
                mixed = dot_tn(values, shares.astype(BF16)) / total
                results.append(mixed)
                logs[0, h : h + 1, i * span : (i + 1) * span] = top + jnp.log(total)
            both = jnp.concatenate(results, axis=0)
            out[i * span : (i + 1) * span, :] = both.T.astype(BF16)

    return call(
        body,
        (
            jax.ShapeDtypeStruct((rows, pairs * width), BF16),
            jax.ShapeDtypeStruct((pairs, 2, rows), F32),
        ),
        (qkv, qkv, first),
        flops=4 * rows * 768 * HD * 2 * pairs * 8,
        nbytes=2 * rows * pairs * width * 2,
        grid=(pairs,),
        in_specs=[
            pl.BlockSpec((rows, width), lambda p: (0, p)),
            pl.BlockSpec((rows, width), lambda p: (0, pairs)),
            pl.BlockSpec((1, rows), lambda p: (0, 0)),
        ],
        out_specs=(
            pl.BlockSpec((rows, width), lambda p: (0, p)),
            pl.BlockSpec((1, 2, rows), lambda p: (p, 0, 0)),
        ),
    )


def attention_back(qkv, first, logs, grads, cosine, sine, pairs):
    rows = qkv.shape[0]
    span = rows // ROW_BLOCKS
    width = 2 * HD

    def body(q, kv, first, logs, grad, c, s, dq, dkv, total):
        @pl.when(pl.program_id(0) == 0)
        def _():
            total[...] = jnp.zeros_like(total)

        lanes = lax.broadcasted_iota(jnp.int32, (span, width), 1)
        for i in range(ROW_BLOCKS):
            low, high = window(i, span)
            allowed = shown(first, i, span)
            at = slice(i * span, (i + 1) * span)
            keys, values = kv[low:high, :HD], kv[low:high, HD:]
            results, key_part, value_part = [], 0.0, 0.0
            for h in range(2):
                head = slice(h * HD, (h + 1) * HD)
                queries = (q[i * span : (i + 1) * span, head] * 0.125).astype(BF16)
                came = grad[at, head]
                log = logs[0, h : h + 1, i * span : (i + 1) * span]
                shares = jnp.where(allowed, jnp.exp(dot_nt(keys, queries) - log), 0.0)
                change = dot_nt(values, came)
                inner = jnp.sum(shares * change, axis=0, keepdims=True)
                score_grads = (shares * (change - inner)).astype(BF16)
                value_part += jnp.dot(shares.astype(BF16), came, preferred_element_type=F32)
                key_part += jnp.dot(score_grads, queries, preferred_element_type=F32)
                results.append(dot_tn(keys, score_grads) * 0.125)
            total[low:high, :] += jnp.concatenate([key_part, value_part], axis=1)
            query_grad = jnp.concatenate(results, axis=0).T
            dq[at, :] = (
                query_grad * c[at, :] - turned(query_grad * s[at, :], lanes)
            ).astype(BF16)

        @pl.when(pl.program_id(0) == pairs - 1)
        def _():
            for i in range(ROW_BLOCKS):
                at = slice(i * span, (i + 1) * span)
                cos = jnp.where(lanes < HD, c[at, :], 1.0)
                sin = jnp.where(lanes < HD, s[at, :], 0.0)
                part = total[at, :]
                dkv[at, :] = (
                    part * cos - turned(part * sin, lanes)
                ).astype(BF16)

    return call(
        body,
        (
            jax.ShapeDtypeStruct((rows, pairs * width), BF16),
            jax.ShapeDtypeStruct((rows, width), BF16),
        ),
        (qkv, qkv, first, logs, grads, cosine, sine),
        flops=10 * rows * 768 * HD * 2 * pairs * 8,
        nbytes=2 * rows * pairs * width * 3,
        grid=(pairs,),
        in_specs=[
            pl.BlockSpec((rows, width), lambda p: (0, p)),
            pl.BlockSpec((rows, width), lambda p: (0, pairs)),
            pl.BlockSpec((1, rows), lambda p: (0, 0)),
            pl.BlockSpec((1, 2, rows), lambda p: (p, 0, 0)),
            pl.BlockSpec((rows, width), lambda p: (0, p)),
            pl.BlockSpec((rows, width), lambda p: (0, 0)),
            pl.BlockSpec((rows, width), lambda p: (0, 0)),
        ],
        out_specs=(
            pl.BlockSpec((rows, width), lambda p: (0, p)),
            pl.BlockSpec((rows, width), lambda p: (0, 0)),
        ),
        scratch_shapes=[pltpu.VMEM((rows, width), F32)],
    )


def row_kernel(multiply, left, weights, width, extra, outs, finish, tile=TILE):
    rows = left[0].shape[0]
    tile = min(tile, rows)
    many = len(left), len(left) + len(weights), len(left) + len(weights) + len(extra)

    def body(*refs):
        product = multiply(refs[: many[0]], refs[many[0] : many[1]])
        finish(product, refs[many[1] : many[2]], refs[many[2] :])

    def tiles(columns):
        return pl.BlockSpec((tile, columns), lambda i: (i, 0))

    widths = width if isinstance(width, list) else [width] * len(outs)
    inner = sum(weight.size for weight in weights)
    return pl.pallas_call(
        body,
        out_shape=tuple(
            jax.ShapeDtypeStruct((rows, columns), kind)
            for columns, kind in zip(widths, outs, strict=True)
        ),
        grid=(rows // tile,),
        in_specs=[tiles(v.shape[1]) for v in left]
        + [
            pl.BlockSpec(v.shape, lambda i: (0, 0), pipeline_mode=pl.Buffered(1)) for v in weights
        ]
        + [tiles(v.shape[1]) for v in extra],
        out_specs=tuple(tiles(columns) for columns in widths),
        compiler_params=pltpu.CompilerParams(vmem_limit_bytes=VMEM),
        cost_estimate=pl.CostEstimate(flops=1, bytes_accessed=1, transcendentals=0),
    )(*left, *weights, *extra)


def down_rows(left, weights):
    (x,) = left
    total, at = None, 0
    for w in weights:
        term = jnp.dot(x[:, at : at + w.shape[0]], w[...], preferred_element_type=F32)
        total, at = term if total is None else total + term, at + w.shape[0]
    return total


def gate_part(rows_two, weights):
    def finish(product, extra, outs):
        outs[0][...] = product

    return row_kernel(down_rows, [rows_two], weights, weights[0].shape[1], [], [F32], finish)[0]


def up_part(rows_two, weights, gate_pre, cut):
    width = weights[0].shape[1]
    parts = [slice(0, cut), slice(cut, width)] if cut < width else [slice(0, width)]

    def finish(up, extra, outs):
        gate = extra[0][...]
        sigmoid = 1.0 / (1.0 + jnp.exp(-gate))
        silu = gate * sigmoid
        outs[0][...] = (silu * up).astype(BF16)
        in_gate = (up * sigmoid * (1.0 + gate * (1.0 - sigmoid))).astype(BF16)
        in_up = silu.astype(BF16)
        for i, columns in enumerate(parts):
            outs[1 + 2 * i][...] = in_gate[:, columns]
            outs[2 + 2 * i][...] = in_up[:, columns]

    widths = [width] + [part.stop - part.start for part in parts for _ in range(2)]
    hidden, *factors = row_kernel(
        down_rows, [rows_two], weights, widths, [gate_pre], [BF16] * len(widths), finish, 256
    )
    return hidden, factors


def hidden_back(grad_rows, weights, halves, factors):
    width = weights[0].shape[0]

    def multiply(left, weights):
        (x,) = left
        step = weights[0].shape[1] if halves else weights[0].shape[1] // 4
        total = None
        for a, w in enumerate(weights):
            blocks = [(2 * a, 0), (4 + 2 * a, 1), (2 * a + 1, 2), (5 + 2 * a, 3)]
            places = [(a, 0)] if halves else blocks
            for place, at in places:
                term = dot_nt(
                    x[:, place * step : (place + 1) * step], w[:, at * step : (at + 1) * step]
                )
                total = term if total is None else total + term
        return total

    def finish(product, extra, outs):
        for factor, out in zip(extra, outs, strict=True):
            out[...] = (product * factor[...].astype(F32)).astype(BF16)

    return row_kernel(multiply, [grad_rows], weights, width, factors, [BF16] * 2, finish)


def feed_back(grad_gates, grad_ups, w_gates, w_ups):
    count, pieces = len(grad_gates), len(w_gates)

    def multiply(left, weights):
        products = []
        for w_gate, w_up in zip(weights[:pieces], weights[pieces:], strict=True):
            total, at = None, 0
            for gate, up in zip(left[:count], left[count:], strict=True):
                columns = slice(at, at + gate.shape[1])
                term = dot_nt(gate[...], w_gate[:, columns]) + dot_nt(up[...], w_up[:, columns])
                total, at = term if total is None else total + term, columns.stop
            products.append(total)
        return products

    def finish(products, extra, outs):
        at = 0
        for product in products:
            outs[0][:, at : at + product.shape[1]] = product.astype(BF16)
            at += product.shape[1]

    return row_kernel(
        multiply,
        [*grad_gates, *grad_ups],
        [*w_gates, *w_ups],
        sum(w.shape[0] for w in w_gates),
        [],
        [BF16],
        finish,
        256,
    )[0]


def held_rows(order, gathered):
    rows, width = gathered.shape
    count = rows // ROW_BLOCKS

    def body(order, x, out):
        for held, true in spans(order, width):
            out[:, held] = x[:, true]

    spec = pl.BlockSpec((count, width), lambda i: (i, 0))
    return call(
        body,
        jax.ShapeDtypeStruct((rows, width), BF16),
        (order, gathered),
        nbytes=4 * rows * width,
        grid=(ROW_BLOCKS,),
        in_specs=[SCALARS, spec],
        out_specs=spec,
    )


def middle(order, layer_in, came):
    count, width = layer_in.shape

    def body(order, x, came, mid, unit, inverse):
        for held, true in spans(order, width):
            mid[:, held] = x[:, true].astype(F32) + came[:, held].astype(F32)
        values = mid[...]
        scale = lax.rsqrt(jnp.mean(values * values, axis=-1, keepdims=True) + EPSILON)
        inverse[...] = scale
        unit[...] = (values * scale).astype(BF16)

    return call(
        body,
        (
            jax.ShapeDtypeStruct((count, width), F32),
            jax.ShapeDtypeStruct((count, width), BF16),
            jax.ShapeDtypeStruct((count, 1), F32),
        ),
        (order, layer_in, came),
        nbytes=20 * count * width,
        in_specs=[SCALARS] + whole(2),
        out_specs=tuple(whole(3)),
    )


def layer_end(order, mid, came):
    count, width = mid.shape

    def body(order, mid, came, out):
        for held, true in spans(order, width):
            total = mid[:, held] + came[:, held].astype(F32)
            out[:, true] = total.astype(BF16)

    return call(
        body,
        jax.ShapeDtypeStruct((count, width), BF16),
        (order, mid, came),
        nbytes=14 * count * width,
        in_specs=[SCALARS] + whole(2),
        out_specs=whole(1)[0],
    )


def middle_back(order, out_grad, mid, inverse, came):
    count, width = mid.shape

    def body(order, dy, mid, inverse, came, grad, low):
        scale = inverse[...]
        grad_unit = came[...].astype(F32)
        unit = mid[...] * scale
        inner = jnp.mean(grad_unit * unit, axis=-1, keepdims=True)
        grad[...] = scale * (grad_unit - unit * inner)
        for held, true in spans(order, width):
            total = grad[:, held] + dy[:, true].astype(F32)
            grad[:, held] = total
            low[:, held] = total.astype(BF16)

    return call(
        body,
        (
            jax.ShapeDtypeStruct((count, width), F32),
            jax.ShapeDtypeStruct((count, width), BF16),
        ),
        (order, out_grad, mid, inverse, came),
        nbytes=20 * count * width,
        in_specs=[SCALARS] + whole(4),
        out_specs=tuple(whole(2)),
    )


def input_back(order, layer_in, grad_mid, came):
    count, width = grad_mid.shape

    def body(order, x, grad_mid, came, out, unit):
        values = x[...].astype(F32)
        scale = lax.rsqrt(jnp.mean(values * values, axis=-1, keepdims=True) + EPSILON)
        for held, true in spans(order, width):
            unit[:, held] = x[:, true].astype(F32) * scale
        grad_unit = came[...].astype(F32)
        inner = jnp.mean(grad_unit * unit[...], axis=-1, keepdims=True)
        unit[...] = grad_mid[...] + scale * (grad_unit - unit[...] * inner)
        for held, true in spans(order, width):
            out[:, true] = unit[:, held]

    return call(
        body,
        jax.ShapeDtypeStruct((count, width), F32),
        (order, layer_in, grad_mid, came),
        nbytes=16 * count * width,
        in_specs=[SCALARS] + whole(3),
        out_specs=whole(1)[0],
        scratch_shapes=[pltpu.VMEM((count, width), F32)],
    )


def gather_rows(rows):
    return lax.all_gather(rows, "tp", axis=0, tiled=True)


def sum_rows(partial):
    return lax.psum_scatter(partial, "tp", scatter_dimension=0, tiled=True)


class Taker:
    def __init__(self, held):
        self.held = held

    def __getattr__(self, name):
        return self.held.pop(name)


class Held(dict):
    __getattr__ = dict.__getitem__

    @property
    def out(self):
        return Taker(self)


def fence(state):
    if isinstance(state, Held):
        return Held(lax.optimization_barrier(dict(state)))
    return lax.optimization_barrier(state)


def zed(values, step):
    return lax.ppermute(values, "fsdp", [(i, i ^ (2 * step)) for i in range(8)])


def why(values):
    return lax.ppermute(values, "fsdp", [(i, i ^ 1) for i in range(8)])


def teep(values, mask):
    return lax.ppermute(values, "tp", [(i, i ^ mask) for i in range(4)])


def own_gains(gains):
    t = lax.axis_index("tp")
    own = jnp.stack(gains)
    near = jnp.stack([own, teep(own, 1)], axis=1)
    near = jnp.where((t & 1) == 1, near[:, ::-1], near)
    both = jnp.stack([near, teep(near, 2)], axis=1)
    both = jnp.where((t >> 1) == 1, both[:, ::-1], both)
    return both.reshape(len(gains), -1)


def share_gains(terms):
    t = lax.axis_index("tp")
    both = jnp.stack(terms).reshape(len(terms), 2, 2, -1)
    both = jnp.where((t >> 1) == 1, both[:, ::-1], both)
    both = both[:, 0] + teep(both[:, 1], 2)
    both = jnp.where((t & 1) == 1, both[:, ::-1], both)
    both = both[:, 0] + teep(both[:, 1], 1)
    return [both[i] for i in range(len(terms))]


def part(left, right, axis, first, last):
    step = (left if axis == 0 else right).shape[1] // COLUMN_BLOCKS
    at = slice(first * step, last * step)
    if axis == 0:
        return outer(left[:, at], right)
    return outer(left, right[:, at])


def joined(values, axis, first, last, *came):
    step = values.shape[axis] // 4
    total = lax.slice_in_dim(values, first * step, last * step, axis=axis).astype(F32)
    for array, at, count in came:
        size = array.shape[axis] // count
        piece = lax.slice_in_dim(array, at * size, (at + last - first) * size, axis=axis)
        total = total + piece.astype(F32)
    return total


def summed(total, came):
    for values in came:
        total = total + values.astype(F32)
    return total


def scheduled(
    layer_in,
    seq_lengths,
    attn_gain,
    w_query,
    w_key,
    w_value,
    w_output,
    mlp_gain,
    w_gate,
    w_up,
    w_down,
    out_grad,
):
    group_rows = layer_in.shape[0] * lax.axis_size("tp")
    query_width, key_width = w_query.shape[1], w_key.shape[1]
    pairs = query_width // (2 * HD)
    masks = [2 * a + b for b in (0, 1) for a in (0, 2, 1, 3)]
    order = lax.axis_index("fsdp") ^ jnp.array(masks, jnp.int32)
    cut = w_down.shape[0] // 256 * 128 + 128

    input_rows = gather_rows(layer_in)
    down_high = w_down[cut:]
    v = Held(
        o=jnp.concatenate([w_output] + [zed(w_output, a) for a in (2, 1, 3)], axis=1),
        down_high=[down_high, why(down_high)],
        down_low=w_down[:cut],
        gains=own_gains([attn_gain, mlp_gain])[:, :, None],
        order=order,
        layer_in=layer_in,
        out_grad=out_grad,
        w_qkv=jnp.concatenate([w_query, w_key, w_value], axis=1),
        w_gate=w_gate,
        w_up=w_up,
    )
    first_at, where_at = positions(seq_lengths, group_rows)
    v.update(first_at=first_at, tables=rope_tables(where_at[0], HD))
    v = fence(v)

    q = (v.w_qkv.astype(F32) * v.gains[0]).astype(BF16)
    q = jnp.concatenate([q] + [zed(q, a) for a in (2, 1, 3)], axis=0)
    oy = why(v.o)
    g = (v.w_gate.astype(F32) * v.gains[1]).astype(BF16)
    u = (v.w_up.astype(F32) * v.gains[1]).astype(BF16)
    dq = jnp.concatenate(v.out.down_high, axis=1)
    v.update(q=q, oy=oy, g=g, u=u, dq=dq)
    v = fence(v)

    g = [v.g, zed(v.g, 2)]
    qy = why(v.q)
    w_output_all = jnp.concatenate([v.out.o, v.out.oy], axis=1)
    rows_one = unit_rows(v.order, input_rows)
    v.update(g=g, qy=qy, w_output_all=w_output_all, rows_one=rows_one)
    v = fence(v)

    grad_gathered = gather_rows(v.out_grad)
    g = jnp.concatenate(v.g, axis=0)
    g = [g, zed(g, 1), why(g)]
    qkv = project_rotate(v.rows_one, v.q, v.qy, *v.tables)
    attended, logs = attention(qkv, v.first_at, pairs)
    partial = project(attended, v.w_output_all).astype(BF16)
    v.update(g=g, qkv=qkv, attended=attended, logs=logs, partial=partial)
    v = fence(v)

    came = sum_rows(v.out.partial)
    u = [v.u, zed(v.u, 2)]
    g = v.g + [why(v.g[1])]
    grad_rows = held_rows(v.order, grad_gathered)
    v.update(u=u, g=g, grad_rows=grad_rows)
    v = fence(v)

    u = jnp.concatenate(v.u, axis=0)
    u = [u, zed(u, 1), why(u)]
    mid, unit_two, inverse_two = middle(v.order, v.layer_in, came)
    v.update(u=u, mid=mid, unit_two=unit_two, inverse_two=inverse_two)
    v = fence(v)

    rows_two = gather_rows(v.out.unit_two)
    low = v.out.down_low
    low = jnp.concatenate([low] + [zed(low, a) for a in (2, 1, 3)], axis=1)
    u = v.u + [why(v.u[1])]
    v.update(low=low, u=u)
    v = fence(v)

    dq = [v.dq, zed(v.dq, 2)]
    low_across = why(v.low)
    gate_pre = gate_part(rows_two, v.g)
    hidden, factors = up_part(rows_two, v.u, gate_pre, cut)
    down_away = part(hidden, v.grad_rows, 1, 6, 8).astype(BF16)
    v.update(dq=dq, low_across=low_across, rows_two=rows_two, hidden=hidden)
    v.update(factors=factors, down_away=down_away)
    v = fence(v)

    dq = jnp.concatenate(v.dq, axis=1)
    dq = [dq, zed(dq, 1)]
    first = why(v.down_away)
    down_away = part(v.hidden, v.grad_rows, 1, 4, 6).astype(BF16)
    down_kept = part(v.hidden, v.grad_rows, 1, 0, 4).astype(BF16)
    gate_low, up_low = hidden_back(v.grad_rows, [v.low, v.low_across], True, v.factors[:2])
    v.update(dq=dq, first=first, down_away=down_away, down_kept=down_kept)
    v.update(gate_low=gate_low, up_low=up_low)
    v = fence(v)

    near = zed(joined(v.down_kept, 1, 2, 4, (v.first, 0, 2)).astype(BF16), 1)
    second = why(v.down_away)
    gate_high, up_high = hidden_back(v.grad_rows, v.dq, False, v.out.factors[2:])
    gates, ups = [v.out.gate_low, gate_high], [v.out.up_low, up_high]
    partial = feed_back(gates, ups, v.g, v.u)
    gate_away = jnp.concatenate(
        [part(v.rows_two, gate, 0, 6, 8).astype(BF16) for gate in gates], axis=1
    )
    v.update(near=near, second=second, gates=gates, ups=ups, gate_away=gate_away)
    v.update(partial=partial)
    v = fence(v)

    came = sum_rows(v.out.partial)
    far = zed(joined(v.down_kept, 1, 1, 2, (v.second, 1, 2), (v.near, 1, 2)).astype(BF16), 2)
    first = why(v.gate_away)
    grad_gate = jnp.concatenate(v.out.gates, axis=1)
    grad_up = jnp.concatenate(v.out.ups, axis=1)
    gate_away = part(v.rows_two, grad_gate, 0, 4, 6).astype(BF16)
    gate_kept = part(v.rows_two, grad_gate, 0, 0, 4).astype(BF16)
    up_away = [part(v.rows_two, grad_up, 0, 6, 8).astype(BF16)]
    v.update(far=far, first=first)
    v.update(gate_away=gate_away, gate_kept=gate_kept, up_away=up_away, grad_up=grad_up)
    v = fence(v)

    grad_down_sh = joined(v.down_kept, 1, 0, 1, (v.second, 0, 2), (v.near, 0, 2), (v.far, 0, 1))
    near = zed(joined(v.gate_kept, 0, 2, 4, (v.first, 0, 2)).astype(BF16), 1)
    second = why(v.gate_away)
    grad_mid, grad_mid_low = middle_back(v.order, v.out_grad, v.mid, v.inverse_two, came)
    up_away = v.up_away + [part(v.rows_two, v.grad_up, 0, 4, 6).astype(BF16)]
    up_kept = part(v.rows_two, v.grad_up, 0, 0, 4).astype(BF16)
    v.update(grad_down_sh=grad_down_sh, near=near, second=second, grad_mid=grad_mid)
    v.update(grad_mid_low=grad_mid_low)
    v.update(up_away=up_away, up_kept=up_kept)
    v = fence(v)

    grad_mid_rows = gather_rows(v.out.grad_mid_low)
    far = zed(joined(v.gate_kept, 0, 1, 2, (v.second, 1, 2), (v.near, 1, 2)).astype(BF16), 2)
    first = why(v.up_away[0])
    high = v.out.dq
    step = high[0].shape[1] // 4
    columns = [w[:, i * step : (i + 1) * step] for w in high for i in range(4)]
    high_all = jnp.concatenate(columns[0::2] + columns[1::2], axis=1)
    low_all = jnp.concatenate([v.out.low, v.out.low_across], axis=1)
    partial = project(v.hidden[:, :cut], low_all)
    output_part = (partial + project(v.hidden[:, cut:], high_all)).astype(BF16)
    v.update(far=far, first=first, output_part=output_part)
    v = fence(v)

    near = zed(joined(v.up_kept, 0, 2, 4, (v.first, 0, 2)).astype(BF16), 1)
    second = why(v.up_away[1])
    grad_attended = project_back(grad_mid_rows, v.w_output_all).astype(BF16)
    grad_query, grad_kv = attention_back(
        v.qkv, v.first_at, v.logs, grad_attended, *v.tables, pairs
    )
    grad_qkv = jnp.concatenate([grad_query, grad_kv], axis=1)
    came_out = sum_rows(v.output_part)
    v.update(gate_terms=[v.second, v.near, v.far], near=near, second=second)
    v.update(grad_qkv=grad_qkv, grad_mid_rows=grad_mid_rows)
    v = fence(v)

    far = zed(joined(v.up_kept, 0, 1, 2, (v.second, 1, 2), (v.near, 1, 2)).astype(BF16), 2)
    first = why(part(v.rows_one, v.grad_qkv, 0, 4, 8).astype(BF16))
    w_qkv_all = jnp.concatenate([v.q, v.qy], axis=0)
    partial = project_back(v.grad_qkv, w_qkv_all).astype(BF16)
    qkv_kept = part(v.rows_one, v.grad_qkv, 0, 0, 4).astype(BF16)
    output_away = part(v.attended, v.grad_mid_rows, 1, 4, 8).astype(BF16)
    places = [(0, 2), (0, 2), (0, 1)]
    terms = [(term, *place) for term, place in zip(v.out.gate_terms, places, strict=True)]
    grad_gate_sh = joined(v.gate_kept, 0, 0, 1, *terms)
    v.update(far=far, first=first, qkv_kept=qkv_kept, output_away=output_away)
    v.update(partial=partial, grad_gate_sh=grad_gate_sh)
    v = fence(v)

    came = sum_rows(v.out.partial)
    pieces = [
        zed(joined(v.qkv_kept, 0, i, i + 1, (v.first, i, 4)).astype(BF16), a)
        for i, a in ((1, 2), (2, 1), (3, 3))
    ]
    over = why(v.output_away)
    gain_one, gain_two = v.gains[0], v.gains[1]
    grad_gate_sh = v.grad_gate_sh
    grad_up_sh = joined(v.up_kept, 0, 0, 1, (v.second, 0, 2), (v.near, 0, 2), (v.far, 0, 1))
    gain_two_term = jnp.sum(
        grad_gate_sh * v.w_gate.astype(F32) + grad_up_sh * v.w_up.astype(F32), axis=1
    )
    output_kept = part(v.attended, v.grad_mid_rows, 1, 0, 4).astype(BF16)
    layer_out = layer_end(v.order, v.mid, came_out)
    v.update(pieces=pieces, over=over, gain_two_term=gain_two_term)
    v.update(grad_gate_sh=grad_gate_sh * gain_two, grad_up_sh=grad_up_sh * gain_two)
    v.update(output_kept=output_kept, layer_out=layer_out)
    v = fence(v)

    pieces = [
        zed(joined(v.output_kept, 1, i, i + 1, (v.over, i, 4)).astype(BF16), a)
        for i, a in ((1, 2), (2, 1), (3, 3))
    ]
    grad_qkv_sh = summed(joined(v.qkv_kept, 0, 0, 1, (v.first, 0, 4)), v.pieces)
    gain_one_term = jnp.sum(grad_qkv_sh * v.w_qkv.astype(F32), axis=1)
    gain_one_grad, gain_two_grad = share_gains([gain_one_term, v.gain_two_term])
    grad_qkv_sh = grad_qkv_sh * v.gains[0]
    in_grad = input_back(v.order, v.layer_in, v.grad_mid, came)
    in_grad, over = fence((in_grad, v.over))
    return (
        v.layer_out,
        in_grad,
        gain_one_grad,
        grad_qkv_sh[:, :query_width],
        grad_qkv_sh[:, query_width : query_width + key_width],
        grad_qkv_sh[:, query_width + key_width :],
        summed(joined(v.output_kept, 1, 0, 1, (over, 0, 4)), pieces),
        gain_two_grad,
        v.grad_gate_sh,
        v.grad_up_sh,
        v.grad_down_sh,
    )


def direct(
    layer_in,
    seq_lengths,
    attn_gain,
    w_query,
    w_key,
    w_value,
    w_output,
    mlp_gain,
    w_gate,
    w_up,
    w_down,
    out_grad,
):
    def gather(shard, axis):
        return lax.all_gather(shard, "fsdp", axis=axis, tiled=True)

    def scatter(left, right, axis):
        total = outer(left, right).astype(BF16)
        return lax.psum_scatter(total, "fsdp", scatter_dimension=axis, tiled=True).astype(F32)

    group_rows = layer_in.shape[0] * lax.axis_size("tp")
    query_width, key_width = w_query.shape[1], w_key.shape[1]
    pairs = query_width // (2 * HD)
    order = jnp.arange(COLUMN_BLOCKS, dtype=jnp.int32)
    gain_one, gain_two = [
        lax.all_gather(gain, "tp", axis=0, tiled=True)[:, None] for gain in (attn_gain, mlp_gain)
    ]
    w_qkv = jnp.concatenate([w_query, w_key, w_value], axis=1)
    w_output_all = gather(w_output, 1)
    w_qkv_all = gather((w_qkv.astype(F32) * gain_one).astype(BF16), 0)
    w_gate_all = gather((w_gate.astype(F32) * gain_two).astype(BF16), 0)
    w_up_all = gather((w_up.astype(F32) * gain_two).astype(BF16), 0)
    w_down_all = gather(w_down, 1)
    first_at, where_at = positions(seq_lengths, group_rows)
    cosine, sine = rope_tables(where_at[0], HD)
    rows_one = unit_rows(order, gather_rows(layer_in))
    qkv = project_rotate(rows_one, *jnp.split(w_qkv_all, 2), cosine, sine)
    grad_rows = held_rows(order, gather_rows(out_grad))
    attended, logs = attention(qkv, first_at, pairs)
    came = sum_rows(project(attended, w_output_all).astype(BF16))
    mid, unit_two, inverse_two = middle(order, layer_in, came)
    rows_two = gather_rows(unit_two)
    gate_pre = gate_part(rows_two, [w_gate_all])
    hidden, factors = up_part(rows_two, [w_up_all], gate_pre, w_up.shape[1])
    grad_down_sh = scatter(hidden, grad_rows, 1)
    came = sum_rows(project(hidden, w_down_all).astype(BF16))
    layer_out = layer_end(order, mid, came)
    grad_gate, grad_up = hidden_back(
        grad_rows, jnp.split(w_down_all, 2, axis=1), True, factors
    )
    came = sum_rows(feed_back([grad_gate], [grad_up], [w_gate_all], [w_up_all]))
    grad_gate_sh = scatter(rows_two, grad_gate, 0)
    grad_up_sh = scatter(rows_two, grad_up, 0)
    grad_mid, grad_mid_low = middle_back(order, out_grad, mid, inverse_two, came)
    grad_mid_rows = gather_rows(grad_mid_low)
    grad_attended = project_back(grad_mid_rows, w_output_all).astype(BF16)
    grad_output_sh = scatter(attended, grad_mid_rows, 1)
    grad_query, grad_kv = attention_back(
        qkv, first_at, logs, grad_attended, cosine, sine, pairs
    )
    grad_qkv = jnp.concatenate([grad_query, grad_kv], axis=1)
    came = sum_rows(project_back(grad_qkv, w_qkv_all).astype(BF16))
    in_grad = input_back(order, layer_in, grad_mid, came)
    grad_qkv_sh = scatter(rows_one, grad_qkv, 0)
    gain_one_term = jnp.sum(grad_qkv_sh * w_qkv.astype(F32), axis=1)
    gain_two_term = jnp.sum(
        grad_gate_sh * w_gate.astype(F32) + grad_up_sh * w_up.astype(F32), axis=1
    )
    gain_one_grad, gain_two_grad = [
        lax.psum_scatter(term, "tp", scatter_dimension=0, tiled=True)
        for term in (gain_one_term, gain_two_term)
    ]
    grad_qkv_sh = grad_qkv_sh * gain_one
    return (
        layer_out,
        in_grad,
        gain_one_grad,
        grad_qkv_sh[:, :query_width],
        grad_qkv_sh[:, query_width : query_width + key_width],
        grad_qkv_sh[:, query_width + key_width :],
        grad_output_sh,
        gain_two_grad,
        grad_gate_sh * gain_two,
        grad_up_sh * gain_two,
        grad_down_sh,
    )


def solution(mesh):
    placed = (
        P(("fsdp", "tp"), None),
        P("fsdp", None),
        P(("fsdp", "tp")),
        P("fsdp", "tp"),
        P("fsdp", "tp"),
        P("fsdp", "tp"),
        P("tp", "fsdp"),
        P(("fsdp", "tp")),
        P("fsdp", "tp"),
        P("fsdp", "tp"),
        P("tp", "fsdp"),
        P(("fsdp", "tp"), None),
    )
    paired = (mesh.shape["fsdp"], mesh.shape["tp"]) == (8, 4)
    return jax.shard_map(
        scheduled if paired else direct,
        mesh=mesh,
        in_specs=placed,
        out_specs=(
            P(("fsdp", "tp"), None),
            P(("fsdp", "tp"), None),
            P(("fsdp", "tp")),
            P("fsdp", "tp"),
            P("fsdp", "tp"),
            P("fsdp", "tp"),
            P("tp", "fsdp"),
            P(("fsdp", "tp")),
            P("fsdp", "tp"),
            P("fsdp", "tp"),
            P("tp", "fsdp"),
        ),
        check_vma=False,
    )
```

```python
import math

import jax
import jax.numpy as jnp
from jax import lax
from jax.experimental import pallas as pl
from jax.experimental.pallas import tpu as pltpu
from jax.sharding import PartitionSpec as P

HD = 64
MAXLEN = 512
EPSILON = 1e-05
ROPE_BASE = 10000.0
MASKED_OUT = -1e30
TILE = 512
COLUMN_BLOCKS = 8
ROW_BLOCKS = 4
VMEM = 56 * 1024 * 1024
F32 = jnp.float32
BF16 = jnp.bfloat16


def positions(lengths, count):
    starts = jnp.cumsum(lengths, axis=-1) - lengths
    indices = jnp.arange(count, dtype=jnp.int32)
    inside = (indices[None, :, None] >= starts[:, None, :]) & (
        indices[None, :, None] < (starts + lengths)[:, None, :]
    )
    first_at = jnp.sum(jnp.where(inside, starts[:, None, :], 0), axis=-1)
    return first_at, indices[None, :] - first_at


def rope_tables(where_at, width):
    half_width = width // 2
    inverse_freq = ROPE_BASE ** (-(jnp.arange(half_width, dtype=F32) * 2.0 / width))
    angles = where_at.astype(F32)[:, None] * inverse_freq[None, :]
    cosine, sine = jnp.cos(angles), jnp.sin(angles)
    return jnp.concatenate([cosine] * 4, axis=1), jnp.concatenate([sine] * 4, axis=1)


def project(left, weight):
    return jnp.dot(left, weight, preferred_element_type=F32)


def project_back(grad, weight):
    return jnp.einsum("tc,dc->td", grad, weight, preferred_element_type=F32)


def outer(left, right):
    return jnp.einsum("ta,tb->ab", left, right, preferred_element_type=F32)


def call(body, outs, operands, flops=0, nbytes=0, **more):
    return pl.pallas_call(
        body,
        out_shape=outs,
        compiler_params=pltpu.CompilerParams(vmem_limit_bytes=VMEM),
        cost_estimate=pl.CostEstimate(flops=1, bytes_accessed=1, transcendentals=0),
        **more,
    )(*operands)


def whole(count):
    return [pl.BlockSpec(memory_space=pltpu.VMEM)] * count


SCALARS = pl.BlockSpec(memory_space=pltpu.SMEM)


def spans(order, width):
    step = width // COLUMN_BLOCKS
    return [
        (slice(j * step, (j + 1) * step), pl.ds(pl.multiple_of(order[j] * step, step), step))
        for j in range(COLUMN_BLOCKS)
    ]


def turned(values, lanes):
    width = values.shape[-1]
    first = (lanes % HD) < HD // 2
    return jnp.where(
        first, -pltpu.roll(values, width - HD // 2, 1), pltpu.roll(values, HD // 2, 1)
    )


def unit_rows(order, gathered):
    rows, width = gathered.shape
    count = rows // ROW_BLOCKS

    def body(order, x, out):
        values = x[...].astype(F32)
        inverse = lax.rsqrt(jnp.mean(values * values, axis=-1, keepdims=True) + EPSILON)
        for held, true in spans(order, width):
            out[:, held] = (x[:, true].astype(F32) * inverse).astype(BF16)

    spec = pl.BlockSpec((count, width), lambda i: (i, 0))
    return call(
        body,
        jax.ShapeDtypeStruct((rows, width), BF16),
        (order, gathered),
        nbytes=4 * rows * width,
        grid=(ROW_BLOCKS,),
        in_specs=[SCALARS, spec],
        out_specs=spec,
    )


def project_rotate(rows_one, weights_low, weights_high, cosine, sine):
    rows, width = rows_one.shape
    count = rows // ROW_BLOCKS
    half, total = weights_low.shape
    kv = 2 * HD

    def body(x, low, high, c, s, out):
        product = project(x[:, :half], low[...]) + project(x[:, half:], high[...])
        cos, sin = c[...], s[...]
        lanes = lax.broadcasted_iota(jnp.int32, cos.shape, 1)
        for at in range(0, total, 128):
            part = product[:, at : at + 128]
            if at + 128 > total - kv:
                co, si = jnp.where(lanes < HD, cos, 1.0), jnp.where(lanes < HD, sin, 0.0)
            else:
                co, si = cos, sin
            out[:, at : at + 128] = (part * co + turned(part, lanes) * si).astype(BF16)

    def tiles(columns):
        return pl.BlockSpec((count, columns), lambda i: (i, 0))

    weight = pl.BlockSpec((half, total), lambda i: (0, 0), pipeline_mode=pl.Buffered(1))
    return call(
        body,
        jax.ShapeDtypeStruct((rows, total), BF16),
        (rows_one, weights_low, weights_high, cosine, sine),
        flops=2 * rows * width * total,
        nbytes=2 * (rows * width + width * total),
        grid=(ROW_BLOCKS,),
        in_specs=[tiles(width), weight, weight, tiles(2 * HD), tiles(2 * HD)],
        out_specs=tiles(total),
    )


def window(i, span):
    return max(0, i * span - MAXLEN), (i + 1) * span


def shown(first, i, span):
    low, high = window(i, span)
    keys = low + lax.broadcasted_iota(jnp.int32, (high - low, span), 0)
    rows = i * span + lax.broadcasted_iota(jnp.int32, (high - low, span), 1)
    return (keys <= rows) & (keys >= first[:, i * span : (i + 1) * span])


def dot_nt(left, right):
    return lax.dot_general(left, right, (((1,), (1,)), ((), ())), preferred_element_type=F32)


def dot_tn(left, right):
    return lax.dot_general(left, right, (((0,), (0,)), ((), ())), preferred_element_type=F32)


def stacked(values, heads):
    return jnp.concatenate([values[:, h * HD : (h + 1) * HD] for h in range(heads)], axis=0)


def side_by_side(values, span, heads):
    parts = [values[:, h * span : (h + 1) * span] for h in range(heads)]
    return [jnp.concatenate(parts[h : h + 2], axis=0).T for h in range(0, heads, 2)]


def attention(qkv, first, pairs):
    rows = qkv.shape[0]
    span = rows // ROW_BLOCKS
    heads = min(4, 2 * pairs)
    width = heads * HD

    def body(q, kv, first, out, logs):
        for i in range(rows // span):
            low, high = window(i, span)
            at = slice(i * span, (i + 1) * span)
            allowed = jnp.concatenate([shown(first, i, span)] * heads, axis=1)
            keys, values = kv[low:high, :HD], kv[low:high, HD:]
            queries = stacked((q[at, :] * 0.125).astype(BF16), heads)
            scores = jnp.where(allowed, dot_nt(keys, queries), MASKED_OUT)
            top = jnp.max(scores, axis=0, keepdims=True)
            shares = jnp.exp(scores - top)
            total = jnp.sum(shares, axis=0, keepdims=True)
            mixed = dot_tn(values, shares.astype(BF16)) / total
            log = top + jnp.log(total)
            for h in range(heads):
                logs[h // 2, h % 2 : h % 2 + 1, at] = log[:, h * span : (h + 1) * span]
            for p, pair in enumerate(side_by_side(mixed, span, heads)):
                out[at, p * 2 * HD : (p + 1) * 2 * HD] = pair.astype(BF16)

    return call(
        body,
        (
            jax.ShapeDtypeStruct((rows, pairs * 2 * HD), BF16),
            jax.ShapeDtypeStruct((pairs, 2, rows), F32),
        ),
        (qkv, qkv, first),
        grid=(2 * pairs // heads,),
        in_specs=[
            pl.BlockSpec((rows, width), lambda p: (0, p)),
            pl.BlockSpec((rows, 2 * HD), lambda p: (0, pairs)),
            pl.BlockSpec((1, rows), lambda p: (0, 0)),
        ],
        out_specs=(
            pl.BlockSpec((rows, width), lambda p: (0, p)),
            pl.BlockSpec((heads // 2, 2, rows), lambda p: (p, 0, 0)),
        ),
    )


def attention_back(qkv, first, logs, grads, cosine, sine, pairs):
    rows = qkv.shape[0]
    span = rows // (2 * ROW_BLOCKS)
    heads = min(4, 2 * pairs)
    width = heads * HD

    def body(q, kv, first, logs, grad, c, s, dq, dkv, total):
        @pl.when(pl.program_id(0) == 0)
        def _():
            total[...] = jnp.zeros_like(total)

        lanes = lax.broadcasted_iota(jnp.int32, (span, 2 * HD), 1)
        for i in range(rows // span):
            low, high = window(i, span)
            at = slice(i * span, (i + 1) * span)
            allowed = jnp.concatenate([shown(first, i, span)] * heads, axis=1)
            keys, values = kv[low:high, :HD], kv[low:high, HD:]
            queries = stacked((q[at, :] * 0.125).astype(BF16), heads)
            came = stacked(grad[at, :], heads)
            log = jnp.concatenate([logs[h // 2, h % 2 : h % 2 + 1, at] for h in range(heads)], axis=1)
            shares = jnp.where(allowed, jnp.exp(dot_nt(keys, queries) - log), 0.0)
            change = dot_nt(values, came)
            inner = jnp.sum(shares * change, axis=0, keepdims=True)
            score_grads = (shares * (change - inner)).astype(BF16)
            value_part = jnp.dot(shares.astype(BF16), came, preferred_element_type=F32)
            key_part = jnp.dot(score_grads, queries, preferred_element_type=F32)
            total[low:high, :] += jnp.concatenate([key_part, value_part], axis=1)
            query_grads = dot_tn(keys, score_grads) * 0.125
            for p, pair in enumerate(side_by_side(query_grads, span, heads)):
                dq[at, p * 2 * HD : (p + 1) * 2 * HD] = (
                    pair * c[at, :] - turned(pair * s[at, :], lanes)
                ).astype(BF16)

        @pl.when(pl.program_id(0) == 2 * pairs // heads - 1)
        def _():
            for i in range(rows // span):
                at = slice(i * span, (i + 1) * span)
                cos = jnp.where(lanes < HD, c[at, :], 1.0)
                sin = jnp.where(lanes < HD, s[at, :], 0.0)
                part = total[at, :]
                dkv[at, :] = (part * cos - turned(part * sin, lanes)).astype(BF16)

    return call(
        body,
        (
            jax.ShapeDtypeStruct((rows, pairs * 2 * HD), BF16),
            jax.ShapeDtypeStruct((rows, 2 * HD), BF16),
        ),
        (qkv, qkv, first, logs, grads, cosine, sine),
        grid=(2 * pairs // heads,),
        in_specs=[
            pl.BlockSpec((rows, width), lambda p: (0, p)),
            pl.BlockSpec((rows, 2 * HD), lambda p: (0, pairs)),
            pl.BlockSpec((1, rows), lambda p: (0, 0)),
            pl.BlockSpec((heads // 2, 2, rows), lambda p: (p, 0, 0)),
            pl.BlockSpec((rows, width), lambda p: (0, p)),
            pl.BlockSpec((rows, 2 * HD), lambda p: (0, 0)),
            pl.BlockSpec((rows, 2 * HD), lambda p: (0, 0)),
        ],
        out_specs=(
            pl.BlockSpec((rows, width), lambda p: (0, p)),
            pl.BlockSpec((rows, 2 * HD), lambda p: (0, 0)),
        ),
        scratch_shapes=[pltpu.VMEM((rows, 2 * HD), F32)],
    )


def row_kernel(multiply, left, weights, width, extra, outs, finish, tile=TILE):
    rows = left[0].shape[0]
    tile = min(tile, rows)
    many = len(left), len(left) + len(weights), len(left) + len(weights) + len(extra)

    def body(*refs):
        product = multiply(refs[: many[0]], refs[many[0] : many[1]])
        finish(product, refs[many[1] : many[2]], refs[many[2] :])

    def tiles(columns):
        return pl.BlockSpec((tile, columns), lambda i: (i, 0))

    widths = [width] * len(outs)
    inner = sum(weight.size for weight in weights)
    return pl.pallas_call(
        body,
        out_shape=tuple(
            jax.ShapeDtypeStruct((rows, columns), kind)
            for columns, kind in zip(widths, outs, strict=True)
        ),
        grid=(rows // tile,),
        in_specs=[tiles(v.shape[1]) for v in left]
        + [
            pl.BlockSpec(v.shape, lambda i: (0, 0), pipeline_mode=pl.Buffered(1)) for v in weights
        ]
        + [tiles(v.shape[1]) for v in extra],
        out_specs=tuple(tiles(columns) for columns in widths),
        compiler_params=pltpu.CompilerParams(vmem_limit_bytes=VMEM),
        cost_estimate=pl.CostEstimate(flops=1, bytes_accessed=1, transcendentals=0),
    )(*left, *weights, *extra)


def down_rows(left, weights):
    (x,) = left
    total, at = None, 0
    for w in weights:
        term = jnp.dot(x[:, at : at + w.shape[0]], w[...], preferred_element_type=F32)
        total, at = term if total is None else total + term, at + w.shape[0]
    return total


def gate_part(rows_two, weights):
    def finish(product, extra, outs):
        outs[0][...] = product

    return row_kernel(down_rows, [rows_two], weights, weights[0].shape[1], [], [F32], finish)[0]


def up_part(rows_two, weights, gate_pre):
    def finish(up, extra, outs):
        gate = extra[0][...]
        sigmoid = 1.0 / (1.0 + jnp.exp(-gate))
        silu = gate * sigmoid
        outs[0][...] = (silu * up).astype(BF16)
        outs[1][...] = (up * sigmoid * (1.0 + gate * (1.0 - sigmoid))).astype(BF16)
        outs[2][...] = silu.astype(BF16)

    hidden, *factors = row_kernel(
        down_rows, [rows_two], weights, weights[0].shape[1], [gate_pre], [BF16] * 3, finish, 256
    )
    return hidden, factors


def hidden_back(grad_rows, lows, highs, factors):
    def multiply(left, weights):
        (x,) = left
        products, total, at = [], None, 0
        for w in weights[: len(lows)]:
            term = dot_nt(x[:, at : at + w.shape[1]], w[...])
            total, at = term if total is None else total + term, at + w.shape[1]
        products.append(total)
        total = None
        for a, w in enumerate(weights[len(lows) :]):
            step = w.shape[1] // 2
            for place, sub in ((a, 0), (4 + a, 1)):
                term = dot_nt(
                    x[:, place * step : (place + 1) * step], w[:, sub * step : (sub + 1) * step]
                )
                total = term if total is None else total + term
        if highs:
            products.append(total)
        return products

    def finish(products, extra, outs):
        at = 0
        for product in products:
            columns = slice(at, at + product.shape[1])
            for factor, out in zip(extra, outs, strict=True):
                out[:, columns] = (product * factor[:, columns].astype(F32)).astype(BF16)
            at = columns.stop

    width = factors[0].shape[1]
    return row_kernel(
        multiply, [grad_rows], [*lows, *highs], width, factors, [BF16] * 2, finish, 256
    )


def feed_back(grad_gate, grad_up, w_gate, w_ups):
    def multiply(left, weights):
        products, row = [], 0
        for w_up in weights[1:]:
            rows = slice(row, row + w_up.shape[0])
            products.append(dot_nt(left[0][...], weights[0][rows, :]) + dot_nt(left[1][...], w_up[...]))
            row = rows.stop
        return products

    def finish(products, extra, outs):
        at = 0
        for product in products:
            outs[0][:, at : at + product.shape[1]] = product.astype(BF16)
            at += product.shape[1]

    return row_kernel(
        multiply,
        [grad_gate, grad_up],
        [w_gate, *w_ups],
        w_gate.shape[0],
        [],
        [BF16],
        finish,
        256,
    )[0]


def held_rows(order, gathered):
    rows, width = gathered.shape
    count = rows // ROW_BLOCKS

    def body(order, x, out):
        for held, true in spans(order, width):
            out[:, held] = x[:, true]

    spec = pl.BlockSpec((count, width), lambda i: (i, 0))
    return call(
        body,
        jax.ShapeDtypeStruct((rows, width), BF16),
        (order, gathered),
        nbytes=4 * rows * width,
        grid=(ROW_BLOCKS,),
        in_specs=[SCALARS, spec],
        out_specs=spec,
    )


def middle(order, layer_in, came):
    count, width = layer_in.shape

    def body(order, x, came, mid, unit, inverse):
        for held, true in spans(order, width):
            mid[:, held] = x[:, true].astype(F32) + came[:, held].astype(F32)
        values = mid[...]
        scale = lax.rsqrt(jnp.mean(values * values, axis=-1, keepdims=True) + EPSILON)
        inverse[...] = scale
        unit[...] = (values * scale).astype(BF16)

    return call(
        body,
        (
            jax.ShapeDtypeStruct((count, width), F32),
            jax.ShapeDtypeStruct((count, width), BF16),
            jax.ShapeDtypeStruct((count, 1), F32),
        ),
        (order, layer_in, came),
        nbytes=20 * count * width,
        in_specs=[SCALARS] + whole(2),
        out_specs=tuple(whole(3)),
    )


def layer_end(order, mid, came):
    count, width = mid.shape

    def body(order, mid, came, out):
        for held, true in spans(order, width):
            total = mid[:, held] + came[:, held].astype(F32)
            out[:, true] = total.astype(BF16)

    return call(
        body,
        jax.ShapeDtypeStruct((count, width), BF16),
        (order, mid, came),
        nbytes=14 * count * width,
        in_specs=[SCALARS] + whole(2),
        out_specs=whole(1)[0],
    )


def middle_back(order, out_grad, mid, inverse, came):
    count, width = mid.shape

    def body(order, dy, mid, inverse, came, grad, low):
        scale = inverse[...]
        grad_unit = came[...].astype(F32)
        unit = mid[...] * scale
        inner = jnp.mean(grad_unit * unit, axis=-1, keepdims=True)
        grad[...] = scale * (grad_unit - unit * inner)
        for held, true in spans(order, width):
            total = grad[:, held] + dy[:, true].astype(F32)
            grad[:, held] = total
            low[:, held] = total.astype(BF16)

    return call(
        body,
        (
            jax.ShapeDtypeStruct((count, width), F32),
            jax.ShapeDtypeStruct((count, width), BF16),
        ),
        (order, out_grad, mid, inverse, came),
        nbytes=20 * count * width,
        in_specs=[SCALARS] + whole(4),
        out_specs=tuple(whole(2)),
    )


def input_back(order, layer_in, grad_mid, came):
    count, width = grad_mid.shape

    def body(order, x, grad_mid, came, out, unit):
        values = x[...].astype(F32)
        scale = lax.rsqrt(jnp.mean(values * values, axis=-1, keepdims=True) + EPSILON)
        for held, true in spans(order, width):
            unit[:, held] = x[:, true].astype(F32) * scale
        grad_unit = came[...].astype(F32)
        inner = jnp.mean(grad_unit * unit[...], axis=-1, keepdims=True)
        unit[...] = grad_mid[...] + scale * (grad_unit - unit[...] * inner)
        for held, true in spans(order, width):
            out[:, true] = unit[:, held]

    return call(
        body,
        jax.ShapeDtypeStruct((count, width), F32),
        (order, layer_in, grad_mid, came),
        nbytes=16 * count * width,
        in_specs=[SCALARS] + whole(3),
        out_specs=whole(1)[0],
        scratch_shapes=[pltpu.VMEM((count, width), F32)],
    )


def gather_rows(rows):
    return lax.all_gather(rows, "tp", axis=0, tiled=True)


def sum_rows(partial):
    return lax.psum_scatter(partial, "tp", scatter_dimension=0, tiled=True)


class Taker:
    def __init__(self, held):
        self.held = held

    def __getattr__(self, name):
        return self.held.pop(name)


class Held(dict):
    __getattr__ = dict.__getitem__

    @property
    def out(self):
        return Taker(self)


def fence(state):
    if isinstance(state, Held):
        return Held(lax.optimization_barrier(dict(state)))
    return lax.optimization_barrier(state)


def zed(values, step):
    return lax.ppermute(values, "fsdp", [(i, i ^ (2 * step)) for i in range(8)])


def why(values):
    return lax.ppermute(values, "fsdp", [(i, i ^ 1) for i in range(8)])


def teep(values, mask):
    return lax.ppermute(values, "tp", [(i, i ^ mask) for i in range(4)])


def own_gains(gains):
    t = lax.axis_index("tp")
    own = jnp.stack(gains)
    near = jnp.stack([own, teep(own, 1)], axis=1)
    near = jnp.where((t & 1) == 1, near[:, ::-1], near)
    both = jnp.stack([near, teep(near, 2)], axis=1)
    both = jnp.where((t >> 1) == 1, both[:, ::-1], both)
    return both.reshape(len(gains), -1)


def share_gains(terms):
    t = lax.axis_index("tp")
    both = jnp.stack(terms).reshape(len(terms), 2, 2, -1)
    both = jnp.where((t >> 1) == 1, both[:, ::-1], both)
    both = both[:, 0] + teep(both[:, 1], 2)
    both = jnp.where((t & 1) == 1, both[:, ::-1], both)
    both = both[:, 0] + teep(both[:, 1], 1)
    return [both[i] for i in range(len(terms))]


def part(left, right, axis, first, last):
    step = (left if axis == 0 else right).shape[1] // COLUMN_BLOCKS
    at = slice(first * step, last * step)
    if axis == 0:
        return outer(left[:, at], right)
    return outer(left, right[:, at])


def both(left, right, first, last):
    parts = [part(left, right, 1, b + first, b + last).astype(BF16) for b in (0, 4)]
    return jnp.concatenate(parts, axis=1)


def joined(values, axis, first, last, *came):
    step = values.shape[axis] // 4
    total = lax.slice_in_dim(values, first * step, last * step, axis=axis).astype(F32)
    for array, at, count in came:
        size = array.shape[axis] // count
        piece = lax.slice_in_dim(array, at * size, (at + last - first) * size, axis=axis)
        total = total + piece.astype(F32)
    return total


def summed(total, came):
    for values in came:
        total = total + values.astype(F32)
    return total


def scheduled(
    layer_in,
    seq_lengths,
    attn_gain,
    w_query,
    w_key,
    w_value,
    w_output,
    mlp_gain,
    w_gate,
    w_up,
    w_down,
    out_grad,
):
    group_rows = layer_in.shape[0] * lax.axis_size("tp")
    query_width, key_width = w_query.shape[1], w_key.shape[1]
    pairs = query_width // (2 * HD)
    masks = [2 * a + b for b in (0, 1) for a in (0, 2, 1, 3)]
    order = lax.axis_index("fsdp") ^ jnp.array(masks, jnp.int32)
    cut = w_down.shape[0] // 256 * 128 + 128

    input_rows = gather_rows(layer_in)
    down_high = w_down[cut:]
    v = Held(
        o=jnp.concatenate([w_output] + [zed(w_output, a) for a in (2, 1, 3)], axis=1),
        down_high=[down_high, why(down_high)],
        down_low=w_down[:cut],
        gains=own_gains([attn_gain, mlp_gain])[:, :, None],
        order=order,
        layer_in=layer_in,
        out_grad=out_grad,
        w_qkv=jnp.concatenate([w_query, w_key, w_value], axis=1),
        w_gate=w_gate,
        w_up=w_up,
    )
    first_at, where_at = positions(seq_lengths, group_rows)
    v.update(first_at=first_at, tables=rope_tables(where_at[0], HD))
    v = fence(v)

    q = (v.w_qkv.astype(F32) * v.gains[0]).astype(BF16)
    q = jnp.concatenate([q] + [zed(q, a) for a in (2, 1, 3)], axis=0)
    oy = why(v.o)
    g = (v.w_gate.astype(F32) * v.gains[1]).astype(BF16)
    u = (v.w_up.astype(F32) * v.gains[1]).astype(BF16)
    dq = jnp.concatenate(v.out.down_high, axis=1)
    v.update(q=q, oy=oy, g=g, u=u, dq=dq)
    v = fence(v)

    g = [v.g, zed(v.g, 2), zed(v.g, 1)]
    qy = why(v.q)
    w_output_all = jnp.concatenate([v.out.o, v.out.oy], axis=1)
    rows_one = unit_rows(v.order, input_rows)
    v.update(g=g, qy=qy, w_output_all=w_output_all, rows_one=rows_one)
    v = fence(v)

    grad_gathered = gather_rows(v.out_grad)
    g = v.g + [zed(v.g[1], 1)]
    u = [v.u, zed(v.u, 1)]
    gy = [why(v.g[0]), why(v.g[1])]
    qkv = project_rotate(v.rows_one, v.q, v.qy, *v.tables)
    attended, logs = attention(qkv, v.first_at, pairs)
    partial = project(attended, v.w_output_all).astype(BF16)
    v.update(g=g, gy=gy, u=u, qkv=qkv, attended=attended, logs=logs, partial=partial)
    v = fence(v)

    came = sum_rows(v.out.partial)
    u = [v.u[0], zed(v.u[0], 2), v.u[1]]
    gy = v.gy + [why(v.g[2]), why(v.g[3])]
    grad_rows = held_rows(v.order, grad_gathered)
    v.update(u=u, gy=gy, grad_rows=grad_rows)
    v = fence(v)

    u = v.u + [zed(v.u[1], 1)]
    low = v.out.down_low
    low = [low, zed(low, 2), zed(low, 1)]
    uy = [why(v.u[0]), why(v.u[1])]
    w_gate_all = jnp.concatenate(v.out.g + v.out.gy, axis=0)
    mid, unit_two, inverse_two = middle(v.order, v.layer_in, came)
    v.update(u=u, uy=uy, low=low, w_gate_all=w_gate_all)
    v.update(mid=mid, unit_two=unit_two, inverse_two=inverse_two)
    v = fence(v)

    rows_two = gather_rows(v.out.unit_two)
    low = [jnp.concatenate(v.low, axis=1), zed(v.low[1], 1)]
    dq = [v.dq, zed(v.dq, 2)]
    w_ups = [jnp.concatenate(v.u + v.uy, axis=0), why(v.u[2]), why(v.u[3])]
    v.update(low=low, dq=dq, w_ups=w_ups)
    v = fence(v)

    low = v.low + [why(v.low[0]), why(v.low[1])]
    dq = v.dq + [zed(v.dq[0], 1), zed(v.dq[1], 1)]
    gate_pre = gate_part(rows_two, [v.w_gate_all])
    hidden, factors = up_part(rows_two, v.w_ups, gate_pre)
    low_away = part(hidden[:, :cut], v.grad_rows, 1, 4, 8).astype(BF16)
    high_away = both(hidden[:, cut:], v.grad_rows, 2, 4)
    v.update(dq=dq, low=low, rows_two=rows_two, hidden=hidden)
    v.update(factors=factors, low_away=low_away, high_away=high_away)
    v = fence(v)

    first = why(v.low_away)
    high_near = zed(v.high_away, 1)
    grad_gate, grad_up = hidden_back(v.grad_rows, v.low, v.dq, v.out.factors)
    partial = feed_back(grad_gate, grad_up, v.w_gate_all, v.w_ups)
    gate_away = part(v.rows_two, grad_gate, 0, 6, 8).astype(BF16)
    low_kept = part(v.hidden[:, :cut], v.grad_rows, 1, 0, 4).astype(BF16)
    high_kept = both(v.hidden[:, cut:], v.grad_rows, 0, 2)
    v.update(first=first, high_near=high_near, gate_away=gate_away)
    v.update(grad_gate=grad_gate, grad_up=grad_up)
    v.update(partial=partial, low_kept=low_kept, high_kept=high_kept)
    v = fence(v)

    came = sum_rows(v.out.partial)
    low_near = zed(joined(v.low_kept, 1, 2, 4, (v.first, 2, 4)).astype(BF16), 1)
    step = v.high_kept.shape[1] // 4
    ones = [slice(b * 2 * step + step, b * 2 * step + 2 * step) for b in (0, 1)]
    high_one = [
        (v.high_kept[:, at].astype(F32) + v.high_near[:, at].astype(F32)).astype(BF16)
        for at in ones
    ]
    high_far = zed(jnp.concatenate(high_one, axis=1), 2)
    gate_first = why(v.gate_away)
    gate_away = part(v.rows_two, v.grad_gate, 0, 4, 6).astype(BF16)
    gate_kept = part(v.rows_two, v.grad_gate, 0, 0, 4).astype(BF16)
    up_away = part(v.rows_two, v.grad_up, 0, 6, 8).astype(BF16)
    v.update(low_near=low_near, high_far=high_far, gate_first=gate_first, gate_away=gate_away)
    v.update(gate_kept=gate_kept, up_away=up_away)
    v = fence(v)

    low_far = zed(joined(v.low_kept, 1, 1, 2, (v.first, 1, 4), (v.low_near, 1, 2)).astype(BF16), 2)
    three = zed(joined(v.gate_kept, 0, 3, 4, (v.gate_first, 1, 2)).astype(BF16), 1)
    gate_second = why(v.gate_away)
    grad_mid, grad_mid_low = middle_back(v.order, v.out_grad, v.mid, v.inverse_two, came)
    zeros = [slice(b * 2 * step, b * 2 * step + step) for b in (0, 1)]
    high_own = [
        v.high_kept[:, at].astype(F32)
        + v.high_near[:, at].astype(F32)
        + v.high_far[:, b * step : (b + 1) * step].astype(F32)
        for b, at in enumerate(zeros)
    ]
    high_over = high_own[1].astype(BF16)
    up_away = [v.up_away, part(v.rows_two, v.grad_up, 0, 4, 6).astype(BF16)]
    up_kept = part(v.rows_two, v.grad_up, 0, 0, 4).astype(BF16)
    v.update(low_far=low_far, three=three, gate_second=gate_second, grad_mid=grad_mid)
    v.update(grad_mid_low=grad_mid_low, high_own=high_own[0], high_over=high_over)
    v.update(up_away=up_away, up_kept=up_kept)
    v = fence(v)

    grad_mid_rows = gather_rows(v.out.grad_mid_low)
    far = joined(v.gate_kept, 0, 1, 2, (v.gate_second, 1, 2), (v.three, 0, 1)).astype(BF16)
    near = joined(v.gate_kept, 0, 2, 3, (v.gate_first, 0, 2)).astype(BF16)
    gate_came = [zed(far, 2), zed(near, 1)]
    up_first = why(v.up_away[0])
    low_sh = joined(
        v.low_kept, 1, 0, 1, (v.first, 0, 4), (v.low_near, 0, 2), (v.low_far, 0, 1)
    )
    high = v.out.dq
    high = [w[:, :step] for w in high] + [w[:, step:] for w in high]
    high_all = jnp.concatenate(high, axis=1)
    low_all = jnp.concatenate(v.out.low, axis=1)
    partial = project(v.hidden[:, :cut], low_all)
    output_part = (partial + project(v.hidden[:, cut:], high_all)).astype(BF16)
    v.update(gate_came=gate_came, up_first=up_first, low_sh=low_sh, output_part=output_part)
    v = fence(v)

    three = zed(joined(v.up_kept, 0, 3, 4, (v.up_first, 1, 2)).astype(BF16), 1)
    up_second = why(v.up_away[1])
    grad_attended = project_back(grad_mid_rows, v.w_output_all).astype(BF16)
    grad_query, grad_kv = attention_back(
        v.qkv, v.first_at, v.logs, grad_attended, *v.tables, pairs
    )
    grad_qkv = jnp.concatenate([grad_query, grad_kv], axis=1)
    qkv_away = part(v.rows_one, grad_qkv, 0, 4, 8).astype(BF16)
    came_out = sum_rows(v.output_part)
    v.update(three=three, up_second=up_second, grad_qkv=grad_qkv, grad_mid_rows=grad_mid_rows)
    v.update(qkv_away=qkv_away)
    v = fence(v)

    far = joined(v.up_kept, 0, 1, 2, (v.up_second, 1, 2), (v.three, 0, 1)).astype(BF16)
    near = joined(v.up_kept, 0, 2, 3, (v.up_first, 0, 2)).astype(BF16)
    up_came = [zed(far, 2), zed(near, 1)]
    first = why(v.out.qkv_away)
    w_qkv_all = jnp.concatenate([v.q, v.qy], axis=0)
    partial = project_back(v.grad_qkv, w_qkv_all).astype(BF16)
    qkv_kept = part(v.rows_one, v.grad_qkv, 0, 0, 4).astype(BF16)
    output_away = part(v.attended, v.grad_mid_rows, 1, 4, 8).astype(BF16)
    grad_gate_sh = summed(joined(v.gate_kept, 0, 0, 1, (v.gate_second, 0, 2)), v.gate_came)
    v.update(up_came=up_came, first=first, qkv_kept=qkv_kept, output_away=output_away)
    v.update(partial=partial, grad_gate_sh=grad_gate_sh)
    v = fence(v)

    came = sum_rows(v.out.partial)
    pieces = [
        zed(joined(v.qkv_kept, 0, i, i + 1, (v.first, i, 4)).astype(BF16), a)
        for i, a in ((1, 2), (2, 1), (3, 3))
    ]
    over = why(v.output_away)
    high_over = why(v.high_over)
    gain_one, gain_two = v.gains[0], v.gains[1]
    grad_gate_sh = v.grad_gate_sh
    grad_up_sh = summed(joined(v.up_kept, 0, 0, 1, (v.up_second, 0, 2)), v.up_came)
    gain_two_term = jnp.sum(
        grad_gate_sh * v.w_gate.astype(F32) + grad_up_sh * v.w_up.astype(F32), axis=1
    )
    output_kept = part(v.attended, v.grad_mid_rows, 1, 0, 4).astype(BF16)
    layer_out = layer_end(v.order, v.mid, came_out)
    v.update(pieces=pieces, over=over, high_over=high_over, gain_two_term=gain_two_term)
    v.update(grad_gate_sh=grad_gate_sh * gain_two, grad_up_sh=grad_up_sh * gain_two)
    v.update(output_kept=output_kept, layer_out=layer_out)
    v = fence(v)

    pieces = [
        zed(joined(v.output_kept, 1, i, i + 1, (v.over, i, 4)).astype(BF16), a)
        for i, a in ((1, 2), (2, 1), (3, 3))
    ]
    grad_down_sh = jnp.concatenate([v.low_sh, v.high_own + v.high_over.astype(F32)], axis=0)
    in_grad = input_back(v.order, v.layer_in, v.grad_mid, came)
    in_grad, came_pieces, over = fence((in_grad, v.pieces, v.over))
    grad_qkv_sh = summed(joined(v.qkv_kept, 0, 0, 1, (v.first, 0, 4)), came_pieces)
    gain_one_term = jnp.sum(grad_qkv_sh * v.w_qkv.astype(F32), axis=1)
    gain_one_grad, gain_two_grad = share_gains([gain_one_term, v.gain_two_term])
    grad_qkv_sh = grad_qkv_sh * v.gains[0]
    return (
        v.layer_out,
        in_grad,
        gain_one_grad,
        grad_qkv_sh[:, :query_width],
        grad_qkv_sh[:, query_width : query_width + key_width],
        grad_qkv_sh[:, query_width + key_width :],
        summed(joined(v.output_kept, 1, 0, 1, (over, 0, 4)), pieces),
        gain_two_grad,
        v.grad_gate_sh,
        v.grad_up_sh,
        grad_down_sh,
    )


def direct(
    layer_in,
    seq_lengths,
    attn_gain,
    w_query,
    w_key,
    w_value,
    w_output,
    mlp_gain,
    w_gate,
    w_up,
    w_down,
    out_grad,
):
    def gather(shard, axis):
        return lax.all_gather(shard, "fsdp", axis=axis, tiled=True)

    def scatter(left, right, axis):
        total = outer(left, right).astype(BF16)
        return lax.psum_scatter(total, "fsdp", scatter_dimension=axis, tiled=True).astype(F32)

    group_rows = layer_in.shape[0] * lax.axis_size("tp")
    query_width, key_width = w_query.shape[1], w_key.shape[1]
    pairs = query_width // (2 * HD)
    order = jnp.arange(COLUMN_BLOCKS, dtype=jnp.int32)
    gain_one, gain_two = [
        lax.all_gather(gain, "tp", axis=0, tiled=True)[:, None] for gain in (attn_gain, mlp_gain)
    ]
    w_qkv = jnp.concatenate([w_query, w_key, w_value], axis=1)
    w_output_all = gather(w_output, 1)
    w_qkv_all = gather((w_qkv.astype(F32) * gain_one).astype(BF16), 0)
    w_gate_all = gather((w_gate.astype(F32) * gain_two).astype(BF16), 0)
    w_up_all = gather((w_up.astype(F32) * gain_two).astype(BF16), 0)
    w_down_all = gather(w_down, 1)
    first_at, where_at = positions(seq_lengths, group_rows)
    cosine, sine = rope_tables(where_at[0], HD)
    rows_one = unit_rows(order, gather_rows(layer_in))
    qkv = project_rotate(rows_one, *jnp.split(w_qkv_all, 2), cosine, sine)
    grad_rows = held_rows(order, gather_rows(out_grad))
    attended, logs = attention(qkv, first_at, pairs)
    came = sum_rows(project(attended, w_output_all).astype(BF16))
    mid, unit_two, inverse_two = middle(order, layer_in, came)
    rows_two = gather_rows(unit_two)
    gate_pre = gate_part(rows_two, [w_gate_all])
    hidden, factors = up_part(rows_two, [w_up_all], gate_pre)
    grad_down_sh = scatter(hidden, grad_rows, 1)
    came = sum_rows(project(hidden, w_down_all).astype(BF16))
    layer_out = layer_end(order, mid, came)
    grad_gate, grad_up = hidden_back(grad_rows, [w_down_all], [], factors)
    came = sum_rows(feed_back(grad_gate, grad_up, w_gate_all, [w_up_all]))
    grad_gate_sh = scatter(rows_two, grad_gate, 0)
    grad_up_sh = scatter(rows_two, grad_up, 0)
    grad_mid, grad_mid_low = middle_back(order, out_grad, mid, inverse_two, came)
    grad_mid_rows = gather_rows(grad_mid_low)
    grad_attended = project_back(grad_mid_rows, w_output_all).astype(BF16)
    grad_output_sh = scatter(attended, grad_mid_rows, 1)
    grad_query, grad_kv = attention_back(
        qkv, first_at, logs, grad_attended, cosine, sine, pairs
    )
    grad_qkv = jnp.concatenate([grad_query, grad_kv], axis=1)
    came = sum_rows(project_back(grad_qkv, w_qkv_all).astype(BF16))
    in_grad = input_back(order, layer_in, grad_mid, came)
    grad_qkv_sh = scatter(rows_one, grad_qkv, 0)
    gain_one_term = jnp.sum(grad_qkv_sh * w_qkv.astype(F32), axis=1)
    gain_two_term = jnp.sum(
        grad_gate_sh * w_gate.astype(F32) + grad_up_sh * w_up.astype(F32), axis=1
    )
    gain_one_grad, gain_two_grad = [
        lax.psum_scatter(term, "tp", scatter_dimension=0, tiled=True)
        for term in (gain_one_term, gain_two_term)
    ]
    grad_qkv_sh = grad_qkv_sh * gain_one
    return (
        layer_out,
        in_grad,
        gain_one_grad,
        grad_qkv_sh[:, :query_width],
        grad_qkv_sh[:, query_width : query_width + key_width],
        grad_qkv_sh[:, query_width + key_width :],
        grad_output_sh,
        gain_two_grad,
        grad_gate_sh * gain_two,
        grad_up_sh * gain_two,
        grad_down_sh,
    )


def solution(mesh):
    placed = (
        P(("fsdp", "tp"), None),
        P("fsdp", None),
        P(("fsdp", "tp")),
        P("fsdp", "tp"),
        P("fsdp", "tp"),
        P("fsdp", "tp"),
        P("tp", "fsdp"),
        P(("fsdp", "tp")),
        P("fsdp", "tp"),
        P("fsdp", "tp"),
        P("tp", "fsdp"),
        P(("fsdp", "tp"), None),
    )
    paired = (mesh.shape["fsdp"], mesh.shape["tp"]) == (8, 4)
    return jax.shard_map(
        scheduled if paired else direct,
        mesh=mesh,
        in_specs=placed,
        out_specs=(
            P(("fsdp", "tp"), None),
            P(("fsdp", "tp"), None),
            P(("fsdp", "tp")),
            P("fsdp", "tp"),
            P("fsdp", "tp"),
            P("fsdp", "tp"),
            P("tp", "fsdp"),
            P(("fsdp", "tp")),
            P("fsdp", "tp"),
            P("fsdp", "tp"),
            P("tp", "fsdp"),
        ),
        check_vma=False,
    )
```

```python
import math

import jax
import jax.numpy as jnp
from jax import lax
from jax.experimental import pallas as pl
from jax.experimental.pallas import tpu as pltpu
from jax.sharding import PartitionSpec as P

HD = 64
MAXLEN = 512
EPSILON = 1e-05
ROPE_BASE = 10000.0
MASKED_OUT = -1e30
TILE = 512
COLUMN_BLOCKS = 8
ROW_BLOCKS = 4
VMEM = 56 * 1024 * 1024
F32 = jnp.float32
BF16 = jnp.bfloat16


def positions(lengths, count):
    starts = jnp.cumsum(lengths, axis=-1) - lengths
    indices = jnp.arange(count, dtype=jnp.int32)
    inside = (indices[None, :, None] >= starts[:, None, :]) & (
        indices[None, :, None] < (starts + lengths)[:, None, :]
    )
    first_at = jnp.sum(jnp.where(inside, starts[:, None, :], 0), axis=-1)
    return first_at, indices[None, :] - first_at


def rope_tables(where_at, width):
    half_width = width // 2
    inverse_freq = ROPE_BASE ** (-(jnp.arange(half_width, dtype=F32) * 2.0 / width))
    angles = where_at.astype(F32)[:, None] * inverse_freq[None, :]
    cosine, sine = jnp.cos(angles), jnp.sin(angles)
    return jnp.concatenate([cosine] * 4, axis=1), jnp.concatenate([sine] * 4, axis=1)


def project(left, weight):
    return jnp.dot(left, weight, preferred_element_type=F32)


def project_back(grad, weight):
    return jnp.einsum("tc,dc->td", grad, weight, preferred_element_type=F32)


def outer(left, right):
    return jnp.einsum("ta,tb->ab", left, right, preferred_element_type=F32)


def call(body, outs, operands, flops=0, nbytes=0, **more):
    return pl.pallas_call(
        body,
        out_shape=outs,
        compiler_params=pltpu.CompilerParams(vmem_limit_bytes=VMEM),
        cost_estimate=pl.CostEstimate(flops=1, bytes_accessed=1, transcendentals=0),
        **more,
    )(*operands)


def whole(count):
    return [pl.BlockSpec(memory_space=pltpu.VMEM)] * count


SCALARS = pl.BlockSpec(memory_space=pltpu.SMEM)


def spans(order, width):
    step = width // COLUMN_BLOCKS
    return [
        (slice(j * step, (j + 1) * step), pl.ds(pl.multiple_of(order[j] * step, step), step))
        for j in range(COLUMN_BLOCKS)
    ]


def turned(values, lanes):
    width = values.shape[-1]
    first = (lanes % HD) < HD // 2
    return jnp.where(
        first, -pltpu.roll(values, width - HD // 2, 1), pltpu.roll(values, HD // 2, 1)
    )


def unit_rows(order, gathered):
    rows, width = gathered.shape
    count = rows // ROW_BLOCKS

    def body(order, x, out):
        values = x[...].astype(F32)
        inverse = lax.rsqrt(jnp.mean(values * values, axis=-1, keepdims=True) + EPSILON)
        for held, true in spans(order, width):
            out[:, held] = (x[:, true].astype(F32) * inverse).astype(BF16)

    spec = pl.BlockSpec((count, width), lambda i: (i, 0))
    return call(
        body,
        jax.ShapeDtypeStruct((rows, width), BF16),
        (order, gathered),
        nbytes=4 * rows * width,
        grid=(ROW_BLOCKS,),
        in_specs=[SCALARS, spec],
        out_specs=spec,
    )


def project_rotate(rows_one, weights_low, weights_high, cosine, sine):
    rows, width = rows_one.shape
    count = rows // ROW_BLOCKS
    half, total = weights_low.shape
    kv = 2 * HD

    def body(x, low, high, c, s, out):
        product = project(x[:, :half], low[...]) + project(x[:, half:], high[...])
        cos, sin = c[...], s[...]
        lanes = lax.broadcasted_iota(jnp.int32, cos.shape, 1)
        for at in range(0, total, 128):
            part = product[:, at : at + 128]
            if at + 128 > total - kv:
                co, si = jnp.where(lanes < HD, cos, 1.0), jnp.where(lanes < HD, sin, 0.0)
            else:
                co, si = cos, sin
            out[:, at : at + 128] = (part * co + turned(part, lanes) * si).astype(BF16)

    def tiles(columns):
        return pl.BlockSpec((count, columns), lambda i: (i, 0))

    weight = pl.BlockSpec((half, total), lambda i: (0, 0), pipeline_mode=pl.Buffered(1))
    return call(
        body,
        jax.ShapeDtypeStruct((rows, total), BF16),
        (rows_one, weights_low, weights_high, cosine, sine),
        flops=2 * rows * width * total,
        nbytes=2 * (rows * width + width * total),
        grid=(ROW_BLOCKS,),
        in_specs=[tiles(width), weight, weight, tiles(2 * HD), tiles(2 * HD)],
        out_specs=tiles(total),
    )


def window(i, span):
    return max(0, i * span - MAXLEN), (i + 1) * span


def shown(first, i, span):
    low, high = window(i, span)
    keys = low + lax.broadcasted_iota(jnp.int32, (high - low, span), 0)
    rows = i * span + lax.broadcasted_iota(jnp.int32, (high - low, span), 1)
    return (keys <= rows) & (keys >= first[:, i * span : (i + 1) * span])


def dot_nt(left, right):
    return lax.dot_general(left, right, (((1,), (1,)), ((), ())), preferred_element_type=F32)


def dot_tn(left, right):
    return lax.dot_general(left, right, (((0,), (0,)), ((), ())), preferred_element_type=F32)


def stacked(values, heads):
    return jnp.concatenate([values[:, h * HD : (h + 1) * HD] for h in range(heads)], axis=0)


def side_by_side(values, span, heads):
    parts = [values[:, h * span : (h + 1) * span] for h in range(heads)]
    return [jnp.concatenate(parts[h : h + 2], axis=0).T for h in range(0, heads, 2)]


def attention(qkv, first, pairs):
    rows = qkv.shape[0]
    span = rows // ROW_BLOCKS
    heads = min(4, 2 * pairs)
    width = heads * HD

    def body(q, kv, first, out, logs):
        for i in range(rows // span):
            low, high = window(i, span)
            at = slice(i * span, (i + 1) * span)
            allowed = jnp.concatenate([shown(first, i, span)] * heads, axis=1)
            keys, values = kv[low:high, :HD], kv[low:high, HD:]
            queries = stacked((q[at, :] * 0.125).astype(BF16), heads)
            scores = jnp.where(allowed, dot_nt(keys, queries), MASKED_OUT)
            top = jnp.max(scores, axis=0, keepdims=True)
            shares = jnp.exp(scores - top)
            total = jnp.sum(shares, axis=0, keepdims=True)
            mixed = dot_tn(values, shares.astype(BF16)) / total
            log = top + jnp.log(total)
            for h in range(heads):
                logs[h // 2, h % 2 : h % 2 + 1, at] = log[:, h * span : (h + 1) * span]
            for p, pair in enumerate(side_by_side(mixed, span, heads)):
                out[at, p * 2 * HD : (p + 1) * 2 * HD] = pair.astype(BF16)

    return call(
        body,
        (
            jax.ShapeDtypeStruct((rows, pairs * 2 * HD), BF16),
            jax.ShapeDtypeStruct((pairs, 2, rows), F32),
        ),
        (qkv, qkv, first),
        grid=(2 * pairs // heads,),
        in_specs=[
            pl.BlockSpec((rows, width), lambda p: (0, p)),
            pl.BlockSpec((rows, 2 * HD), lambda p: (0, pairs)),
            pl.BlockSpec((1, rows), lambda p: (0, 0)),
        ],
        out_specs=(
            pl.BlockSpec((rows, width), lambda p: (0, p)),
            pl.BlockSpec((heads // 2, 2, rows), lambda p: (p, 0, 0)),
        ),
    )


def attention_back(qkv, first, logs, grads, cosine, sine, pairs):
    rows = qkv.shape[0]
    span = rows // (2 * ROW_BLOCKS)
    heads = min(4, 2 * pairs)
    width = heads * HD

    def body(q, kv, first, logs, grad, c, s, dq, dkv, total):
        @pl.when(pl.program_id(0) == 0)
        def _():
            total[...] = jnp.zeros_like(total)

        lanes = lax.broadcasted_iota(jnp.int32, (span, 2 * HD), 1)
        for i in range(rows // span):
            low, high = window(i, span)
            at = slice(i * span, (i + 1) * span)
            allowed = jnp.concatenate([shown(first, i, span)] * heads, axis=1)
            keys, values = kv[low:high, :HD], kv[low:high, HD:]
            queries = stacked((q[at, :] * 0.125).astype(BF16), heads)
            came = stacked(grad[at, :], heads)
            log = jnp.concatenate([logs[h // 2, h % 2 : h % 2 + 1, at] for h in range(heads)], axis=1)
            shares = jnp.where(allowed, jnp.exp(dot_nt(keys, queries) - log), 0.0)
            change = dot_nt(values, came)
            inner = jnp.sum(shares * change, axis=0, keepdims=True)
            score_grads = (shares * (change - inner)).astype(BF16)
            value_part = jnp.dot(shares.astype(BF16), came, preferred_element_type=F32)
            key_part = jnp.dot(score_grads, queries, preferred_element_type=F32)
            total[low:high, :] += jnp.concatenate([key_part, value_part], axis=1)
            query_grads = dot_tn(keys, score_grads) * 0.125
            for p, pair in enumerate(side_by_side(query_grads, span, heads)):
                dq[at, p * 2 * HD : (p + 1) * 2 * HD] = (
                    pair * c[at, :] - turned(pair * s[at, :], lanes)
                ).astype(BF16)

        @pl.when(pl.program_id(0) == 2 * pairs // heads - 1)
        def _():
            for i in range(rows // span):
                at = slice(i * span, (i + 1) * span)
                cos = jnp.where(lanes < HD, c[at, :], 1.0)
                sin = jnp.where(lanes < HD, s[at, :], 0.0)
                part = total[at, :]
                dkv[at, :] = (part * cos - turned(part * sin, lanes)).astype(BF16)

    return call(
        body,
        (
            jax.ShapeDtypeStruct((rows, pairs * 2 * HD), BF16),
            jax.ShapeDtypeStruct((rows, 2 * HD), BF16),
        ),
        (qkv, qkv, first, logs, grads, cosine, sine),
        grid=(2 * pairs // heads,),
        in_specs=[
            pl.BlockSpec((rows, width), lambda p: (0, p)),
            pl.BlockSpec((rows, 2 * HD), lambda p: (0, pairs)),
            pl.BlockSpec((1, rows), lambda p: (0, 0)),
            pl.BlockSpec((heads // 2, 2, rows), lambda p: (p, 0, 0)),
            pl.BlockSpec((rows, width), lambda p: (0, p)),
            pl.BlockSpec((rows, 2 * HD), lambda p: (0, 0)),
            pl.BlockSpec((rows, 2 * HD), lambda p: (0, 0)),
        ],
        out_specs=(
            pl.BlockSpec((rows, width), lambda p: (0, p)),
            pl.BlockSpec((rows, 2 * HD), lambda p: (0, 0)),
        ),
        scratch_shapes=[pltpu.VMEM((rows, 2 * HD), F32)],
    )


def row_kernel(multiply, left, weights, width, extra, outs, finish, tile=TILE):
    rows = left[0].shape[0]
    tile = min(tile, rows)
    many = len(left), len(left) + len(weights), len(left) + len(weights) + len(extra)

    def body(*refs):
        product = multiply(refs[: many[0]], refs[many[0] : many[1]])
        finish(product, refs[many[1] : many[2]], refs[many[2] :])

    def tiles(columns):
        return pl.BlockSpec((tile, columns), lambda i: (i, 0))

    widths = [width] * len(outs)
    inner = sum(weight.size for weight in weights)
    return pl.pallas_call(
        body,
        out_shape=tuple(
            jax.ShapeDtypeStruct((rows, columns), kind)
            for columns, kind in zip(widths, outs, strict=True)
        ),
        grid=(rows // tile,),
        in_specs=[tiles(v.shape[1]) for v in left]
        + [
            pl.BlockSpec(v.shape, lambda i: (0, 0), pipeline_mode=pl.Buffered(1)) for v in weights
        ]
        + [tiles(v.shape[1]) for v in extra],
        out_specs=tuple(tiles(columns) for columns in widths),
        compiler_params=pltpu.CompilerParams(vmem_limit_bytes=VMEM),
        cost_estimate=pl.CostEstimate(flops=1, bytes_accessed=1, transcendentals=0),
    )(*left, *weights, *extra)


def down_rows(left, weights):
    (x,) = left
    total, at = None, 0
    for w in weights:
        term = jnp.dot(x[:, at : at + w.shape[0]], w[...], preferred_element_type=F32)
        total, at = term if total is None else total + term, at + w.shape[0]
    return total


def gate_part(rows_two, weights):
    def finish(product, extra, outs):
        outs[0][...] = product

    return row_kernel(down_rows, [rows_two], weights, weights[0].shape[1], [], [F32], finish)[0]


def up_part(rows_two, weights, gate_pre):
    def finish(up, extra, outs):
        gate = extra[0][...]
        sigmoid = 1.0 / (1.0 + jnp.exp(-gate))
        silu = gate * sigmoid
        outs[0][...] = (silu * up).astype(BF16)
        outs[1][...] = (up * sigmoid * (1.0 + gate * (1.0 - sigmoid))).astype(BF16)
        outs[2][...] = silu.astype(BF16)

    hidden, *factors = row_kernel(
        down_rows, [rows_two], weights, weights[0].shape[1], [gate_pre], [BF16] * 3, finish, 256
    )
    return hidden, factors


def hidden_back(grad_rows, lows, highs, factors):
    def multiply(left, weights):
        (x,) = left
        products, total, at = [], None, 0
        for w in weights[: len(lows)]:
            term = dot_nt(x[:, at : at + w.shape[1]], w[...])
            total, at = term if total is None else total + term, at + w.shape[1]
        products.append(total)
        total = None
        for a, w in enumerate(weights[len(lows) :]):
            step = w.shape[1] // 2
            for place, sub in ((a, 0), (4 + a, 1)):
                term = dot_nt(
                    x[:, place * step : (place + 1) * step], w[:, sub * step : (sub + 1) * step]
                )
                total = term if total is None else total + term
        if highs:
            products.append(total)
        return products

    def finish(products, extra, outs):
        at = 0
        for product in products:
            columns = slice(at, at + product.shape[1])
            for factor, out in zip(extra, outs, strict=True):
                out[:, columns] = (product * factor[:, columns].astype(F32)).astype(BF16)
            at = columns.stop

    width = factors[0].shape[1]
    return row_kernel(
        multiply, [grad_rows], [*lows, *highs], width, factors, [BF16] * 2, finish, 256
    )


def feed_back(grad_gate, grad_up, w_gate, w_ups):
    def multiply(left, weights):
        products, row = [], 0
        for w_up in weights[1:]:
            rows = slice(row, row + w_up.shape[0])
            products.append(dot_nt(left[0][...], weights[0][rows, :]) + dot_nt(left[1][...], w_up[...]))
            row = rows.stop
        return products

    def finish(products, extra, outs):
        at = 0
        for product in products:
            outs[0][:, at : at + product.shape[1]] = product.astype(BF16)
            at += product.shape[1]

    return row_kernel(
        multiply,
        [grad_gate, grad_up],
        [w_gate, *w_ups],
        w_gate.shape[0],
        [],
        [BF16],
        finish,
        256,
    )[0]


def held_rows(order, gathered):
    rows, width = gathered.shape
    count = rows // ROW_BLOCKS

    def body(order, x, out):
        for held, true in spans(order, width):
            out[:, held] = x[:, true]

    spec = pl.BlockSpec((count, width), lambda i: (i, 0))
    return call(
        body,
        jax.ShapeDtypeStruct((rows, width), BF16),
        (order, gathered),
        nbytes=4 * rows * width,
        grid=(ROW_BLOCKS,),
        in_specs=[SCALARS, spec],
        out_specs=spec,
    )


def middle(order, layer_in, came):
    count, width = layer_in.shape

    def body(order, x, came, mid, unit, inverse):
        for held, true in spans(order, width):
            mid[:, held] = x[:, true].astype(F32) + came[:, held].astype(F32)
        values = mid[...]
        scale = lax.rsqrt(jnp.mean(values * values, axis=-1, keepdims=True) + EPSILON)
        inverse[...] = scale
        unit[...] = (values * scale).astype(BF16)

    return call(
        body,
        (
            jax.ShapeDtypeStruct((count, width), F32),
            jax.ShapeDtypeStruct((count, width), BF16),
            jax.ShapeDtypeStruct((count, 1), F32),
        ),
        (order, layer_in, came),
        nbytes=20 * count * width,
        in_specs=[SCALARS] + whole(2),
        out_specs=tuple(whole(3)),
    )


def layer_end(order, mid, came):
    count, width = mid.shape

    def body(order, mid, came, out):
        for held, true in spans(order, width):
            total = mid[:, held] + came[:, held].astype(F32)
            out[:, true] = total.astype(BF16)

    return call(
        body,
        jax.ShapeDtypeStruct((count, width), BF16),
        (order, mid, came),
        nbytes=14 * count * width,
        in_specs=[SCALARS] + whole(2),
        out_specs=whole(1)[0],
    )


def middle_back(order, out_grad, mid, inverse, came):
    count, width = mid.shape

    def body(order, dy, mid, inverse, came, grad, low):
        scale = inverse[...]
        grad_unit = came[...].astype(F32)
        unit = mid[...] * scale
        inner = jnp.mean(grad_unit * unit, axis=-1, keepdims=True)
        grad[...] = scale * (grad_unit - unit * inner)
        for held, true in spans(order, width):
            total = grad[:, held] + dy[:, true].astype(F32)
            grad[:, held] = total
            low[:, held] = total.astype(BF16)

    return call(
        body,
        (
            jax.ShapeDtypeStruct((count, width), F32),
            jax.ShapeDtypeStruct((count, width), BF16),
        ),
        (order, out_grad, mid, inverse, came),
        nbytes=20 * count * width,
        in_specs=[SCALARS] + whole(4),
        out_specs=tuple(whole(2)),
    )


def input_back(order, layer_in, grad_mid, came):
    count, width = grad_mid.shape

    def body(order, x, grad_mid, came, out, unit):
        values = x[...].astype(F32)
        scale = lax.rsqrt(jnp.mean(values * values, axis=-1, keepdims=True) + EPSILON)
        for held, true in spans(order, width):
            unit[:, held] = x[:, true].astype(F32) * scale
        grad_unit = came[...].astype(F32)
        inner = jnp.mean(grad_unit * unit[...], axis=-1, keepdims=True)
        unit[...] = grad_mid[...] + scale * (grad_unit - unit[...] * inner)
        for held, true in spans(order, width):
            out[:, true] = unit[:, held]

    return call(
        body,
        jax.ShapeDtypeStruct((count, width), F32),
        (order, layer_in, grad_mid, came),
        nbytes=16 * count * width,
        in_specs=[SCALARS] + whole(3),
        out_specs=whole(1)[0],
        scratch_shapes=[pltpu.VMEM((count, width), F32)],
    )


def gather_rows(rows):
    return lax.all_gather(rows, "tp", axis=0, tiled=True)


def sum_rows(partial):
    return lax.psum_scatter(partial, "tp", scatter_dimension=0, tiled=True)


class Taker:
    def __init__(self, held):
        self.held = held

    def __getattr__(self, name):
        return self.held.pop(name)


class Held(dict):
    __getattr__ = dict.__getitem__

    @property
    def out(self):
        return Taker(self)


def fence(state):
    if isinstance(state, Held):
        return Held(lax.optimization_barrier(dict(state)))
    return lax.optimization_barrier(state)


def zed(values, step):
    return lax.ppermute(values, "fsdp", [(i, i ^ (2 * step)) for i in range(8)])


def why(values):
    return lax.ppermute(values, "fsdp", [(i, i ^ 1) for i in range(8)])


def teep(values, mask):
    return lax.ppermute(values, "tp", [(i, i ^ mask) for i in range(4)])


def own_gains(gains):
    t = lax.axis_index("tp")
    own = jnp.stack(gains)
    near = jnp.stack([own, teep(own, 1)], axis=1)
    near = jnp.where((t & 1) == 1, near[:, ::-1], near)
    both = jnp.stack([near, teep(near, 2)], axis=1)
    both = jnp.where((t >> 1) == 1, both[:, ::-1], both)
    return both.reshape(len(gains), -1)


def share_gains(terms):
    t = lax.axis_index("tp")
    both = jnp.stack(terms).reshape(len(terms), 2, 2, -1)
    both = jnp.where((t >> 1) == 1, both[:, ::-1], both)
    both = both[:, 0] + teep(both[:, 1], 2)
    both = jnp.where((t & 1) == 1, both[:, ::-1], both)
    both = both[:, 0] + teep(both[:, 1], 1)
    return [both[i] for i in range(len(terms))]


def part(left, right, axis, first, last):
    step = (left if axis == 0 else right).shape[1] // COLUMN_BLOCKS
    at = slice(first * step, last * step)
    if axis == 0:
        return outer(left[:, at], right)
    return outer(left, right[:, at])


def both(left, right, first, last):
    parts = [part(left, right, 1, b + first, b + last).astype(BF16) for b in (0, 4)]
    return jnp.concatenate(parts, axis=1)


def joined(values, axis, first, last, *came):
    step = values.shape[axis] // 4
    total = lax.slice_in_dim(values, first * step, last * step, axis=axis).astype(F32)
    for array, at, count in came:
        size = array.shape[axis] // count
        piece = lax.slice_in_dim(array, at * size, (at + last - first) * size, axis=axis)
        total = total + piece.astype(F32)
    return total


def summed(total, came):
    for values in came:
        total = total + values.astype(F32)
    return total


def scheduled(
    layer_in,
    seq_lengths,
    attn_gain,
    w_query,
    w_key,
    w_value,
    w_output,
    mlp_gain,
    w_gate,
    w_up,
    w_down,
    out_grad,
):
    group_rows = layer_in.shape[0] * lax.axis_size("tp")
    query_width, key_width = w_query.shape[1], w_key.shape[1]
    pairs = query_width // (2 * HD)
    masks = [2 * a + b for b in (0, 1) for a in (0, 2, 1, 3)]
    order = lax.axis_index("fsdp") ^ jnp.array(masks, jnp.int32)
    cut = w_down.shape[0] // 256 * 128 + 128

    input_rows = gather_rows(layer_in)
    down_high = w_down[cut:]
    v = Held(
        o=jnp.concatenate([w_output] + [zed(w_output, a) for a in (2, 1, 3)], axis=1),
        down_high=[down_high, why(down_high)],
        down_low=w_down[:cut],
        gains=own_gains([attn_gain, mlp_gain])[:, :, None],
        order=order,
        layer_in=layer_in,
        out_grad=out_grad,
        w_qkv=jnp.concatenate([w_query, w_key, w_value], axis=1),
        w_gate=w_gate,
        w_up=w_up,
    )
    first_at, where_at = positions(seq_lengths, group_rows)
    v.update(first_at=first_at, tables=rope_tables(where_at[0], HD))
    v = fence(v)

    q = (v.w_qkv.astype(F32) * v.gains[0]).astype(BF16)
    q = jnp.concatenate([q] + [zed(q, a) for a in (2, 1, 3)], axis=0)
    oy = why(v.o)
    g = (v.w_gate.astype(F32) * v.gains[1]).astype(BF16)
    u = (v.w_up.astype(F32) * v.gains[1]).astype(BF16)
    dq = jnp.concatenate(v.out.down_high, axis=1)
    v.update(q=q, oy=oy, g=g, u=u, dq=dq)
    v = fence(v)

    g = [v.g, zed(v.g, 2), zed(v.g, 1)]
    qy = why(v.q)
    w_output_all = jnp.concatenate([v.out.o, v.out.oy], axis=1)
    rows_one = unit_rows(v.order, input_rows)
    v.update(g=g, qy=qy, w_output_all=w_output_all, rows_one=rows_one)
    v = fence(v)

    grad_gathered = gather_rows(v.out_grad)
    g = v.g + [zed(v.g[1], 1)]
    u = [v.u, zed(v.u, 1)]
    gy = [why(v.g[0]), why(v.g[1])]
    qkv = project_rotate(v.rows_one, v.q, v.qy, *v.tables)
    attended, logs = attention(qkv, v.first_at, pairs)
    partial = project(attended, v.w_output_all).astype(BF16)
    v.update(g=g, gy=gy, u=u, qkv=qkv, attended=attended, logs=logs, partial=partial)
    v = fence(v)

    came = sum_rows(v.out.partial)
    u = [v.u[0], zed(v.u[0], 2), v.u[1]]
    gy = v.gy + [why(v.g[2]), why(v.g[3])]
    grad_rows = held_rows(v.order, grad_gathered)
    v.update(u=u, gy=gy, grad_rows=grad_rows)
    v = fence(v)

    u = v.u + [zed(v.u[1], 1)]
    low = v.out.down_low
    low = [low, zed(low, 2), zed(low, 1)]
    uy = [why(v.u[0]), why(v.u[1])]
    w_gate_all = jnp.concatenate(v.out.g + v.out.gy, axis=0)
    mid, unit_two, inverse_two = middle(v.order, v.layer_in, came)
    v.update(u=u, uy=uy, low=low, w_gate_all=w_gate_all)
    v.update(mid=mid, unit_two=unit_two, inverse_two=inverse_two)
    v = fence(v)

    rows_two = gather_rows(v.out.unit_two)
    low = [jnp.concatenate(v.low, axis=1), zed(v.low[1], 1)]
    dq = [v.dq, zed(v.dq, 2)]
    w_ups = [jnp.concatenate(v.u + v.uy, axis=0), why(v.u[2]), why(v.u[3])]
    v.update(low=low, dq=dq, w_ups=w_ups)
    v = fence(v)

    low = v.low + [why(v.low[0]), why(v.low[1])]
    dq = v.dq + [zed(v.dq[0], 1), zed(v.dq[1], 1)]
    gate_pre = gate_part(rows_two, [v.w_gate_all])
    hidden, factors = up_part(rows_two, v.w_ups, gate_pre)
    low_away = part(hidden[:, :cut], v.grad_rows, 1, 4, 8).astype(BF16)
    high_away = both(hidden[:, cut:], v.grad_rows, 2, 4)
    v.update(dq=dq, low=low, rows_two=rows_two, hidden=hidden)
    v.update(factors=factors, low_away=low_away, high_away=high_away)
    v = fence(v)

    first = why(v.low_away)
    high_near = zed(v.high_away, 1)
    grad_gate, grad_up = hidden_back(v.grad_rows, v.low, v.dq, v.out.factors)
    partial = feed_back(grad_gate, grad_up, v.w_gate_all, v.w_ups)
    gate_away = part(v.rows_two, grad_gate, 0, 6, 8).astype(BF16)
    v.update(first=first, high_near=high_near, gate_away=gate_away)
    v.update(grad_gate=grad_gate, grad_up=grad_up)
    v.update(partial=partial)
    v = fence(v)

    came = sum_rows(v.out.partial)
    hidden_low, hidden_high = v.hidden[:, :cut], v.hidden[:, cut:]
    half = v.first.shape[1] // 2
    low_near = part(hidden_low, v.grad_rows, 1, 2, 4) + v.first[:, half:].astype(F32)
    low_near = zed(low_near.astype(BF16), 1)
    step = half // 2
    ones = [slice(b * half + step, b * half + 2 * step) for b in (0, 1)]
    high_one = [
        (
            part(hidden_high, v.grad_rows, 1, 4 * b + 1, 4 * b + 2)
            + v.high_near[:, at].astype(F32)
        ).astype(BF16)
        for b, at in enumerate(ones)
    ]
    high_far = zed(jnp.concatenate(high_one, axis=1), 2)
    gate_first = why(v.gate_away)
    gate_away = part(v.rows_two, v.grad_gate, 0, 4, 6).astype(BF16)
    gate_kept = part(v.rows_two, v.grad_gate, 0, 0, 4).astype(BF16)
    up_away = part(v.rows_two, v.grad_up, 0, 6, 8).astype(BF16)
    v.update(low_near=low_near, high_far=high_far, gate_first=gate_first, gate_away=gate_away)
    low_kept = part(hidden_low, v.grad_rows, 1, 0, 2).astype(BF16)
    v.update(gate_kept=gate_kept, up_away=up_away, low_kept=low_kept)
    v = fence(v)

    low_sums = v.low_kept.astype(F32) + v.first[:, :half].astype(F32) + v.low_near.astype(F32)
    low_far = zed(low_sums[:, step:].astype(BF16), 2)
    three = zed(joined(v.gate_kept, 0, 3, 4, (v.gate_first, 1, 2)).astype(BF16), 1)
    gate_second = why(v.gate_away)
    grad_mid, grad_mid_low = middle_back(v.order, v.out_grad, v.mid, v.inverse_two, came)
    zeros = [slice(b * half, b * half + step) for b in (0, 1)]
    high_own = [
        part(v.hidden[:, cut:], v.grad_rows, 1, 4 * b, 4 * b + 1)
        + v.high_near[:, at].astype(F32)
        + v.high_far[:, b * step : (b + 1) * step].astype(F32)
        for b, at in enumerate(zeros)
    ]
    high_over = high_own[1].astype(BF16)
    up_away = [v.up_away, part(v.rows_two, v.grad_up, 0, 4, 6).astype(BF16)]
    up_kept = part(v.rows_two, v.grad_up, 0, 0, 4).astype(BF16)
    v.update(low_far=low_far, three=three, gate_second=gate_second, grad_mid=grad_mid)
    v.update(grad_mid_low=grad_mid_low, high_own=high_own[0], high_over=high_over)
    v.update(up_away=up_away, up_kept=up_kept)
    v = fence(v)

    grad_mid_rows = gather_rows(v.out.grad_mid_low)
    far = joined(v.gate_kept, 0, 1, 2, (v.gate_second, 1, 2), (v.three, 0, 1)).astype(BF16)
    near = joined(v.gate_kept, 0, 2, 3, (v.gate_first, 0, 2)).astype(BF16)
    gate_came = [zed(far, 2), zed(near, 1)]
    up_first = why(v.up_away[0])
    low_terms = [term[:, :step] for term in (v.low_kept, v.first, v.low_near)]
    low_sh = summed(v.low_far.astype(F32), low_terms)
    high = v.out.dq
    high = [w[:, :step] for w in high] + [w[:, step:] for w in high]
    high_all = jnp.concatenate(high, axis=1)
    low_all = jnp.concatenate(v.out.low, axis=1)
    partial = project(v.hidden[:, :cut], low_all)
    output_part = (partial + project(v.hidden[:, cut:], high_all)).astype(BF16)
    v.update(gate_came=gate_came, up_first=up_first, low_sh=low_sh, output_part=output_part)
    v = fence(v)

    three = zed(joined(v.up_kept, 0, 3, 4, (v.up_first, 1, 2)).astype(BF16), 1)
    up_second = why(v.up_away[1])
    grad_attended = project_back(grad_mid_rows, v.w_output_all).astype(BF16)
    grad_query, grad_kv = attention_back(
        v.qkv, v.first_at, v.logs, grad_attended, *v.tables, pairs
    )
    grad_qkv = jnp.concatenate([grad_query, grad_kv], axis=1)
    qkv_away = part(v.rows_one, grad_qkv, 0, 4, 8).astype(BF16)
    came_out = sum_rows(v.output_part)
    v.update(three=three, up_second=up_second, grad_qkv=grad_qkv, grad_mid_rows=grad_mid_rows)
    v.update(qkv_away=qkv_away)
    v = fence(v)

    far = joined(v.up_kept, 0, 1, 2, (v.up_second, 1, 2), (v.three, 0, 1)).astype(BF16)
    near = joined(v.up_kept, 0, 2, 3, (v.up_first, 0, 2)).astype(BF16)
    up_came = [zed(far, 2), zed(near, 1)]
    first = why(v.out.qkv_away)
    w_qkv_all = jnp.concatenate([v.q, v.qy], axis=0)
    partial = project_back(v.grad_qkv, w_qkv_all).astype(BF16)
    qkv_kept = part(v.rows_one, v.grad_qkv, 0, 0, 4).astype(BF16)
    output_away = part(v.attended, v.grad_mid_rows, 1, 4, 8).astype(BF16)
    grad_gate_sh = summed(joined(v.gate_kept, 0, 0, 1, (v.gate_second, 0, 2)), v.gate_came)
    v.update(up_came=up_came, first=first, qkv_kept=qkv_kept, output_away=output_away)
    v.update(partial=partial, grad_gate_sh=grad_gate_sh)
    v = fence(v)

    came = sum_rows(v.out.partial)
    pieces = [
        zed(joined(v.qkv_kept, 0, i, i + 1, (v.first, i, 4)).astype(BF16), a)
        for i, a in ((1, 2), (2, 1), (3, 3))
    ]
    over = why(v.output_away)
    high_over = why(v.high_over)
    gain_one, gain_two = v.gains[0], v.gains[1]
    grad_gate_sh = v.grad_gate_sh
    grad_up_sh = summed(joined(v.up_kept, 0, 0, 1, (v.up_second, 0, 2)), v.up_came)
    gain_two_term = jnp.sum(
        grad_gate_sh * v.w_gate.astype(F32) + grad_up_sh * v.w_up.astype(F32), axis=1
    )
    output_kept = part(v.attended, v.grad_mid_rows, 1, 0, 4).astype(BF16)
    layer_out = layer_end(v.order, v.mid, came_out)
    v.update(pieces=pieces, over=over, high_over=high_over, gain_two_term=gain_two_term)
    v.update(grad_gate_sh=grad_gate_sh * gain_two, grad_up_sh=grad_up_sh * gain_two)
    v.update(output_kept=output_kept, layer_out=layer_out)
    v = fence(v)

    pieces = [
        zed(joined(v.output_kept, 1, i, i + 1, (v.over, i, 4)).astype(BF16), a)
        for i, a in ((1, 2), (2, 1), (3, 3))
    ]
    grad_down_sh = jnp.concatenate([v.low_sh, v.high_own + v.high_over.astype(F32)], axis=0)
    in_grad = input_back(v.order, v.layer_in, v.grad_mid, came)
    in_grad, came_pieces, over = fence((in_grad, v.pieces, v.over))
    grad_qkv_sh = summed(joined(v.qkv_kept, 0, 0, 1, (v.first, 0, 4)), came_pieces)
    gain_one_term = jnp.sum(grad_qkv_sh * v.w_qkv.astype(F32), axis=1)
    gain_one_grad, gain_two_grad = share_gains([gain_one_term, v.gain_two_term])
    grad_qkv_sh = grad_qkv_sh * v.gains[0]
    over, gain_one_grad, gain_two_grad = fence((over, gain_one_grad, gain_two_grad))
    return (
        v.layer_out,
        in_grad,
        gain_one_grad,
        grad_qkv_sh[:, :query_width],
        grad_qkv_sh[:, query_width : query_width + key_width],
        grad_qkv_sh[:, query_width + key_width :],
        summed(joined(v.output_kept, 1, 0, 1, (over, 0, 4)), pieces),
        gain_two_grad,
        v.grad_gate_sh,
        v.grad_up_sh,
        grad_down_sh,
    )


def direct(
    layer_in,
    seq_lengths,
    attn_gain,
    w_query,
    w_key,
    w_value,
    w_output,
    mlp_gain,
    w_gate,
    w_up,
    w_down,
    out_grad,
):
    def gather(shard, axis):
        return lax.all_gather(shard, "fsdp", axis=axis, tiled=True)

    def scatter(left, right, axis):
        total = outer(left, right).astype(BF16)
        return lax.psum_scatter(total, "fsdp", scatter_dimension=axis, tiled=True).astype(F32)

    group_rows = layer_in.shape[0] * lax.axis_size("tp")
    query_width, key_width = w_query.shape[1], w_key.shape[1]
    pairs = query_width // (2 * HD)
    order = jnp.arange(COLUMN_BLOCKS, dtype=jnp.int32)
    gain_one, gain_two = [
        lax.all_gather(gain, "tp", axis=0, tiled=True)[:, None] for gain in (attn_gain, mlp_gain)
    ]
    w_qkv = jnp.concatenate([w_query, w_key, w_value], axis=1)
    w_output_all = gather(w_output, 1)
    w_qkv_all = gather((w_qkv.astype(F32) * gain_one).astype(BF16), 0)
    w_gate_all = gather((w_gate.astype(F32) * gain_two).astype(BF16), 0)
    w_up_all = gather((w_up.astype(F32) * gain_two).astype(BF16), 0)
    w_down_all = gather(w_down, 1)
    first_at, where_at = positions(seq_lengths, group_rows)
    cosine, sine = rope_tables(where_at[0], HD)
    rows_one = unit_rows(order, gather_rows(layer_in))
    qkv = project_rotate(rows_one, *jnp.split(w_qkv_all, 2), cosine, sine)
    grad_rows = held_rows(order, gather_rows(out_grad))
    attended, logs = attention(qkv, first_at, pairs)
    came = sum_rows(project(attended, w_output_all).astype(BF16))
    mid, unit_two, inverse_two = middle(order, layer_in, came)
    rows_two = gather_rows(unit_two)
    gate_pre = gate_part(rows_two, [w_gate_all])
    hidden, factors = up_part(rows_two, [w_up_all], gate_pre)
    grad_down_sh = scatter(hidden, grad_rows, 1)
    came = sum_rows(project(hidden, w_down_all).astype(BF16))
    layer_out = layer_end(order, mid, came)
    grad_gate, grad_up = hidden_back(grad_rows, [w_down_all], [], factors)
    came = sum_rows(feed_back(grad_gate, grad_up, w_gate_all, [w_up_all]))
    grad_gate_sh = scatter(rows_two, grad_gate, 0)
    grad_up_sh = scatter(rows_two, grad_up, 0)
    grad_mid, grad_mid_low = middle_back(order, out_grad, mid, inverse_two, came)
    grad_mid_rows = gather_rows(grad_mid_low)
    grad_attended = project_back(grad_mid_rows, w_output_all).astype(BF16)
    grad_output_sh = scatter(attended, grad_mid_rows, 1)
    grad_query, grad_kv = attention_back(
        qkv, first_at, logs, grad_attended, cosine, sine, pairs
    )
    grad_qkv = jnp.concatenate([grad_query, grad_kv], axis=1)
    came = sum_rows(project_back(grad_qkv, w_qkv_all).astype(BF16))
    in_grad = input_back(order, layer_in, grad_mid, came)
    grad_qkv_sh = scatter(rows_one, grad_qkv, 0)
    gain_one_term = jnp.sum(grad_qkv_sh * w_qkv.astype(F32), axis=1)
    gain_two_term = jnp.sum(
        grad_gate_sh * w_gate.astype(F32) + grad_up_sh * w_up.astype(F32), axis=1
    )
    gain_one_grad, gain_two_grad = [
        lax.psum_scatter(term, "tp", scatter_dimension=0, tiled=True)
        for term in (gain_one_term, gain_two_term)
    ]
    grad_qkv_sh = grad_qkv_sh * gain_one
    return (
        layer_out,
        in_grad,
        gain_one_grad,
        grad_qkv_sh[:, :query_width],
        grad_qkv_sh[:, query_width : query_width + key_width],
        grad_qkv_sh[:, query_width + key_width :],
        grad_output_sh,
        gain_two_grad,
        grad_gate_sh * gain_two,
        grad_up_sh * gain_two,
        grad_down_sh,
    )


def solution(mesh):
    placed = (
        P(("fsdp", "tp"), None),
        P("fsdp", None),
        P(("fsdp", "tp")),
        P("fsdp", "tp"),
        P("fsdp", "tp"),
        P("fsdp", "tp"),
        P("tp", "fsdp"),
        P(("fsdp", "tp")),
        P("fsdp", "tp"),
        P("fsdp", "tp"),
        P("tp", "fsdp"),
        P(("fsdp", "tp"), None),
    )
    paired = (mesh.shape["fsdp"], mesh.shape["tp"]) == (8, 4)
    return jax.shard_map(
        scheduled if paired else direct,
        mesh=mesh,
        in_specs=placed,
        out_specs=(
            P(("fsdp", "tp"), None),
            P(("fsdp", "tp"), None),
            P(("fsdp", "tp")),
            P("fsdp", "tp"),
            P("fsdp", "tp"),
            P("fsdp", "tp"),
            P("tp", "fsdp"),
            P(("fsdp", "tp")),
            P("fsdp", "tp"),
            P("fsdp", "tp"),
            P("tp", "fsdp"),
        ),
        check_vma=False,
    )
```

```python
import math

import jax
import jax.numpy as jnp
from jax import lax
from jax.experimental import pallas as pl
from jax.experimental.pallas import tpu as pltpu
from jax.sharding import PartitionSpec as P

HD = 64
MAXLEN = 512
EPSILON = 1e-05
ROPE_BASE = 10000.0
MASKED_OUT = -1e30
TILE = 512
COLUMN_BLOCKS = 8
ROW_BLOCKS = 4
VMEM = 56 * 1024 * 1024
F32 = jnp.float32
BF16 = jnp.bfloat16


def positions(lengths, count):
    starts = jnp.cumsum(lengths, axis=-1) - lengths
    indices = jnp.arange(count, dtype=jnp.int32)
    inside = (indices[None, :, None] >= starts[:, None, :]) & (
        indices[None, :, None] < (starts + lengths)[:, None, :]
    )
    first_at = jnp.sum(jnp.where(inside, starts[:, None, :], 0), axis=-1)
    return first_at, indices[None, :] - first_at


def rope_tables(where_at, width):
    half_width = width // 2
    inverse_freq = ROPE_BASE ** (-(jnp.arange(half_width, dtype=F32) * 2.0 / width))
    angles = where_at.astype(F32)[:, None] * inverse_freq[None, :]
    cosine, sine = jnp.cos(angles), jnp.sin(angles)
    return jnp.concatenate([cosine] * 4, axis=1), jnp.concatenate([sine] * 4, axis=1)


def project(left, weight):
    return jnp.dot(left, weight, preferred_element_type=F32)


def project_back(grad, weight):
    return jnp.einsum("tc,dc->td", grad, weight, preferred_element_type=F32)


def outer(left, right):
    return jnp.einsum("ta,tb->ab", left, right, preferred_element_type=F32)


def call(body, outs, operands, flops=0, nbytes=0, **more):
    return pl.pallas_call(
        body,
        out_shape=outs,
        compiler_params=pltpu.CompilerParams(vmem_limit_bytes=VMEM),
        cost_estimate=pl.CostEstimate(flops=1, bytes_accessed=1, transcendentals=0),
        **more,
    )(*operands)


def whole(count):
    return [pl.BlockSpec(memory_space=pltpu.VMEM)] * count


SCALARS = pl.BlockSpec(memory_space=pltpu.SMEM)


def spans(order, width):
    step = width // COLUMN_BLOCKS
    return [
        (slice(j * step, (j + 1) * step), pl.ds(pl.multiple_of(order[j] * step, step), step))
        for j in range(COLUMN_BLOCKS)
    ]


def turned(values, lanes):
    width = values.shape[-1]
    first = (lanes % HD) < HD // 2
    return jnp.where(
        first, -pltpu.roll(values, width - HD // 2, 1), pltpu.roll(values, HD // 2, 1)
    )


def unit_rows(order, gathered):
    rows, width = gathered.shape
    count = rows // ROW_BLOCKS

    def body(order, x, out):
        values = x[...].astype(F32)
        inverse = lax.rsqrt(jnp.mean(values * values, axis=-1, keepdims=True) + EPSILON)
        for held, true in spans(order, width):
            out[:, held] = (x[:, true].astype(F32) * inverse).astype(BF16)

    spec = pl.BlockSpec((count, width), lambda i: (i, 0))
    return call(
        body,
        jax.ShapeDtypeStruct((rows, width), BF16),
        (order, gathered),
        nbytes=4 * rows * width,
        grid=(ROW_BLOCKS,),
        in_specs=[SCALARS, spec],
        out_specs=spec,
    )


def project_rotate(rows_one, weights_low, weights_high, cosine, sine):
    rows, width = rows_one.shape
    count = rows // ROW_BLOCKS
    half, total = weights_low.shape
    kv = 2 * HD

    def body(x, low, high, c, s, out):
        product = project(x[:, :half], low[...]) + project(x[:, half:], high[...])
        cos, sin = c[...], s[...]
        lanes = lax.broadcasted_iota(jnp.int32, cos.shape, 1)
        for at in range(0, total, 128):
            part = product[:, at : at + 128]
            if at + 128 > total - kv:
                co, si = jnp.where(lanes < HD, cos, 1.0), jnp.where(lanes < HD, sin, 0.0)
            else:
                co, si = cos, sin
            out[:, at : at + 128] = (part * co + turned(part, lanes) * si).astype(BF16)

    def tiles(columns):
        return pl.BlockSpec((count, columns), lambda i: (i, 0))

    weight = pl.BlockSpec((half, total), lambda i: (0, 0), pipeline_mode=pl.Buffered(1))
    return call(
        body,
        jax.ShapeDtypeStruct((rows, total), BF16),
        (rows_one, weights_low, weights_high, cosine, sine),
        flops=2 * rows * width * total,
        nbytes=2 * (rows * width + width * total),
        grid=(ROW_BLOCKS,),
        in_specs=[tiles(width), weight, weight, tiles(2 * HD), tiles(2 * HD)],
        out_specs=tiles(total),
    )


def window(i, span):
    return max(0, i * span - MAXLEN), (i + 1) * span


def shown(first, i, span):
    low, high = window(i, span)
    keys = low + lax.broadcasted_iota(jnp.int32, (high - low, span), 0)
    rows = i * span + lax.broadcasted_iota(jnp.int32, (high - low, span), 1)
    return (keys <= rows) & (keys >= first[:, i * span : (i + 1) * span])


def dot_nt(left, right):
    return lax.dot_general(left, right, (((1,), (1,)), ((), ())), preferred_element_type=F32)


def dot_tn(left, right):
    return lax.dot_general(left, right, (((0,), (0,)), ((), ())), preferred_element_type=F32)


def stacked(values, heads):
    return jnp.concatenate([values[:, h * HD : (h + 1) * HD] for h in range(heads)], axis=0)


def side_by_side(values, span, heads):
    parts = [values[:, h * span : (h + 1) * span] for h in range(heads)]
    return [jnp.concatenate(parts[h : h + 2], axis=0).T for h in range(0, heads, 2)]


def attention(qkv, first, pairs):
    rows = qkv.shape[0]
    span = rows // ROW_BLOCKS
    heads = min(4, 2 * pairs)
    width = heads * HD

    def body(q, kv, first, out, logs):
        for i in range(rows // span):
            low, high = window(i, span)
            at = slice(i * span, (i + 1) * span)
            allowed = jnp.concatenate([shown(first, i, span)] * heads, axis=1)
            keys, values = kv[low:high, :HD], kv[low:high, HD:]
            queries = stacked((q[at, :] * 0.125).astype(BF16), heads)
            scores = jnp.where(allowed, dot_nt(keys, queries), MASKED_OUT)
            top = jnp.max(scores, axis=0, keepdims=True)
            shares = jnp.exp(scores - top)
            total = jnp.sum(shares, axis=0, keepdims=True)
            mixed = dot_tn(values, shares.astype(BF16)) / total
            log = top + jnp.log(total)
            for h in range(heads):
                logs[h // 2, h % 2 : h % 2 + 1, at] = log[:, h * span : (h + 1) * span]
            for p, pair in enumerate(side_by_side(mixed, span, heads)):
                out[at, p * 2 * HD : (p + 1) * 2 * HD] = pair.astype(BF16)

    return call(
        body,
        (
            jax.ShapeDtypeStruct((rows, pairs * 2 * HD), BF16),
            jax.ShapeDtypeStruct((pairs, 2, rows), F32),
        ),
        (qkv, qkv, first),
        grid=(2 * pairs // heads,),
        in_specs=[
            pl.BlockSpec((rows, width), lambda p: (0, p)),
            pl.BlockSpec((rows, 2 * HD), lambda p: (0, pairs)),
            pl.BlockSpec((1, rows), lambda p: (0, 0)),
        ],
        out_specs=(
            pl.BlockSpec((rows, width), lambda p: (0, p)),
            pl.BlockSpec((heads // 2, 2, rows), lambda p: (p, 0, 0)),
        ),
    )


def attention_back(qkv, first, logs, grads, cosine, sine, pairs):
    rows = qkv.shape[0]
    span = rows // (2 * ROW_BLOCKS)
    heads = min(4, 2 * pairs)
    width = heads * HD

    def body(q, kv, first, logs, grad, c, s, dq, dkv, total):
        @pl.when(pl.program_id(0) == 0)
        def _():
            total[...] = jnp.zeros_like(total)

        lanes = lax.broadcasted_iota(jnp.int32, (span, 2 * HD), 1)
        for i in range(rows // span):
            low, high = window(i, span)
            at = slice(i * span, (i + 1) * span)
            allowed = jnp.concatenate([shown(first, i, span)] * heads, axis=1)
            keys, values = kv[low:high, :HD], kv[low:high, HD:]
            queries = stacked((q[at, :] * 0.125).astype(BF16), heads)
            came = stacked(grad[at, :], heads)
            log = jnp.concatenate([logs[h // 2, h % 2 : h % 2 + 1, at] for h in range(heads)], axis=1)
            shares = jnp.where(allowed, jnp.exp(dot_nt(keys, queries) - log), 0.0)
            change = dot_nt(values, came)
            inner = jnp.sum(shares * change, axis=0, keepdims=True)
            score_grads = (shares * (change - inner)).astype(BF16)
            value_part = jnp.dot(shares.astype(BF16), came, preferred_element_type=F32)
            key_part = jnp.dot(score_grads, queries, preferred_element_type=F32)
            total[low:high, :] += jnp.concatenate([key_part, value_part], axis=1)
            query_grads = dot_tn(keys, score_grads) * 0.125
            for p, pair in enumerate(side_by_side(query_grads, span, heads)):
                dq[at, p * 2 * HD : (p + 1) * 2 * HD] = (
                    pair * c[at, :] - turned(pair * s[at, :], lanes)
                ).astype(BF16)

        @pl.when(pl.program_id(0) == 2 * pairs // heads - 1)
        def _():
            for i in range(rows // span):
                at = slice(i * span, (i + 1) * span)
                cos = jnp.where(lanes < HD, c[at, :], 1.0)
                sin = jnp.where(lanes < HD, s[at, :], 0.0)
                part = total[at, :]
                dkv[at, :] = (part * cos - turned(part * sin, lanes)).astype(BF16)

    return call(
        body,
        (
            jax.ShapeDtypeStruct((rows, pairs * 2 * HD), BF16),
            jax.ShapeDtypeStruct((rows, 2 * HD), BF16),
        ),
        (qkv, qkv, first, logs, grads, cosine, sine),
        grid=(2 * pairs // heads,),
        in_specs=[
            pl.BlockSpec((rows, width), lambda p: (0, p)),
            pl.BlockSpec((rows, 2 * HD), lambda p: (0, pairs)),
            pl.BlockSpec((1, rows), lambda p: (0, 0)),
            pl.BlockSpec((heads // 2, 2, rows), lambda p: (p, 0, 0)),
            pl.BlockSpec((rows, width), lambda p: (0, p)),
            pl.BlockSpec((rows, 2 * HD), lambda p: (0, 0)),
            pl.BlockSpec((rows, 2 * HD), lambda p: (0, 0)),
        ],
        out_specs=(
            pl.BlockSpec((rows, width), lambda p: (0, p)),
            pl.BlockSpec((rows, 2 * HD), lambda p: (0, 0)),
        ),
        scratch_shapes=[pltpu.VMEM((rows, 2 * HD), F32)],
    )


def row_kernel(multiply, left, weights, width, extra, outs, finish, tile=TILE):
    rows = left[0].shape[0]
    tile = min(tile, rows)
    many = len(left), len(left) + len(weights), len(left) + len(weights) + len(extra)

    def body(*refs):
        product = multiply(refs[: many[0]], refs[many[0] : many[1]])
        finish(product, refs[many[1] : many[2]], refs[many[2] :])

    def tiles(columns):
        return pl.BlockSpec((tile, columns), lambda i: (i, 0))

    widths = [width] * len(outs)
    inner = sum(weight.size for weight in weights)
    return pl.pallas_call(
        body,
        out_shape=tuple(
            jax.ShapeDtypeStruct((rows, columns), kind)
            for columns, kind in zip(widths, outs, strict=True)
        ),
        grid=(rows // tile,),
        in_specs=[tiles(v.shape[1]) for v in left]
        + [
            pl.BlockSpec(v.shape, lambda i: (0, 0), pipeline_mode=pl.Buffered(1)) for v in weights
        ]
        + [tiles(v.shape[1]) for v in extra],
        out_specs=tuple(tiles(columns) for columns in widths),
        compiler_params=pltpu.CompilerParams(vmem_limit_bytes=VMEM),
        cost_estimate=pl.CostEstimate(flops=1, bytes_accessed=1, transcendentals=0),
    )(*left, *weights, *extra)


def down_rows(left, weights):
    (x,) = left
    total, at = None, 0
    for w in weights:
        term = jnp.dot(x[:, at : at + w.shape[0]], w[...], preferred_element_type=F32)
        total, at = term if total is None else total + term, at + w.shape[0]
    return total


def hidden_part(rows_two, w_gate, w_ups):
    def multiply(left, weights):
        gate = jnp.dot(left[0][...], weights[0][...], preferred_element_type=F32)
        return gate, down_rows(left, weights[1:])

    def finish(products, extra, outs):
        gate, up = products
        sigmoid = 1.0 / (1.0 + jnp.exp(-gate))
        silu = gate * sigmoid
        outs[0][...] = (silu * up).astype(BF16)
        outs[1][...] = (up * sigmoid * (1.0 + gate * (1.0 - sigmoid))).astype(BF16)
        outs[2][...] = silu.astype(BF16)

    hidden, *factors = row_kernel(
        multiply, [rows_two], [w_gate, *w_ups], w_gate.shape[1], [], [BF16] * 3, finish, 256
    )
    return hidden, factors


def hidden_back(grad_rows, lows, highs, factors):
    def multiply(left, weights):
        (x,) = left
        products, total, at = [], None, 0
        for w in weights[: len(lows)]:
            term = dot_nt(x[:, at : at + w.shape[1]], w[...])
            total, at = term if total is None else total + term, at + w.shape[1]
        products.append(total)
        total = None
        for a, w in enumerate(weights[len(lows) :]):
            step = w.shape[1] // 2
            for place, sub in ((a, 0), (4 + a, 1)):
                term = dot_nt(
                    x[:, place * step : (place + 1) * step], w[:, sub * step : (sub + 1) * step]
                )
                total = term if total is None else total + term
        if highs:
            products.append(total)
        return products

    def finish(products, extra, outs):
        at = 0
        for product in products:
            columns = slice(at, at + product.shape[1])
            for factor, out in zip(extra, outs, strict=True):
                out[:, columns] = (product * factor[:, columns].astype(F32)).astype(BF16)
            at = columns.stop

    width = factors[0].shape[1]
    return row_kernel(
        multiply, [grad_rows], [*lows, *highs], width, factors, [BF16] * 2, finish, 256
    )


def feed_back(grad_gate, grad_up, w_gate, w_ups):
    def multiply(left, weights):
        products, row = [], 0
        for w_up in weights[1:]:
            rows = slice(row, row + w_up.shape[0])
            products.append(dot_nt(left[0][...], weights[0][rows, :]) + dot_nt(left[1][...], w_up[...]))
            row = rows.stop
        return products

    def finish(products, extra, outs):
        at = 0
        for product in products:
            outs[0][:, at : at + product.shape[1]] = product.astype(BF16)
            at += product.shape[1]

    return row_kernel(
        multiply,
        [grad_gate, grad_up],
        [w_gate, *w_ups],
        w_gate.shape[0],
        [],
        [BF16],
        finish,
        256,
    )[0]


def held_rows(order, gathered):
    rows, width = gathered.shape
    count = rows // ROW_BLOCKS

    def body(order, x, out):
        for held, true in spans(order, width):
            out[:, held] = x[:, true]

    spec = pl.BlockSpec((count, width), lambda i: (i, 0))
    return call(
        body,
        jax.ShapeDtypeStruct((rows, width), BF16),
        (order, gathered),
        nbytes=4 * rows * width,
        grid=(ROW_BLOCKS,),
        in_specs=[SCALARS, spec],
        out_specs=spec,
    )


def middle(order, layer_in, came):
    count, width = layer_in.shape

    def body(order, x, came, mid, unit, inverse):
        for held, true in spans(order, width):
            mid[:, held] = x[:, true].astype(F32) + came[:, held].astype(F32)
        values = mid[...]
        scale = lax.rsqrt(jnp.mean(values * values, axis=-1, keepdims=True) + EPSILON)
        inverse[...] = scale
        unit[...] = (values * scale).astype(BF16)

    return call(
        body,
        (
            jax.ShapeDtypeStruct((count, width), F32),
            jax.ShapeDtypeStruct((count, width), BF16),
            jax.ShapeDtypeStruct((count, 1), F32),
        ),
        (order, layer_in, came),
        nbytes=20 * count * width,
        in_specs=[SCALARS] + whole(2),
        out_specs=tuple(whole(3)),
    )


def layer_end(order, mid, came):
    count, width = mid.shape

    def body(order, mid, came, out):
        for held, true in spans(order, width):
            total = mid[:, held] + came[:, held].astype(F32)
            out[:, true] = total.astype(BF16)

    return call(
        body,
        jax.ShapeDtypeStruct((count, width), BF16),
        (order, mid, came),
        nbytes=14 * count * width,
        in_specs=[SCALARS] + whole(2),
        out_specs=whole(1)[0],
    )


def middle_back(order, out_grad, mid, inverse, came):
    count, width = mid.shape

    def body(order, dy, mid, inverse, came, grad, low):
        scale = inverse[...]
        grad_unit = came[...].astype(F32)
        unit = mid[...] * scale
        inner = jnp.mean(grad_unit * unit, axis=-1, keepdims=True)
        grad[...] = scale * (grad_unit - unit * inner)
        for held, true in spans(order, width):
            total = grad[:, held] + dy[:, true].astype(F32)
            grad[:, held] = total
            low[:, held] = total.astype(BF16)

    return call(
        body,
        (
            jax.ShapeDtypeStruct((count, width), F32),
            jax.ShapeDtypeStruct((count, width), BF16),
        ),
        (order, out_grad, mid, inverse, came),
        nbytes=20 * count * width,
        in_specs=[SCALARS] + whole(4),
        out_specs=tuple(whole(2)),
    )


def input_back(order, layer_in, grad_mid, came):
    count, width = grad_mid.shape

    def body(order, x, grad_mid, came, out, unit):
        values = x[...].astype(F32)
        scale = lax.rsqrt(jnp.mean(values * values, axis=-1, keepdims=True) + EPSILON)
        for held, true in spans(order, width):
            unit[:, held] = x[:, true].astype(F32) * scale
        grad_unit = came[...].astype(F32)
        inner = jnp.mean(grad_unit * unit[...], axis=-1, keepdims=True)
        unit[...] = grad_mid[...] + scale * (grad_unit - unit[...] * inner)
        for held, true in spans(order, width):
            out[:, true] = unit[:, held]

    return call(
        body,
        jax.ShapeDtypeStruct((count, width), F32),
        (order, layer_in, grad_mid, came),
        nbytes=16 * count * width,
        in_specs=[SCALARS] + whole(3),
        out_specs=whole(1)[0],
        scratch_shapes=[pltpu.VMEM((count, width), F32)],
    )


def gather_rows(rows):
    return lax.all_gather(rows, "tp", axis=0, tiled=True)


def sum_rows(partial):
    return lax.psum_scatter(partial, "tp", scatter_dimension=0, tiled=True)


class Taker:
    def __init__(self, held):
        self.held = held

    def __getattr__(self, name):
        return self.held.pop(name)


class Held(dict):
    __getattr__ = dict.__getitem__

    @property
    def out(self):
        return Taker(self)


def fence(state):
    if isinstance(state, Held):
        return Held(lax.optimization_barrier(dict(state)))
    return lax.optimization_barrier(state)


def zed(values, step):
    return lax.ppermute(values, "fsdp", [(i, i ^ (2 * step)) for i in range(8)])


def why(values):
    return lax.ppermute(values, "fsdp", [(i, i ^ 1) for i in range(8)])


def teep(values, mask):
    return lax.ppermute(values, "tp", [(i, i ^ mask) for i in range(4)])


def own_gains(gains):
    t = lax.axis_index("tp")
    own = jnp.stack(gains)
    near = jnp.stack([own, teep(own, 1)], axis=1)
    near = jnp.where((t & 1) == 1, near[:, ::-1], near)
    both = jnp.stack([near, teep(near, 2)], axis=1)
    both = jnp.where((t >> 1) == 1, both[:, ::-1], both)
    return both.reshape(len(gains), -1)


def share_gains(terms):
    t = lax.axis_index("tp")
    both = jnp.stack(terms).reshape(len(terms), 2, 2, -1)
    both = jnp.where((t >> 1) == 1, both[:, ::-1], both)
    both = both[:, 0] + teep(both[:, 1], 2)
    both = jnp.where((t & 1) == 1, both[:, ::-1], both)
    both = both[:, 0] + teep(both[:, 1], 1)
    return [both[i] for i in range(len(terms))]


def part(left, right, axis, first, last):
    step = (left if axis == 0 else right).shape[1] // COLUMN_BLOCKS
    at = slice(first * step, last * step)
    if axis == 0:
        return outer(left[:, at], right)
    return outer(left, right[:, at])


def both(left, right, first, last):
    parts = [part(left, right, 1, b + first, b + last).astype(BF16) for b in (0, 4)]
    return jnp.concatenate(parts, axis=1)


def joined(values, axis, first, last, *came):
    step = values.shape[axis] // 4
    total = lax.slice_in_dim(values, first * step, last * step, axis=axis).astype(F32)
    for array, at, count in came:
        size = array.shape[axis] // count
        piece = lax.slice_in_dim(array, at * size, (at + last - first) * size, axis=axis)
        total = total + piece.astype(F32)
    return total


def summed(total, came):
    for values in came:
        total = total + values.astype(F32)
    return total


def scheduled(
    layer_in,
    seq_lengths,
    attn_gain,
    w_query,
    w_key,
    w_value,
    w_output,
    mlp_gain,
    w_gate,
    w_up,
    w_down,
    out_grad,
):
    group_rows = layer_in.shape[0] * lax.axis_size("tp")
    query_width, key_width = w_query.shape[1], w_key.shape[1]
    pairs = query_width // (2 * HD)
    masks = [2 * a + b for b in (0, 1) for a in (0, 2, 1, 3)]
    order = lax.axis_index("fsdp") ^ jnp.array(masks, jnp.int32)
    cut = w_down.shape[0] // 256 * 128 + 128

    input_rows = gather_rows(layer_in)
    down_high = w_down[cut:]
    v = Held(
        o=jnp.concatenate([w_output] + [zed(w_output, a) for a in (2, 1, 3)], axis=1),
        down_high=[down_high, why(down_high)],
        down_low=w_down[:cut],
        gains=own_gains([attn_gain, mlp_gain])[:, :, None],
        order=order,
        layer_in=layer_in,
        out_grad=out_grad,
        w_qkv=jnp.concatenate([w_query, w_key, w_value], axis=1),
        w_gate=w_gate,
        w_up=w_up,
    )
    first_at, where_at = positions(seq_lengths, group_rows)
    v.update(first_at=first_at, tables=rope_tables(where_at[0], HD))
    v = fence(v)

    q = (v.w_qkv.astype(F32) * v.gains[0]).astype(BF16)
    q = jnp.concatenate([q] + [zed(q, a) for a in (2, 1, 3)], axis=0)
    oy = why(v.o)
    g = (v.w_gate.astype(F32) * v.gains[1]).astype(BF16)
    u = (v.w_up.astype(F32) * v.gains[1]).astype(BF16)
    dq = jnp.concatenate(v.out.down_high, axis=1)
    v.update(q=q, oy=oy, g=g, u=u, dq=dq)
    v = fence(v)

    g = [v.g, zed(v.g, 2), zed(v.g, 1)]
    qy = why(v.q)
    w_output_all = jnp.concatenate([v.out.o, v.out.oy], axis=1)
    rows_one = unit_rows(v.order, input_rows)
    v.update(g=g, qy=qy, w_output_all=w_output_all, rows_one=rows_one)
    v = fence(v)

    grad_gathered = gather_rows(v.out_grad)
    g = v.g + [zed(v.g[1], 1)]
    u = [v.u, zed(v.u, 1)]
    gy = [why(v.g[0]), why(v.g[1])]
    qkv = project_rotate(v.rows_one, v.q, v.qy, *v.tables)
    attended, logs = attention(qkv, v.first_at, pairs)
    partial = project(attended, v.w_output_all).astype(BF16)
    v.update(g=g, gy=gy, u=u, qkv=qkv, attended=attended, logs=logs, partial=partial)
    v = fence(v)

    came = sum_rows(v.out.partial)
    u = [v.u[0], zed(v.u[0], 2), v.u[1]]
    gy = v.gy + [why(v.g[2]), why(v.g[3])]
    grad_rows = held_rows(v.order, grad_gathered)
    v.update(u=u, gy=gy, grad_rows=grad_rows)
    v = fence(v)

    u = v.u + [zed(v.u[1], 1)]
    low = v.out.down_low
    low = [low, zed(low, 2), zed(low, 1)]
    uy = [why(v.u[0]), why(v.u[1])]
    w_gate_all = jnp.concatenate(v.out.g + v.out.gy, axis=0)
    mid, unit_two, inverse_two = middle(v.order, v.layer_in, came)
    v.update(u=u, uy=uy, low=low, w_gate_all=w_gate_all)
    v.update(mid=mid, unit_two=unit_two, inverse_two=inverse_two)
    v = fence(v)

    rows_two = gather_rows(v.out.unit_two)
    low = [jnp.concatenate(v.low, axis=1), zed(v.low[1], 1)]
    dq = [v.dq, zed(v.dq, 2)]
    w_ups = [jnp.concatenate(v.u + v.uy, axis=0), why(v.u[2]), why(v.u[3])]
    v.update(low=low, dq=dq, w_ups=w_ups)
    v = fence(v)

    low = v.low + [why(v.low[0]), why(v.low[1])]
    dq = v.dq + [zed(v.dq[0], 1), zed(v.dq[1], 1)]
    hidden, factors = hidden_part(rows_two, v.w_gate_all, v.w_ups)
    low_away = part(hidden[:, :cut], v.grad_rows, 1, 4, 8).astype(BF16)
    high_away = both(hidden[:, cut:], v.grad_rows, 2, 4)
    v.update(dq=dq, low=low, rows_two=rows_two, hidden=hidden)
    v.update(factors=factors, low_away=low_away, high_away=high_away)
    v = fence(v)

    first = why(v.low_away)
    high_near = zed(v.high_away, 1)
    grad_gate, grad_up = hidden_back(v.grad_rows, v.low, v.dq, v.out.factors)
    partial = feed_back(grad_gate, grad_up, v.w_gate_all, v.w_ups)
    gate_away = part(v.rows_two, grad_gate, 0, 6, 8).astype(BF16)
    v.update(first=first, high_near=high_near, gate_away=gate_away)
    v.update(grad_gate=grad_gate, grad_up=grad_up)
    v.update(partial=partial)
    v = fence(v)

    came = sum_rows(v.out.partial)
    hidden_low, hidden_high = v.hidden[:, :cut], v.hidden[:, cut:]
    half = v.first.shape[1] // 2
    low_near = part(hidden_low, v.grad_rows, 1, 2, 4) + v.first[:, half:].astype(F32)
    low_near = zed(low_near.astype(BF16), 1)
    step = half // 2
    ones = [slice(b * half + step, b * half + 2 * step) for b in (0, 1)]
    high_one = [
        (
            part(hidden_high, v.grad_rows, 1, 4 * b + 1, 4 * b + 2)
            + v.high_near[:, at].astype(F32)
        ).astype(BF16)
        for b, at in enumerate(ones)
    ]
    high_far = zed(jnp.concatenate(high_one, axis=1), 2)
    gate_first = why(v.gate_away)
    gate_away = part(v.rows_two, v.grad_gate, 0, 4, 6).astype(BF16)
    gate_kept = part(v.rows_two, v.grad_gate, 0, 0, 4).astype(BF16)
    up_away = part(v.rows_two, v.grad_up, 0, 6, 8).astype(BF16)
    v.update(low_near=low_near, high_far=high_far, gate_first=gate_first, gate_away=gate_away)
    low_kept = part(hidden_low, v.grad_rows, 1, 0, 2).astype(BF16)
    v.update(gate_kept=gate_kept, up_away=up_away, low_kept=low_kept)
    v = fence(v)

    low_sums = v.low_kept.astype(F32) + v.first[:, :half].astype(F32) + v.low_near.astype(F32)
    low_far = zed(low_sums[:, step:].astype(BF16), 2)
    three = zed(joined(v.gate_kept, 0, 3, 4, (v.gate_first, 1, 2)).astype(BF16), 1)
    gate_second = why(v.gate_away)
    grad_mid, grad_mid_low = middle_back(v.order, v.out_grad, v.mid, v.inverse_two, came)
    zeros = [slice(b * half, b * half + step) for b in (0, 1)]
    high_own = [
        part(v.hidden[:, cut:], v.grad_rows, 1, 4 * b, 4 * b + 1)
        + v.high_near[:, at].astype(F32)
        + v.high_far[:, b * step : (b + 1) * step].astype(F32)
        for b, at in enumerate(zeros)
    ]
    high_over = high_own[1].astype(BF16)
    up_away = [v.up_away, part(v.rows_two, v.grad_up, 0, 4, 6).astype(BF16)]
    up_kept = part(v.rows_two, v.grad_up, 0, 0, 4).astype(BF16)
    v.update(low_far=low_far, three=three, gate_second=gate_second, grad_mid=grad_mid)
    v.update(grad_mid_low=grad_mid_low, high_own=high_own[0], high_over=high_over)
    v.update(up_away=up_away, up_kept=up_kept)
    v = fence(v)

    grad_mid_rows = gather_rows(v.out.grad_mid_low)
    far = joined(v.gate_kept, 0, 1, 2, (v.gate_second, 1, 2), (v.three, 0, 1)).astype(BF16)
    near = joined(v.gate_kept, 0, 2, 3, (v.gate_first, 0, 2)).astype(BF16)
    gate_came = [zed(far, 2), zed(near, 1)]
    up_first = why(v.up_away[0])
    low_terms = [term[:, :step] for term in (v.low_kept, v.first, v.low_near)]
    low_sh = summed(v.low_far.astype(F32), low_terms)
    high = v.out.dq
    high = [w[:, :step] for w in high] + [w[:, step:] for w in high]
    high_all = jnp.concatenate(high, axis=1)
    low_all = jnp.concatenate(v.out.low, axis=1)
    partial = project(v.hidden[:, :cut], low_all)
    output_part = (partial + project(v.hidden[:, cut:], high_all)).astype(BF16)
    v.update(gate_came=gate_came, up_first=up_first, low_sh=low_sh, output_part=output_part)
    v = fence(v)

    three = zed(joined(v.up_kept, 0, 3, 4, (v.up_first, 1, 2)).astype(BF16), 1)
    up_second = why(v.up_away[1])
    grad_attended = project_back(grad_mid_rows, v.w_output_all).astype(BF16)
    grad_query, grad_kv = attention_back(
        v.qkv, v.first_at, v.logs, grad_attended, *v.tables, pairs
    )
    grad_qkv = jnp.concatenate([grad_query, grad_kv], axis=1)
    qkv_away = part(v.rows_one, grad_qkv, 0, 4, 8).astype(BF16)
    came_out = sum_rows(v.output_part)
    v.update(three=three, up_second=up_second, grad_qkv=grad_qkv, grad_mid_rows=grad_mid_rows)
    v.update(qkv_away=qkv_away)
    v = fence(v)

    far = joined(v.up_kept, 0, 1, 2, (v.up_second, 1, 2), (v.three, 0, 1)).astype(BF16)
    near = joined(v.up_kept, 0, 2, 3, (v.up_first, 0, 2)).astype(BF16)
    up_came = [zed(far, 2), zed(near, 1)]
    first = why(v.out.qkv_away)
    w_qkv_all = jnp.concatenate([v.q, v.qy], axis=0)
    partial = project_back(v.grad_qkv, w_qkv_all).astype(BF16)
    qkv_kept = part(v.rows_one, v.grad_qkv, 0, 0, 4).astype(BF16)
    output_away = part(v.attended, v.grad_mid_rows, 1, 4, 8).astype(BF16)
    grad_gate_sh = summed(joined(v.gate_kept, 0, 0, 1, (v.gate_second, 0, 2)), v.gate_came)
    v.update(up_came=up_came, first=first, qkv_kept=qkv_kept, output_away=output_away)
    v.update(partial=partial, grad_gate_sh=grad_gate_sh)
    v = fence(v)

    came = sum_rows(v.out.partial)
    pieces = [
        zed(joined(v.qkv_kept, 0, i, i + 1, (v.first, i, 4)).astype(BF16), a)
        for i, a in ((1, 2), (2, 1), (3, 3))
    ]
    over = why(v.output_away)
    high_over = why(v.high_over)
    gain_one, gain_two = v.gains[0], v.gains[1]
    grad_gate_sh = v.grad_gate_sh
    grad_up_sh = summed(joined(v.up_kept, 0, 0, 1, (v.up_second, 0, 2)), v.up_came)
    gain_two_term = jnp.sum(
        grad_gate_sh * v.w_gate.astype(F32) + grad_up_sh * v.w_up.astype(F32), axis=1
    )
    output_kept = part(v.attended, v.grad_mid_rows, 1, 0, 4).astype(BF16)
    layer_out = layer_end(v.order, v.mid, came_out)
    v.update(pieces=pieces, over=over, high_over=high_over, gain_two_term=gain_two_term)
    v.update(grad_gate_sh=grad_gate_sh * gain_two, grad_up_sh=grad_up_sh * gain_two)
    v.update(output_kept=output_kept, layer_out=layer_out)
    v = fence(v)

    pieces = [
        zed(joined(v.output_kept, 1, i, i + 1, (v.over, i, 4)).astype(BF16), a)
        for i, a in ((1, 2), (2, 1), (3, 3))
    ]
    grad_down_sh = jnp.concatenate([v.low_sh, v.high_own + v.high_over.astype(F32)], axis=0)
    in_grad = input_back(v.order, v.layer_in, v.grad_mid, came)
    in_grad, came_pieces, over = fence((in_grad, v.pieces, v.over))
    grad_qkv_sh = summed(joined(v.qkv_kept, 0, 0, 1, (v.first, 0, 4)), came_pieces)
    gain_one_term = jnp.sum(grad_qkv_sh * v.w_qkv.astype(F32), axis=1)
    gain_one_grad, gain_two_grad = share_gains([gain_one_term, v.gain_two_term])
    grad_qkv_sh = grad_qkv_sh * v.gains[0]
    over, gain_one_grad, gain_two_grad = fence((over, gain_one_grad, gain_two_grad))
    return (
        v.layer_out,
        in_grad,
        gain_one_grad,
        grad_qkv_sh[:, :query_width],
        grad_qkv_sh[:, query_width : query_width + key_width],
        grad_qkv_sh[:, query_width + key_width :],
        summed(joined(v.output_kept, 1, 0, 1, (over, 0, 4)), pieces),
        gain_two_grad,
        v.grad_gate_sh,
        v.grad_up_sh,
        grad_down_sh,
    )


def direct(
    layer_in,
    seq_lengths,
    attn_gain,
    w_query,
    w_key,
    w_value,
    w_output,
    mlp_gain,
    w_gate,
    w_up,
    w_down,
    out_grad,
):
    def gather(shard, axis):
        return lax.all_gather(shard, "fsdp", axis=axis, tiled=True)

    def scatter(left, right, axis):
        total = outer(left, right).astype(BF16)
        return lax.psum_scatter(total, "fsdp", scatter_dimension=axis, tiled=True).astype(F32)

    group_rows = layer_in.shape[0] * lax.axis_size("tp")
    query_width, key_width = w_query.shape[1], w_key.shape[1]
    pairs = query_width // (2 * HD)
    order = jnp.arange(COLUMN_BLOCKS, dtype=jnp.int32)
    gain_one, gain_two = [
        lax.all_gather(gain, "tp", axis=0, tiled=True)[:, None] for gain in (attn_gain, mlp_gain)
    ]
    w_qkv = jnp.concatenate([w_query, w_key, w_value], axis=1)
    w_output_all = gather(w_output, 1)
    w_qkv_all = gather((w_qkv.astype(F32) * gain_one).astype(BF16), 0)
    w_gate_all = gather((w_gate.astype(F32) * gain_two).astype(BF16), 0)
    w_up_all = gather((w_up.astype(F32) * gain_two).astype(BF16), 0)
    w_down_all = gather(w_down, 1)
    first_at, where_at = positions(seq_lengths, group_rows)
    cosine, sine = rope_tables(where_at[0], HD)
    rows_one = unit_rows(order, gather_rows(layer_in))
    qkv = project_rotate(rows_one, *jnp.split(w_qkv_all, 2), cosine, sine)
    grad_rows = held_rows(order, gather_rows(out_grad))
    attended, logs = attention(qkv, first_at, pairs)
    came = sum_rows(project(attended, w_output_all).astype(BF16))
    mid, unit_two, inverse_two = middle(order, layer_in, came)
    rows_two = gather_rows(unit_two)
    hidden, factors = hidden_part(rows_two, w_gate_all, [w_up_all])
    grad_down_sh = scatter(hidden, grad_rows, 1)
    came = sum_rows(project(hidden, w_down_all).astype(BF16))
    layer_out = layer_end(order, mid, came)
    grad_gate, grad_up = hidden_back(grad_rows, [w_down_all], [], factors)
    came = sum_rows(feed_back(grad_gate, grad_up, w_gate_all, [w_up_all]))
    grad_gate_sh = scatter(rows_two, grad_gate, 0)
    grad_up_sh = scatter(rows_two, grad_up, 0)
    grad_mid, grad_mid_low = middle_back(order, out_grad, mid, inverse_two, came)
    grad_mid_rows = gather_rows(grad_mid_low)
    grad_attended = project_back(grad_mid_rows, w_output_all).astype(BF16)
    grad_output_sh = scatter(attended, grad_mid_rows, 1)
    grad_query, grad_kv = attention_back(
        qkv, first_at, logs, grad_attended, cosine, sine, pairs
    )
    grad_qkv = jnp.concatenate([grad_query, grad_kv], axis=1)
    came = sum_rows(project_back(grad_qkv, w_qkv_all).astype(BF16))
    in_grad = input_back(order, layer_in, grad_mid, came)
    grad_qkv_sh = scatter(rows_one, grad_qkv, 0)
    gain_one_term = jnp.sum(grad_qkv_sh * w_qkv.astype(F32), axis=1)
    gain_two_term = jnp.sum(
        grad_gate_sh * w_gate.astype(F32) + grad_up_sh * w_up.astype(F32), axis=1
    )
    gain_one_grad, gain_two_grad = [
        lax.psum_scatter(term, "tp", scatter_dimension=0, tiled=True)
        for term in (gain_one_term, gain_two_term)
    ]
    grad_qkv_sh = grad_qkv_sh * gain_one
    return (
        layer_out,
        in_grad,
        gain_one_grad,
        grad_qkv_sh[:, :query_width],
        grad_qkv_sh[:, query_width : query_width + key_width],
        grad_qkv_sh[:, query_width + key_width :],
        grad_output_sh,
        gain_two_grad,
        grad_gate_sh * gain_two,
        grad_up_sh * gain_two,
        grad_down_sh,
    )


def solution(mesh):
    placed = (
        P(("fsdp", "tp"), None),
        P("fsdp", None),
        P(("fsdp", "tp")),
        P("fsdp", "tp"),
        P("fsdp", "tp"),
        P("fsdp", "tp"),
        P("tp", "fsdp"),
        P(("fsdp", "tp")),
        P("fsdp", "tp"),
        P("fsdp", "tp"),
        P("tp", "fsdp"),
        P(("fsdp", "tp"), None),
    )
    paired = (mesh.shape["fsdp"], mesh.shape["tp"]) == (8, 4)
    return jax.shard_map(
        scheduled if paired else direct,
        mesh=mesh,
        in_specs=placed,
        out_specs=(
            P(("fsdp", "tp"), None),
            P(("fsdp", "tp"), None),
            P(("fsdp", "tp")),
            P("fsdp", "tp"),
            P("fsdp", "tp"),
            P("fsdp", "tp"),
            P("tp", "fsdp"),
            P(("fsdp", "tp")),
            P("fsdp", "tp"),
            P("fsdp", "tp"),
            P("tp", "fsdp"),
        ),
        check_vma=False,
    )
```

```python
import math

import jax
import jax.numpy as jnp
from jax import lax
from jax.experimental import pallas as pl
from jax.experimental.pallas import tpu as pltpu
from jax.sharding import PartitionSpec as P

HD = 64
MAXLEN = 512
EPSILON = 1e-05
ROPE_BASE = 10000.0
MASKED_OUT = -1e30
TILE = 512
COLUMN_BLOCKS = 8
ROW_BLOCKS = 4
VMEM = 58 * 1024 * 1024
F32 = jnp.float32
BF16 = jnp.bfloat16


def positions(lengths, count):
    starts = jnp.cumsum(lengths, axis=-1) - lengths
    indices = jnp.arange(count, dtype=jnp.int32)
    inside = (indices[None, :, None] >= starts[:, None, :]) & (
        indices[None, :, None] < (starts + lengths)[:, None, :]
    )
    first_at = jnp.sum(jnp.where(inside, starts[:, None, :], 0), axis=-1)
    return first_at, indices[None, :] - first_at


def rope_tables(where_at, width):
    half_width = width // 2
    inverse_freq = ROPE_BASE ** (-(jnp.arange(half_width, dtype=F32) * 2.0 / width))
    angles = where_at.astype(F32)[:, None] * inverse_freq[None, :]
    cosine, sine = jnp.cos(angles), jnp.sin(angles)
    return jnp.concatenate([cosine] * 4, axis=1), jnp.concatenate([sine] * 4, axis=1)


def project(left, weight):
    return jnp.dot(left, weight, preferred_element_type=F32)


def project_back(grad, weight):
    return jnp.einsum("tc,dc->td", grad, weight, preferred_element_type=F32)


def outer(left, right):
    return jnp.einsum("ta,tb->ab", left, right, preferred_element_type=F32)


def call(body, outs, operands, flops=0, nbytes=0, **more):
    return pl.pallas_call(
        body,
        out_shape=outs,
        compiler_params=pltpu.CompilerParams(vmem_limit_bytes=VMEM),
        cost_estimate=pl.CostEstimate(flops=1, bytes_accessed=1, transcendentals=0),
        **more,
    )(*operands)


def whole(count):
    return [pl.BlockSpec(memory_space=pltpu.VMEM)] * count


SCALARS = pl.BlockSpec(memory_space=pltpu.SMEM)


def spans(order, width):
    step = width // COLUMN_BLOCKS
    return [
        (slice(j * step, (j + 1) * step), pl.ds(pl.multiple_of(order[j] * step, step), step))
        for j in range(COLUMN_BLOCKS)
    ]


def turned(values, lanes):
    width = values.shape[-1]
    first = (lanes % HD) < HD // 2
    return jnp.where(
        first, -pltpu.roll(values, width - HD // 2, 1), pltpu.roll(values, HD // 2, 1)
    )


def unit_rows(order, gathered):
    rows, width = gathered.shape
    count = rows // ROW_BLOCKS

    def body(order, x, out):
        values = x[...].astype(F32)
        inverse = lax.rsqrt(jnp.mean(values * values, axis=-1, keepdims=True) + EPSILON)
        for held, true in spans(order, width):
            out[:, held] = (x[:, true].astype(F32) * inverse).astype(BF16)

    spec = pl.BlockSpec((count, width), lambda i: (i, 0))
    return call(
        body,
        jax.ShapeDtypeStruct((rows, width), BF16),
        (order, gathered),
        nbytes=4 * rows * width,
        grid=(ROW_BLOCKS,),
        in_specs=[SCALARS, spec],
        out_specs=spec,
    )


def project_rotate(rows_one, weights_low, weights_high, cosine, sine):
    rows, width = rows_one.shape
    count = rows // ROW_BLOCKS
    half, total = weights_low.shape
    kv = 2 * HD

    def body(x, low, high, c, s, out):
        product = project(x[:, :half], low[...]) + project(x[:, half:], high[...])
        cos, sin = c[...], s[...]
        lanes = lax.broadcasted_iota(jnp.int32, cos.shape, 1)
        for at in range(0, total, 128):
            part = product[:, at : at + 128]
            if at + 128 > total - kv:
                co, si = jnp.where(lanes < HD, cos, 1.0), jnp.where(lanes < HD, sin, 0.0)
            else:
                co, si = cos, sin
            out[:, at : at + 128] = (part * co + turned(part, lanes) * si).astype(BF16)

    def tiles(columns):
        return pl.BlockSpec((count, columns), lambda i: (i, 0))

    weight = pl.BlockSpec((half, total), lambda i: (0, 0), pipeline_mode=pl.Buffered(1))
    return call(
        body,
        jax.ShapeDtypeStruct((rows, total), BF16),
        (rows_one, weights_low, weights_high, cosine, sine),
        flops=2 * rows * width * total,
        nbytes=2 * (rows * width + width * total),
        grid=(ROW_BLOCKS,),
        in_specs=[tiles(width), weight, weight, tiles(2 * HD), tiles(2 * HD)],
        out_specs=tiles(total),
    )


def window(i, span):
    return max(0, i * span - MAXLEN), (i + 1) * span


def shown(first, i, span):
    low, high = window(i, span)
    keys = low + lax.broadcasted_iota(jnp.int32, (high - low, span), 0)
    rows = i * span + lax.broadcasted_iota(jnp.int32, (high - low, span), 1)
    return (keys <= rows) & (keys >= first[:, i * span : (i + 1) * span])


def dot_nt(left, right):
    return lax.dot_general(left, right, (((1,), (1,)), ((), ())), preferred_element_type=F32)


def dot_tn(left, right):
    return lax.dot_general(left, right, (((0,), (0,)), ((), ())), preferred_element_type=F32)


def stacked(values, heads):
    return jnp.concatenate([values[:, h * HD : (h + 1) * HD] for h in range(heads)], axis=0)


def side_by_side(values, span, heads):
    parts = [values[:, h * span : (h + 1) * span] for h in range(heads)]
    return [jnp.concatenate(parts[h : h + 2], axis=0).T for h in range(0, heads, 2)]


def attention(qkv, first, pairs):
    rows = qkv.shape[0]
    span = rows // ROW_BLOCKS
    heads = min(4, 2 * pairs)
    width = heads * HD

    def body(q, kv, first, out, logs):
        for i in range(rows // span):
            low, high = window(i, span)
            at = slice(i * span, (i + 1) * span)
            allowed = jnp.concatenate([shown(first, i, span)] * heads, axis=1)
            keys, values = kv[low:high, :HD], kv[low:high, HD:]
            queries = stacked((q[at, :] * 0.125).astype(BF16), heads)
            scores = jnp.where(allowed, dot_nt(keys, queries), MASKED_OUT)
            top = jnp.max(scores, axis=0, keepdims=True)
            shares = jnp.exp(scores - top)
            total = jnp.sum(shares, axis=0, keepdims=True)
            mixed = dot_tn(values, shares.astype(BF16)) / total
            log = top + jnp.log(total)
            for h in range(heads):
                logs[h // 2, h % 2 : h % 2 + 1, at] = log[:, h * span : (h + 1) * span]
            for p, pair in enumerate(side_by_side(mixed, span, heads)):
                out[at, p * 2 * HD : (p + 1) * 2 * HD] = pair.astype(BF16)

    return call(
        body,
        (
            jax.ShapeDtypeStruct((rows, pairs * 2 * HD), BF16),
            jax.ShapeDtypeStruct((pairs, 2, rows), F32),
        ),
        (qkv, qkv, first),
        grid=(2 * pairs // heads,),
        in_specs=[
            pl.BlockSpec((rows, width), lambda p: (0, p)),
            pl.BlockSpec((rows, 2 * HD), lambda p: (0, pairs)),
            pl.BlockSpec((1, rows), lambda p: (0, 0)),
        ],
        out_specs=(
            pl.BlockSpec((rows, width), lambda p: (0, p)),
            pl.BlockSpec((heads // 2, 2, rows), lambda p: (p, 0, 0)),
        ),
    )


def attention_back(qkv, first, logs, grads, cosine, sine, pairs):
    rows = qkv.shape[0]
    span = rows // (2 * ROW_BLOCKS)
    heads = min(4, 2 * pairs)
    width = heads * HD

    def body(q, kv, first, logs, grad, c, s, dq, dkv, total):
        @pl.when(pl.program_id(0) == 0)
        def _():
            total[...] = jnp.zeros_like(total)

        lanes = lax.broadcasted_iota(jnp.int32, (span, 2 * HD), 1)
        for i in range(rows // span):
            low, high = window(i, span)
            at = slice(i * span, (i + 1) * span)
            allowed = jnp.concatenate([shown(first, i, span)] * heads, axis=1)
            keys, values = kv[low:high, :HD], kv[low:high, HD:]
            queries = stacked((q[at, :] * 0.125).astype(BF16), heads)
            came = stacked(grad[at, :], heads)
            log = jnp.concatenate([logs[h // 2, h % 2 : h % 2 + 1, at] for h in range(heads)], axis=1)
            shares = jnp.where(allowed, jnp.exp(dot_nt(keys, queries) - log), 0.0)
            change = dot_nt(values, came)
            inner = jnp.sum(shares * change, axis=0, keepdims=True)
            score_grads = (shares * (change - inner)).astype(BF16)
            value_part = jnp.dot(shares.astype(BF16), came, preferred_element_type=F32)
            key_part = jnp.dot(score_grads, queries, preferred_element_type=F32)
            total[low:high, :] += jnp.concatenate([key_part, value_part], axis=1)
            query_grads = dot_tn(keys, score_grads) * 0.125
            for p, pair in enumerate(side_by_side(query_grads, span, heads)):
                dq[at, p * 2 * HD : (p + 1) * 2 * HD] = (
                    pair * c[at, :] - turned(pair * s[at, :], lanes)
                ).astype(BF16)

        @pl.when(pl.program_id(0) == 2 * pairs // heads - 1)
        def _():
            for i in range(rows // span):
                at = slice(i * span, (i + 1) * span)
                cos = jnp.where(lanes < HD, c[at, :], 1.0)
                sin = jnp.where(lanes < HD, s[at, :], 0.0)
                part = total[at, :]
                dkv[at, :] = (part * cos - turned(part * sin, lanes)).astype(BF16)

    return call(
        body,
        (
            jax.ShapeDtypeStruct((rows, pairs * 2 * HD), BF16),
            jax.ShapeDtypeStruct((rows, 2 * HD), BF16),
        ),
        (qkv, qkv, first, logs, grads, cosine, sine),
        grid=(2 * pairs // heads,),
        in_specs=[
            pl.BlockSpec((rows, width), lambda p: (0, p)),
            pl.BlockSpec((rows, 2 * HD), lambda p: (0, pairs)),
            pl.BlockSpec((1, rows), lambda p: (0, 0)),
            pl.BlockSpec((heads // 2, 2, rows), lambda p: (p, 0, 0)),
            pl.BlockSpec((rows, width), lambda p: (0, p)),
            pl.BlockSpec((rows, 2 * HD), lambda p: (0, 0)),
            pl.BlockSpec((rows, 2 * HD), lambda p: (0, 0)),
        ],
        out_specs=(
            pl.BlockSpec((rows, width), lambda p: (0, p)),
            pl.BlockSpec((rows, 2 * HD), lambda p: (0, 0)),
        ),
        scratch_shapes=[pltpu.VMEM((rows, 2 * HD), F32)],
    )


def row_kernel(multiply, left, weights, width, extra, outs, finish, tile=TILE):
    rows = left[0].shape[0]
    tile = min(tile, rows)
    many = len(left), len(left) + len(weights), len(left) + len(weights) + len(extra)

    def body(*refs):
        product = multiply(refs[: many[0]], refs[many[0] : many[1]])
        finish(product, refs[many[1] : many[2]], refs[many[2] :])

    def tiles(columns):
        return pl.BlockSpec((tile, columns), lambda i: (i, 0))

    widths = [width] * len(outs)
    inner = sum(weight.size for weight in weights)
    return pl.pallas_call(
        body,
        out_shape=tuple(
            jax.ShapeDtypeStruct((rows, columns), kind)
            for columns, kind in zip(widths, outs, strict=True)
        ),
        grid=(rows // tile,),
        in_specs=[tiles(v.shape[1]) for v in left]
        + [
            pl.BlockSpec(v.shape, lambda i: (0, 0), pipeline_mode=pl.Buffered(1)) for v in weights
        ]
        + [tiles(v.shape[1]) for v in extra],
        out_specs=tuple(tiles(columns) for columns in widths),
        compiler_params=pltpu.CompilerParams(vmem_limit_bytes=VMEM),
        cost_estimate=pl.CostEstimate(flops=1, bytes_accessed=1, transcendentals=0),
    )(*left, *weights, *extra)


def down_rows(left, weights):
    (x,) = left
    total, at = None, 0
    for w in weights:
        term = jnp.dot(x[:, at : at + w.shape[0]], w[...], preferred_element_type=F32)
        total, at = term if total is None else total + term, at + w.shape[0]
    return total


def hidden_part(rows_two, w_gate, w_ups):
    def multiply(left, weights):
        gate = jnp.dot(left[0][...], weights[0][...], preferred_element_type=F32)
        return gate, down_rows(left, weights[1:])

    def finish(products, extra, outs):
        gate, up = products
        sigmoid = 1.0 / (1.0 + jnp.exp(-gate))
        silu = gate * sigmoid
        outs[0][...] = (silu * up).astype(BF16)
        outs[1][...] = (up * sigmoid * (1.0 + gate * (1.0 - sigmoid))).astype(BF16)
        outs[2][...] = silu.astype(BF16)

    hidden, *factors = row_kernel(
        multiply, [rows_two], [w_gate, *w_ups], w_gate.shape[1], [], [BF16] * 3, finish, 256
    )
    return hidden, factors


def hidden_back(grad_rows, lows, highs, factors):
    def multiply(left, weights):
        (x,) = left
        products, total, at = [], None, 0
        for w in weights[: len(lows)]:
            term = dot_nt(x[:, at : at + w.shape[1]], w[...])
            total, at = term if total is None else total + term, at + w.shape[1]
        products.append(total)
        total = None
        for a, w in enumerate(weights[len(lows) :]):
            step = w.shape[1] // 2
            for place, sub in ((a, 0), (4 + a, 1)):
                term = dot_nt(
                    x[:, place * step : (place + 1) * step], w[:, sub * step : (sub + 1) * step]
                )
                total = term if total is None else total + term
        if highs:
            products.append(total)
        return products

    def finish(products, extra, outs):
        at = 0
        for product in products:
            columns = slice(at, at + product.shape[1])
            for factor, out in zip(extra, outs, strict=True):
                out[:, columns] = (product * factor[:, columns].astype(F32)).astype(BF16)
            at = columns.stop

    width = factors[0].shape[1]
    return row_kernel(
        multiply, [grad_rows], [*lows, *highs], width, factors, [BF16] * 2, finish, 256
    )


def feed_back(grad_gate, grad_up, w_gate, w_ups):
    def multiply(left, weights):
        products, row = [], 0
        for w_up in weights[1:]:
            rows = slice(row, row + w_up.shape[0])
            products.append(dot_nt(left[0][...], weights[0][rows, :]) + dot_nt(left[1][...], w_up[...]))
            row = rows.stop
        return products

    def finish(products, extra, outs):
        at = 0
        for product in products:
            outs[0][:, at : at + product.shape[1]] = product.astype(BF16)
            at += product.shape[1]

    return row_kernel(
        multiply,
        [grad_gate, grad_up],
        [w_gate, *w_ups],
        w_gate.shape[0],
        [],
        [BF16],
        finish,
        256,
    )[0]


def held_rows(order, gathered):
    rows, width = gathered.shape
    count = rows // ROW_BLOCKS

    def body(order, x, out):
        for held, true in spans(order, width):
            out[:, held] = x[:, true]

    spec = pl.BlockSpec((count, width), lambda i: (i, 0))
    return call(
        body,
        jax.ShapeDtypeStruct((rows, width), BF16),
        (order, gathered),
        nbytes=4 * rows * width,
        grid=(ROW_BLOCKS,),
        in_specs=[SCALARS, spec],
        out_specs=spec,
    )


def middle(order, layer_in, came):
    count, width = layer_in.shape

    def body(order, x, came, mid, unit, inverse):
        for held, true in spans(order, width):
            mid[:, held] = x[:, true].astype(F32) + came[:, held].astype(F32)
        values = mid[...]
        scale = lax.rsqrt(jnp.mean(values * values, axis=-1, keepdims=True) + EPSILON)
        inverse[...] = scale
        unit[...] = (values * scale).astype(BF16)

    return call(
        body,
        (
            jax.ShapeDtypeStruct((count, width), F32),
            jax.ShapeDtypeStruct((count, width), BF16),
            jax.ShapeDtypeStruct((count, 1), F32),
        ),
        (order, layer_in, came),
        nbytes=20 * count * width,
        in_specs=[SCALARS] + whole(2),
        out_specs=tuple(whole(3)),
    )


def layer_end(order, mid, came):
    count, width = mid.shape

    def body(order, mid, came, out):
        for held, true in spans(order, width):
            total = mid[:, held] + came[:, held].astype(F32)
            out[:, true] = total.astype(BF16)

    return call(
        body,
        jax.ShapeDtypeStruct((count, width), BF16),
        (order, mid, came),
        nbytes=14 * count * width,
        in_specs=[SCALARS] + whole(2),
        out_specs=whole(1)[0],
    )


def middle_back(order, out_grad, mid, inverse, came):
    count, width = mid.shape

    def body(order, dy, mid, inverse, came, grad, low):
        scale = inverse[...]
        grad_unit = came[...].astype(F32)
        unit = mid[...] * scale
        inner = jnp.mean(grad_unit * unit, axis=-1, keepdims=True)
        grad[...] = scale * (grad_unit - unit * inner)
        for held, true in spans(order, width):
            total = grad[:, held] + dy[:, true].astype(F32)
            grad[:, held] = total
            low[:, held] = total.astype(BF16)

    return call(
        body,
        (
            jax.ShapeDtypeStruct((count, width), F32),
            jax.ShapeDtypeStruct((count, width), BF16),
        ),
        (order, out_grad, mid, inverse, came),
        nbytes=20 * count * width,
        in_specs=[SCALARS] + whole(4),
        out_specs=tuple(whole(2)),
    )


def input_back(order, layer_in, grad_mid, came):
    count, width = grad_mid.shape

    def body(order, x, grad_mid, came, out, unit):
        values = x[...].astype(F32)
        scale = lax.rsqrt(jnp.mean(values * values, axis=-1, keepdims=True) + EPSILON)
        for held, true in spans(order, width):
            unit[:, held] = x[:, true].astype(F32) * scale
        grad_unit = came[...].astype(F32)
        inner = jnp.mean(grad_unit * unit[...], axis=-1, keepdims=True)
        unit[...] = grad_mid[...] + scale * (grad_unit - unit[...] * inner)
        for held, true in spans(order, width):
            out[:, true] = unit[:, held]

    return call(
        body,
        jax.ShapeDtypeStruct((count, width), F32),
        (order, layer_in, grad_mid, came),
        nbytes=16 * count * width,
        in_specs=[SCALARS] + whole(3),
        out_specs=whole(1)[0],
        scratch_shapes=[pltpu.VMEM((count, width), F32)],
    )


def gather_rows(rows):
    return lax.all_gather(rows, "tp", axis=0, tiled=True)


def sum_rows(partial):
    return lax.psum_scatter(partial, "tp", scatter_dimension=0, tiled=True)


class Taker:
    def __init__(self, held):
        self.held = held

    def __getattr__(self, name):
        return self.held.pop(name)


class Held(dict):
    __getattr__ = dict.__getitem__

    @property
    def out(self):
        return Taker(self)


def fence(state):
    if isinstance(state, Held):
        return Held(lax.optimization_barrier(dict(state)))
    return lax.optimization_barrier(state)


def zed(values, step):
    return lax.ppermute(values, "fsdp", [(i, i ^ (2 * step)) for i in range(8)])


def why(values):
    return lax.ppermute(values, "fsdp", [(i, i ^ 1) for i in range(8)])


def teep(values, mask):
    return lax.ppermute(values, "tp", [(i, i ^ mask) for i in range(4)])


def own_gains(gains):
    t = lax.axis_index("tp")
    own = jnp.stack(gains)
    near = jnp.stack([own, teep(own, 1)], axis=1)
    near = jnp.where((t & 1) == 1, near[:, ::-1], near)
    both = jnp.stack([near, teep(near, 2)], axis=1)
    both = jnp.where((t >> 1) == 1, both[:, ::-1], both)
    return both.reshape(len(gains), -1)


def share_gains(terms):
    t = lax.axis_index("tp")
    both = jnp.stack(terms).reshape(len(terms), 2, 2, -1)
    both = jnp.where((t >> 1) == 1, both[:, ::-1], both)
    both = both[:, 0] + teep(both[:, 1], 2)
    both = jnp.where((t & 1) == 1, both[:, ::-1], both)
    both = both[:, 0] + teep(both[:, 1], 1)
    return [both[i] for i in range(len(terms))]


def part(left, right, axis, first, last):
    step = (left if axis == 0 else right).shape[1] // COLUMN_BLOCKS
    at = slice(first * step, last * step)
    if axis == 0:
        return outer(left[:, at], right)
    return outer(left, right[:, at])


def both(left, right, first, last):
    parts = [part(left, right, 1, b + first, b + last).astype(BF16) for b in (0, 4)]
    return jnp.concatenate(parts, axis=1)


def joined(values, axis, first, last, *came):
    step = values.shape[axis] // 4
    total = lax.slice_in_dim(values, first * step, last * step, axis=axis).astype(F32)
    for array, at, count in came:
        size = array.shape[axis] // count
        piece = lax.slice_in_dim(array, at * size, (at + last - first) * size, axis=axis)
        total = total + piece.astype(F32)
    return total


def summed(total, came):
    for values in came:
        total = total + values.astype(F32)
    return total


def scheduled(
    layer_in,
    seq_lengths,
    attn_gain,
    w_query,
    w_key,
    w_value,
    w_output,
    mlp_gain,
    w_gate,
    w_up,
    w_down,
    out_grad,
):
    group_rows = layer_in.shape[0] * lax.axis_size("tp")
    query_width, key_width = w_query.shape[1], w_key.shape[1]
    pairs = query_width // (2 * HD)
    masks = [2 * a + b for b in (0, 1) for a in (0, 2, 1, 3)]
    order = lax.axis_index("fsdp") ^ jnp.array(masks, jnp.int32)
    cut = w_down.shape[0] // 256 * 128 + 128

    input_rows = gather_rows(layer_in)
    down_high = w_down[cut:]
    v = Held(
        o=jnp.concatenate([w_output] + [zed(w_output, a) for a in (2, 1, 3)], axis=1),
        down_high=[down_high, why(down_high)],
        down_low=w_down[:cut],
        gains=own_gains([attn_gain, mlp_gain])[:, :, None],
        order=order,
        layer_in=layer_in,
        out_grad=out_grad,
        w_qkv=jnp.concatenate([w_query, w_key, w_value], axis=1),
        w_gate=w_gate,
        w_up=w_up,
    )
    first_at, where_at = positions(seq_lengths, group_rows)
    v.update(first_at=first_at, tables=rope_tables(where_at[0], HD))
    v = fence(v)

    q = (v.w_qkv.astype(F32) * v.gains[0]).astype(BF16)
    q = jnp.concatenate([q] + [zed(q, a) for a in (2, 1, 3)], axis=0)
    oy = why(v.o)
    g = (v.w_gate.astype(F32) * v.gains[1]).astype(BF16)
    u = (v.w_up.astype(F32) * v.gains[1]).astype(BF16)
    dq = jnp.concatenate(v.out.down_high, axis=1)
    v.update(q=q, oy=oy, g=g, u=u, dq=dq)
    v = fence(v)

    g = [v.g, zed(v.g, 2), zed(v.g, 1)]
    qy = why(v.q)
    w_output_all = jnp.concatenate([v.out.o, v.out.oy], axis=1)
    rows_one = unit_rows(v.order, input_rows)
    v.update(g=g, qy=qy, w_output_all=w_output_all, rows_one=rows_one)
    v = fence(v)

    grad_gathered = gather_rows(v.out_grad)
    g = v.g + [zed(v.g[1], 1)]
    u = [v.u, zed(v.u, 1)]
    gy = [why(v.g[0]), why(v.g[1])]
    qkv = project_rotate(v.rows_one, v.q, v.qy, *v.tables)
    attended, logs = attention(qkv, v.first_at, pairs)
    partial = project(attended, v.w_output_all).astype(BF16)
    v.update(g=g, gy=gy, u=u, qkv=qkv, attended=attended, logs=logs, partial=partial)
    v = fence(v)

    came = sum_rows(v.out.partial)
    u = [v.u[0], zed(v.u[0], 2), v.u[1]]
    gy = v.gy + [why(v.g[2]), why(v.g[3])]
    grad_rows = held_rows(v.order, grad_gathered)
    v.update(u=u, gy=gy, grad_rows=grad_rows)
    v = fence(v)

    u = v.u + [zed(v.u[1], 1)]
    low = v.out.down_low
    low = [low, zed(low, 2), zed(low, 1)]
    uy = [why(v.u[0]), why(v.u[1])]
    w_gate_all = jnp.concatenate(v.out.g + v.out.gy, axis=0)
    mid, unit_two, inverse_two = middle(v.order, v.layer_in, came)
    v.update(u=u, uy=uy, low=low, w_gate_all=w_gate_all)
    v.update(mid=mid, unit_two=unit_two, inverse_two=inverse_two)
    v = fence(v)

    rows_two = gather_rows(v.out.unit_two)
    low = [jnp.concatenate(v.low, axis=1), zed(v.low[1], 1)]
    dq = [v.dq, zed(v.dq, 2)]
    w_ups = [jnp.concatenate(v.u + v.uy, axis=0), why(v.u[2]), why(v.u[3])]
    v.update(low=low, dq=dq, w_ups=w_ups)
    v = fence(v)

    low = v.low + [why(v.low[0]), why(v.low[1])]
    dq = v.dq + [zed(v.dq[0], 1), zed(v.dq[1], 1)]
    hidden, factors = hidden_part(rows_two, v.w_gate_all, v.w_ups)
    low_away = part(hidden[:, :cut], v.grad_rows, 1, 4, 8).astype(BF16)
    high_away = both(hidden[:, cut:], v.grad_rows, 2, 4)
    v.update(dq=dq, low=low, rows_two=rows_two, hidden=hidden)
    v.update(factors=factors, low_away=low_away, high_away=high_away)
    v = fence(v)

    first = why(v.low_away)
    high_near = zed(v.high_away, 1)
    grad_gate, grad_up = hidden_back(v.grad_rows, v.low, v.dq, v.out.factors)
    partial = feed_back(grad_gate, grad_up, v.w_gate_all, v.w_ups)
    gate_away = part(v.rows_two, grad_gate, 0, 6, 8).astype(BF16)
    v.update(first=first, high_near=high_near, gate_away=gate_away)
    v.update(grad_gate=grad_gate, grad_up=grad_up)
    v.update(partial=partial)
    v = fence(v)

    came = sum_rows(v.out.partial)
    hidden_low, hidden_high = v.hidden[:, :cut], v.hidden[:, cut:]
    half = v.first.shape[1] // 2
    low_near = part(hidden_low, v.grad_rows, 1, 2, 4) + v.first[:, half:].astype(F32)
    low_near = zed(low_near.astype(BF16), 1)
    step = half // 2
    ones = [slice(b * half + step, b * half + 2 * step) for b in (0, 1)]
    high_one = [
        (
            part(hidden_high, v.grad_rows, 1, 4 * b + 1, 4 * b + 2)
            + v.high_near[:, at].astype(F32)
        ).astype(BF16)
        for b, at in enumerate(ones)
    ]
    high_far = zed(jnp.concatenate(high_one, axis=1), 2)
    gate_first = why(v.gate_away)
    gate_away = part(v.rows_two, v.grad_gate, 0, 4, 6).astype(BF16)
    gate_kept = part(v.rows_two, v.grad_gate, 0, 0, 4).astype(BF16)
    up_away = part(v.rows_two, v.grad_up, 0, 6, 8).astype(BF16)
    v.update(low_near=low_near, high_far=high_far, gate_first=gate_first, gate_away=gate_away)
    low_kept = part(hidden_low, v.grad_rows, 1, 0, 2).astype(BF16)
    v.update(gate_kept=gate_kept, up_away=up_away, low_kept=low_kept)
    v = fence(v)

    low_sums = v.low_kept.astype(F32) + v.first[:, :half].astype(F32) + v.low_near.astype(F32)
    low_far = zed(low_sums[:, step:].astype(BF16), 2)
    three = zed(joined(v.gate_kept, 0, 3, 4, (v.gate_first, 1, 2)).astype(BF16), 1)
    gate_second = why(v.gate_away)
    grad_mid, grad_mid_low = middle_back(v.order, v.out_grad, v.mid, v.inverse_two, came)
    zeros = [slice(b * half, b * half + step) for b in (0, 1)]
    high_own = [
        part(v.hidden[:, cut:], v.grad_rows, 1, 4 * b, 4 * b + 1)
        + v.high_near[:, at].astype(F32)
        + v.high_far[:, b * step : (b + 1) * step].astype(F32)
        for b, at in enumerate(zeros)
    ]
    high_over = high_own[1].astype(BF16)
    up_away = [v.up_away, part(v.rows_two, v.grad_up, 0, 4, 6).astype(BF16)]
    up_kept = part(v.rows_two, v.grad_up, 0, 0, 4).astype(BF16)
    v.update(low_far=low_far, three=three, gate_second=gate_second, grad_mid=grad_mid)
    v.update(grad_mid_low=grad_mid_low, high_own=high_own[0], high_over=high_over)
    v.update(up_away=up_away, up_kept=up_kept)
    v = fence(v)

    grad_mid_rows = gather_rows(v.out.grad_mid_low)
    far = joined(v.gate_kept, 0, 1, 2, (v.gate_second, 1, 2), (v.three, 0, 1)).astype(BF16)
    near = joined(v.gate_kept, 0, 2, 3, (v.gate_first, 0, 2)).astype(BF16)
    gate_came = [zed(far, 2), zed(near, 1)]
    up_first = why(v.up_away[0])
    low_terms = [term[:, :step] for term in (v.low_kept, v.first, v.low_near)]
    low_sh = summed(v.low_far.astype(F32), low_terms)
    high = v.out.dq
    high = [w[:, :step] for w in high] + [w[:, step:] for w in high]
    high_all = jnp.concatenate(high, axis=1)
    low_all = jnp.concatenate(v.out.low, axis=1)
    partial = project(v.hidden[:, :cut], low_all)
    output_part = (partial + project(v.hidden[:, cut:], high_all)).astype(BF16)
    v.update(gate_came=gate_came, up_first=up_first, low_sh=low_sh, output_part=output_part)
    v = fence(v)

    three = zed(joined(v.up_kept, 0, 3, 4, (v.up_first, 1, 2)).astype(BF16), 1)
    up_second = why(v.up_away[1])
    grad_attended = project_back(grad_mid_rows, v.w_output_all).astype(BF16)
    grad_query, grad_kv = attention_back(
        v.qkv, v.first_at, v.logs, grad_attended, *v.tables, pairs
    )
    grad_qkv = jnp.concatenate([grad_query, grad_kv], axis=1)
    qkv_away = part(v.rows_one, grad_qkv, 0, 4, 8).astype(BF16)
    came_out = sum_rows(v.output_part)
    v.update(three=three, up_second=up_second, grad_qkv=grad_qkv, grad_mid_rows=grad_mid_rows)
    v.update(qkv_away=qkv_away)
    v = fence(v)

    far = joined(v.up_kept, 0, 1, 2, (v.up_second, 1, 2), (v.three, 0, 1)).astype(BF16)
    near = joined(v.up_kept, 0, 2, 3, (v.up_first, 0, 2)).astype(BF16)
    up_came = [zed(far, 2), zed(near, 1)]
    first = why(v.out.qkv_away)
    w_qkv_all = jnp.concatenate([v.q, v.qy], axis=0)
    partial = project_back(v.grad_qkv, w_qkv_all).astype(BF16)
    qkv_kept = part(v.rows_one, v.grad_qkv, 0, 0, 4).astype(BF16)
    output_away = part(v.attended, v.grad_mid_rows, 1, 4, 8).astype(BF16)
    grad_gate_sh = summed(joined(v.gate_kept, 0, 0, 1, (v.gate_second, 0, 2)), v.gate_came)
    v.update(up_came=up_came, first=first, qkv_kept=qkv_kept, output_away=output_away)
    v.update(partial=partial, grad_gate_sh=grad_gate_sh)
    v = fence(v)

    came = sum_rows(v.out.partial)
    pieces = [
        zed(joined(v.qkv_kept, 0, i, i + 1, (v.first, i, 4)).astype(BF16), a)
        for i, a in ((1, 2), (2, 1), (3, 3))
    ]
    over = why(v.output_away)
    high_over = why(v.high_over)
    gain_one, gain_two = v.gains[0], v.gains[1]
    grad_gate_sh = v.grad_gate_sh
    grad_up_sh = summed(joined(v.up_kept, 0, 0, 1, (v.up_second, 0, 2)), v.up_came)
    gain_two_term = jnp.sum(
        grad_gate_sh * v.w_gate.astype(F32) + grad_up_sh * v.w_up.astype(F32), axis=1
    )
    output_kept = part(v.attended, v.grad_mid_rows, 1, 0, 4).astype(BF16)
    layer_out = layer_end(v.order, v.mid, came_out)
    v.update(pieces=pieces, over=over, high_over=high_over, gain_two_term=gain_two_term)
    v.update(grad_gate_sh=grad_gate_sh * gain_two, grad_up_sh=grad_up_sh * gain_two)
    v.update(output_kept=output_kept, layer_out=layer_out)
    v = fence(v)

    pieces = [
        zed(joined(v.output_kept, 1, i, i + 1, (v.over, i, 4)).astype(BF16), a)
        for i, a in ((1, 2), (2, 1), (3, 3))
    ]
    grad_down_sh = jnp.concatenate([v.low_sh, v.high_own + v.high_over.astype(F32)], axis=0)
    in_grad = input_back(v.order, v.layer_in, v.grad_mid, came)
    in_grad, came_pieces, over = fence((in_grad, v.pieces, v.over))
    grad_qkv_sh = summed(joined(v.qkv_kept, 0, 0, 1, (v.first, 0, 4)), came_pieces)
    gain_one_term = jnp.sum(grad_qkv_sh * v.w_qkv.astype(F32), axis=1)
    gain_one_grad, gain_two_grad = share_gains([gain_one_term, v.gain_two_term])
    grad_qkv_sh = grad_qkv_sh * v.gains[0]
    over, gain_one_grad, gain_two_grad = fence((over, gain_one_grad, gain_two_grad))
    return (
        v.layer_out,
        in_grad,
        gain_one_grad,
        grad_qkv_sh[:, :query_width],
        grad_qkv_sh[:, query_width : query_width + key_width],
        grad_qkv_sh[:, query_width + key_width :],
        summed(joined(v.output_kept, 1, 0, 1, (over, 0, 4)), pieces),
        gain_two_grad,
        v.grad_gate_sh,
        v.grad_up_sh,
        grad_down_sh,
    )


def direct(
    layer_in,
    seq_lengths,
    attn_gain,
    w_query,
    w_key,
    w_value,
    w_output,
    mlp_gain,
    w_gate,
    w_up,
    w_down,
    out_grad,
):
    def gather(shard, axis):
        return lax.all_gather(shard, "fsdp", axis=axis, tiled=True)

    def scatter(left, right, axis):
        total = outer(left, right).astype(BF16)
        return lax.psum_scatter(total, "fsdp", scatter_dimension=axis, tiled=True).astype(F32)

    group_rows = layer_in.shape[0] * lax.axis_size("tp")
    query_width, key_width = w_query.shape[1], w_key.shape[1]
    pairs = query_width // (2 * HD)
    order = jnp.arange(COLUMN_BLOCKS, dtype=jnp.int32)
    gain_one, gain_two = [
        lax.all_gather(gain, "tp", axis=0, tiled=True)[:, None] for gain in (attn_gain, mlp_gain)
    ]
    w_qkv = jnp.concatenate([w_query, w_key, w_value], axis=1)
    w_output_all = gather(w_output, 1)
    w_qkv_all = gather((w_qkv.astype(F32) * gain_one).astype(BF16), 0)
    w_gate_all = gather((w_gate.astype(F32) * gain_two).astype(BF16), 0)
    w_up_all = gather((w_up.astype(F32) * gain_two).astype(BF16), 0)
    w_down_all = gather(w_down, 1)
    first_at, where_at = positions(seq_lengths, group_rows)
    cosine, sine = rope_tables(where_at[0], HD)
    rows_one = unit_rows(order, gather_rows(layer_in))
    qkv = project_rotate(rows_one, *jnp.split(w_qkv_all, 2), cosine, sine)
    grad_rows = held_rows(order, gather_rows(out_grad))
    attended, logs = attention(qkv, first_at, pairs)
    came = sum_rows(project(attended, w_output_all).astype(BF16))
    mid, unit_two, inverse_two = middle(order, layer_in, came)
    rows_two = gather_rows(unit_two)
    hidden, factors = hidden_part(rows_two, w_gate_all, [w_up_all])
    grad_down_sh = scatter(hidden, grad_rows, 1)
    came = sum_rows(project(hidden, w_down_all).astype(BF16))
    layer_out = layer_end(order, mid, came)
    grad_gate, grad_up = hidden_back(grad_rows, [w_down_all], [], factors)
    came = sum_rows(feed_back(grad_gate, grad_up, w_gate_all, [w_up_all]))
    grad_gate_sh = scatter(rows_two, grad_gate, 0)
    grad_up_sh = scatter(rows_two, grad_up, 0)
    grad_mid, grad_mid_low = middle_back(order, out_grad, mid, inverse_two, came)
    grad_mid_rows = gather_rows(grad_mid_low)
    grad_attended = project_back(grad_mid_rows, w_output_all).astype(BF16)
    grad_output_sh = scatter(attended, grad_mid_rows, 1)
    grad_query, grad_kv = attention_back(
        qkv, first_at, logs, grad_attended, cosine, sine, pairs
    )
    grad_qkv = jnp.concatenate([grad_query, grad_kv], axis=1)
    came = sum_rows(project_back(grad_qkv, w_qkv_all).astype(BF16))
    in_grad = input_back(order, layer_in, grad_mid, came)
    grad_qkv_sh = scatter(rows_one, grad_qkv, 0)
    gain_one_term = jnp.sum(grad_qkv_sh * w_qkv.astype(F32), axis=1)
    gain_two_term = jnp.sum(
        grad_gate_sh * w_gate.astype(F32) + grad_up_sh * w_up.astype(F32), axis=1
    )
    gain_one_grad, gain_two_grad = [
        lax.psum_scatter(term, "tp", scatter_dimension=0, tiled=True)
        for term in (gain_one_term, gain_two_term)
    ]
    grad_qkv_sh = grad_qkv_sh * gain_one
    return (
        layer_out,
        in_grad,
        gain_one_grad,
        grad_qkv_sh[:, :query_width],
        grad_qkv_sh[:, query_width : query_width + key_width],
        grad_qkv_sh[:, query_width + key_width :],
        grad_output_sh,
        gain_two_grad,
        grad_gate_sh * gain_two,
        grad_up_sh * gain_two,
        grad_down_sh,
    )


def solution(mesh):
    placed = (
        P(("fsdp", "tp"), None),
        P("fsdp", None),
        P(("fsdp", "tp")),
        P("fsdp", "tp"),
        P("fsdp", "tp"),
        P("fsdp", "tp"),
        P("tp", "fsdp"),
        P(("fsdp", "tp")),
        P("fsdp", "tp"),
        P("fsdp", "tp"),
        P("tp", "fsdp"),
        P(("fsdp", "tp"), None),
    )
    paired = (mesh.shape["fsdp"], mesh.shape["tp"]) == (8, 4)
    return jax.shard_map(
        scheduled if paired else direct,
        mesh=mesh,
        in_specs=placed,
        out_specs=(
            P(("fsdp", "tp"), None),
            P(("fsdp", "tp"), None),
            P(("fsdp", "tp")),
            P("fsdp", "tp"),
            P("fsdp", "tp"),
            P("fsdp", "tp"),
            P("tp", "fsdp"),
            P(("fsdp", "tp")),
            P("fsdp", "tp"),
            P("fsdp", "tp"),
            P("tp", "fsdp"),
        ),
        check_vma=False,
    )
```
